128 devices in a mesh: dp: 16 (over y, z_lo, core), tensor: 8 (over z_hi, x).
Axes of the slice: x: 4, y: 4, z: 4 (z_hi: 2, z_lo: 2; z = z_hi * 2 + z_lo), core: 2. Of those that a mesh axis runs over, the one named last changes fastest.
Arguments:
- tokens: bfloat16 [16384, 2048], P(('dp', 'tensor')), may hold values from -6 to 6
- seq_length: int32 [64], replicated, may hold values from 0 to 1024, as said below
- seq_owner: int32 [64], replicated, may hold values from 0 to 15, as said below
- ln1_gain: float32 [2048], replicated, may hold values from 0.5 to 1.5
- ln1_bias: float32 [2048], replicated, may hold values from -3 to 3
- qkv_weight: bfloat16 [3, 2048, 2048], P(None, None, 'tensor'), may hold values from -0.1875 to 0.1875
- qkv_bias: float32 [3, 2048], P(None, 'tensor'), may hold values from -3 to 3
- out_weight: bfloat16 [2048, 2048], P('tensor'), may hold values from -0.75 to 0.75
- ln2_gain: float32 [2048], replicated, may hold values from 0.5 to 1.5
- ln2_bias: float32 [2048], replicated, may hold values from -3 to 3
- gate_up_weight: bfloat16 [2, 2048, 5632], P(None, None, 'tensor'), may hold values from -0.125 to 0.125
- down_weight: bfloat16 [5632, 2048], P('tensor'), may hold values from -0.15625 to 0.15625
- out_grad: bfloat16 [16384, 2048], P(('dp', 'tensor')), may hold values from -6 to 6
Outputs:
- mixed: bfloat16 [16384, 2048], P(('dp', 'tensor'))
- input_grad: float32 [16384, 2048], P(('dp', 'tensor'))
- ln1_gain_grad: float32 [2048], replicated
- ln1_bias_grad: float32 [2048], replicated
- qkv_weight_grad: float32 [3, 2048, 2048], P(None, None, 'tensor')
- qkv_bias_grad: float32 [3, 2048], P(None, 'tensor')
- out_weight_grad: float32 [2048, 2048], P('tensor')
- ln2_gain_grad: float32 [2048], replicated
- ln2_bias_grad: float32 [2048], replicated
- gate_up_grad: float32 [2, 2048, 5632], P(None, None, 'tensor')
- down_grad: float32 [5632, 2048], P('tensor')
The draws below stay inside these ranges and needn't reach their ends.
Inputs may be any that keep to these rules, and one draw needn't show every extreme that they name: `seq_length`: 0 marks an unused entry; the entries that one dp index owns sum to at most 1024; one entry has length exactly 1024. `seq_owner`: every dp index owns exactly 4 entries.
All inputs are finite; a program needn't handle non-finite values.
Results may differ from the reference program's by a relative error of at most 0.02.
The reference program's roundings to bfloat16 on the way count: a program that leaves them out, or rounds other values in their place, can miss the bound.
Values may be sent and summed in bfloat16 or wider, within the bound.
A program may use at most 192 MiB of HBM per device.

```python
import jax
import jax.numpy as jnp
from jax import lax

D = 2048
HEADS = 32
HEAD_DIM = 64
ROT = 16
FF = 5632
LONGEST = 1024
PER = 4
MEMBER = 1024
NSEQ = 64
TOKENS = 16384
N_DP = 16


def deal_sequences(key):
    chosen = jax.random.randint(jax.random.fold_in(key, 11), (), 0, N_DP)
    longest_other = min(MEMBER // PER, LONGEST)
    spread = jax.random.randint(jax.random.fold_in(key, 12), (N_DP, PER), 1, longest_other + 1)
    member_ids = jnp.arange(N_DP, dtype=jnp.int32)
    slot_ids = jnp.arange(PER, dtype=jnp.int32)
    single = jnp.where(slot_ids == 0, LONGEST, 0).astype(jnp.int32)
    length_table = jnp.where((member_ids == chosen)[:, None], single[None, :], spread)
    owners = jnp.broadcast_to(member_ids[:, None], (N_DP, PER))
    shuffle = jax.random.permutation(jax.random.fold_in(key, 13), N_DP * PER)
    return (length_table.reshape(-1)[shuffle].astype(jnp.int32), owners.reshape(-1)[shuffle].astype(jnp.int32))


def draw_seq_length(key, part):
    shared = deal_sequences(key)
    return shared[0]


def draw_seq_owner(key, part):
    shared = deal_sequences(key)
    return shared[1]


def block_scale(rng, shape, shards, least, top_value):
    loudness, own = 1.0, jax.random.fold_in(rng, 6)
    for dim, blocks in shards:
        heights = jnp.exp(jax.random.uniform(jax.random.fold_in(own, dim), (blocks,), jnp.float32, least / len(shards), top_value / len(shards)))
        loudness = loudness * jnp.repeat(heights, shape[dim] // blocks).reshape([-1 if axis == dim else 1 for axis in range(len(shape))])
    return loudness


def centred(stream_key, extent, width, most, pieces=(), kind=jnp.bfloat16):
    loudness = block_scale(stream_key, extent, pieces, -0.22, 0.18) if pieces else 1.0
    drawn = jax.random.normal(stream_key, extent, jnp.float32) * width * loudness
    return jnp.minimum(jnp.maximum(drawn, -most), most).astype(kind)


def setup_inputs(seed: int = 0) -> dict:
    keys = jax.random.split(jax.random.key(seed), 14)
    tokens = centred(keys[0], (TOKENS, D), 1.0, 6.0, ((0, 128),))
    seq_length = draw_seq_length(jax.random.fold_in(keys[13], 71), 0)
    seq_owner = draw_seq_owner(jax.random.fold_in(keys[13], 71), 0)
    ln1_gain = jnp.clip(1.0 + 0.1 * jax.random.normal(keys[3], (D,), jnp.float32), 0.5, 1.5)
    ln1_bias = centred(keys[4], (D,), 0.5, 3.0, (), jnp.float32)
    qkv_weight = centred(keys[5], (3, D, D), (D // 2) ** -0.5, 0.1875, ((2, 8),))
    qkv_bias = centred(keys[6], (3, D), 0.5, 3.0, ((1, 8),), jnp.float32)
    out_weight = centred(keys[7], (D, D), HEAD_DIM ** -0.5, 0.75, ((0, 8),))
    ln2_gain = jnp.clip(1.0 + 0.1 * jax.random.normal(keys[8], (D,), jnp.float32), 0.5, 1.5)
    ln2_bias = centred(keys[9], (D,), 0.5, 3.0, (), jnp.float32)
    gate_up_weight = centred(keys[10], (2, D, FF), D ** -0.5, 0.125, ((2, 8),))
    down_weight = centred(keys[11], (FF, D), (FF // 4) ** -0.5, 0.15625, ((0, 8),))
    out_grad = centred(keys[12], (TOKENS, D), 1.0, 6.0, ((0, 128),))
    return {"tokens": tokens, "seq_length": seq_length, "seq_owner": seq_owner, "ln1_gain": ln1_gain, "ln1_bias": ln1_bias, "qkv_weight": qkv_weight, "qkv_bias": qkv_bias, "out_weight": out_weight, "ln2_gain": ln2_gain, "ln2_bias": ln2_bias, "gate_up_weight": gate_up_weight, "down_weight": down_weight, "out_grad": out_grad}


HIGHEST = lax.Precision.HIGHEST

@jax.custom_vjp
def low(v):
    return lax.optimization_barrier(v.astype(jnp.bfloat16)).astype(jnp.float32)

@jax.custom_vjp
def low_back(v):
    return v

def low_keep(v):
    return (low(v), None)

def low_pass(kept, grad):
    return (grad,)

def back_keep(v):
    return (v, None)

def back_low(kept, grad):
    return (low(grad),)
low.defvjp(low_keep, low_pass)
low_back.defvjp(back_keep, back_low)

def member_layout(seq_length, seq_owner, member):
    row_ids = jnp.arange(MEMBER, dtype=jnp.int32)
    entry_ids = jnp.arange(NSEQ, dtype=jnp.int32)
    earlier = (entry_ids[:, None] < entry_ids[None, :]).astype(jnp.int32)
    sharing = (seq_owner[:, None] == seq_owner[None, :]).astype(jnp.int32)
    starts = lax.optimization_barrier(jnp.sum(seq_length[:, None] * sharing * earlier, axis=0))
    owned_now = (seq_owner == member).astype(jnp.int32)
    inside = owned_now[None, :] * (row_ids[:, None] >= starts[None, :]).astype(jnp.int32) * (row_ids[:, None] < (starts + seq_length)[None, :]).astype(jnp.int32)
    live_rows = lax.optimization_barrier(jnp.sum(inside, axis=1))
    segment = lax.optimization_barrier(jnp.sum(inside * entry_ids[None, :], axis=1)) + (1 - live_rows) * (NSEQ + row_ids)
    position = lax.optimization_barrier(jnp.sum(inside * (row_ids[:, None] - starts[None, :]), axis=1))
    return (segment, position, live_rows)

def rotary_tables(position):
    half_rot = ROT // 2
    frequency = jnp.power(jnp.float32(10000.0), -2.0 * jnp.arange(half_rot, dtype=jnp.float32) / ROT)
    angles = position.astype(jnp.float32)[:, None] * frequency[None, :]
    return (jnp.cos(angles)[:, None, :], jnp.sin(angles)[:, None, :])

def rotate(values, cosine, sine_table):
    half_rot = ROT // 2
    first_half = values[..., :half_rot]
    second_half = values[..., half_rot:ROT]
    return jnp.concatenate([first_half * cosine - second_half * sine_table, second_half * cosine + first_half * sine_table, values[..., ROT:]], axis=-1)

def layer_norm(values, gain_vec, shift_vec):
    centre = values - lax.optimization_barrier(jnp.mean(values, axis=-1, keepdims=True))
    scale_inv = lax.rsqrt(lax.optimization_barrier(jnp.mean(centre * centre, axis=-1, keepdims=True)) + 1e-05)
    return centre * scale_inv * gain_vec + shift_vec

@jax.checkpoint
def attend(queries, keys_low, values_low, segment):
    row_ids = jnp.arange(queries.shape[0], dtype=jnp.int32)
    allowed = (segment[:, None] == segment[None, :]) & (row_ids[None, :] <= row_ids[:, None])
    scores = low_back(jnp.einsum('qhd,khd->hqk', queries, keys_low, precision=HIGHEST) * HEAD_DIM ** (-0.5))
    scores = jnp.where(allowed[None], scores, -1e+30)
    row_max = lax.optimization_barrier(jnp.max(scores, axis=-1, keepdims=True))
    exp_scores = jnp.exp(scores - row_max)
    attn_prob = exp_scores / lax.optimization_barrier(jnp.sum(exp_scores, axis=-1, keepdims=True))
    return jnp.einsum('hqk,khd->qhd', low(attn_prob), values_low, precision=HIGHEST)

def reference(tokens, seq_length, seq_owner, ln1_gain, ln1_bias, qkv_weight, qkv_bias, out_weight, ln2_gain, ln2_bias, gate_up_weight, down_weight, out_grad):
    segment, position, live_rows = jax.vmap(lambda member: member_layout(seq_length, seq_owner, member))(jnp.arange(N_DP, dtype=jnp.int32))
    cosine, sine_table = rotary_tables(position.reshape(-1))

    def forward(stream_in, norm1_gain, norm1_shift, qkv_all, qkv_shift, out_proj, norm2_gain, norm2_shift, gate_up, down_proj):
        normed1 = low(layer_norm(stream_in, norm1_gain, norm1_shift))
        projected = [low_back(jnp.dot(normed1, qkv_all[channel], precision=HIGHEST, preferred_element_type=jnp.float32) + qkv_shift[channel]) for channel in range(3)]
        shaped = [proj_item.reshape(TOKENS, HEADS, HEAD_DIM) for proj_item in projected]
        queries = low(rotate(shaped[0], cosine, sine_table))
        keys_low = low(rotate(shaped[1], cosine, sine_table))
        values_low = low(shaped[2])
        member_parts = (queries.reshape(N_DP, MEMBER, HEADS, HEAD_DIM), keys_low.reshape(N_DP, MEMBER, HEADS, HEAD_DIM), values_low.reshape(N_DP, MEMBER, HEADS, HEAD_DIM), segment)
        attended = lax.map(lambda parts_now: attend(*parts_now), member_parts)
        attended = low(low_back(attended.reshape(TOKENS, D)))
        attn_out = low_back(jnp.dot(attended, out_proj, precision=HIGHEST, preferred_element_type=jnp.float32))
        mid_stream = stream_in + attn_out
        normed2 = low(layer_norm(mid_stream, norm2_gain, norm2_shift))
        gate_act = low_back(jnp.dot(normed2, gate_up[0], precision=HIGHEST, preferred_element_type=jnp.float32))
        up_act = low_back(jnp.dot(normed2, gate_up[1], precision=HIGHEST, preferred_element_type=jnp.float32))
        hidden = low(jax.nn.silu(gate_act) * up_act)
        return mid_stream + low_back(jnp.dot(hidden, down_proj, precision=HIGHEST, preferred_element_type=jnp.float32))
    float_args = (tokens.astype(jnp.float32), ln1_gain, ln1_bias, qkv_weight.astype(jnp.float32), qkv_bias, out_weight.astype(jnp.float32), ln2_gain, ln2_bias, gate_up_weight.astype(jnp.float32), down_weight.astype(jnp.float32))
    mixed_f, pullback = jax.vjp(forward, *float_args)
    cotangent = out_grad.astype(jnp.float32) * live_rows.reshape(-1).astype(jnp.float32)[:, None]
    gradients = pullback(cotangent)
    return (mixed_f.astype(jnp.bfloat16), gradients[0], gradients[1], gradients[2], gradients[3], gradients[4], gradients[5], gradients[6], gradients[7], gradients[8], gradients[9])
```

```python
import functools

import jax
import jax.numpy as jnp
from jax import lax
from jax.experimental import pallas as pl
from jax.experimental.pallas import tpu as pltpu
from jax.sharding import PartitionSpec as P

HEAD_DIM = 64
ROT = 16
SIDE = 4
BLOCK = 128
AXES = ("dp", "tensor")
MESH = pl.DeviceIdType.MESH
VMEM_LIMIT = 56 * 2**20


def here():
    dp, tensor = lax.axis_index("dp"), lax.axis_index("tensor")
    x, z_hi = lax.rem(tensor, SIDE), lax.div(tensor, SIDE)
    y, z_lo, core = lax.div(dp, SIDE), lax.rem(lax.div(dp, 2), 2), lax.rem(dp, 2)
    return x, y, z_hi, z_lo, core


def device(x, y, z_hi, z_lo, core):
    return ((y * 2 + z_lo) * 2 + core, z_hi * SIDE + x)


def turned(value, by):
    return lax.rem(value + by, SIDE)


def pairs(move):
    found = []
    for dp in range(16):
        for tensor in range(8):
            goal = move(tensor % 4, dp // 4, tensor // 4, (dp // 2) % 2, dp % 2)
            if goal is not None:
                to_dp, to_tensor = device(*goal)
                found.append((dp * 8 + tensor, to_dp * 8 + to_tensor))
    return found


def permute(array, move):
    return lax.ppermute(array, AXES, pairs(move))


def swap_rows(x, y, z_hi, z_lo, core):
    return (x, y, core, z_lo, z_hi)


def remote(source, target, sends, arrives, index, device_id):
    return pltpu.make_async_remote_copy(
        src_ref=source,
        dst_ref=target,
        send_sem=sends.at[index],
        recv_sem=arrives.at[index],
        device_id=device_id,
        device_id_type=MESH,
    )


def greet(peers):
    barrier = pltpu.get_barrier_semaphore()
    for peer in peers:
        pl.semaphore_signal(barrier, inc=1, device_id=peer, device_id_type=MESH)
    pl.semaphore_wait(barrier, len(peers))


def line_peers(place):
    x, y, z_hi, z_lo, core = place
    found = [device(turned(x, k), y, z_hi, z_lo, core) for k in (1, 2, 3)]
    return found + [device(x, y, z_hi, z_lo, 1 - core)]


def row_block(full, core, x):
    return full.at[pl.ds(pl.multiple_of((core * SIDE + x) * BLOCK, BLOCK), BLOCK)]


class Gather:
    scratch = (
        pltpu.SemaphoreType.DMA((3,)),
        pltpu.SemaphoreType.DMA((3,)),
        pltpu.SemaphoreType.DMA((4,)),
        pltpu.SemaphoreType.DMA((4,)),
        pltpu.SemaphoreType.DMA,
    )

    def __init__(self, block, full, place, sems):
        x, y, z_hi, z_lo, core = place
        x_send, x_arrive, core_send, core_arrive, own_sem = sems
        self.own = pltpu.make_async_copy(block, row_block(full, core, x), own_sem)
        self.along = [
            remote(
                block,
                row_block(full, core, x),
                x_send,
                x_arrive,
                step - 1,
                device(turned(x, step), y, z_hi, z_lo, core),
            )
            for step in (1, 2, 3)
        ]
        partner = device(x, y, z_hi, z_lo, 1 - core)
        self.across = [remote(block, row_block(full, core, x), core_send, core_arrive, 0, partner)]
        for step in (1, 2, 3):
            arrived = row_block(full, core, turned(x, SIDE - step))
            self.across.append(remote(arrived, arrived, core_send, core_arrive, step, partner))

    def start(self):
        for step in (2, 1, 3):
            self.along[step - 1].start()
        self.across[0].start()
        self.own.start()

    def finish(self):
        for step in (1, 3, 2):
            self.along[step - 1].wait_recv()
            self.across[step].start()
        for copy in self.along:
            copy.wait_send()
        for copy in self.across:
            copy.wait()
        self.own.wait()


class Scatter:
    scratch = (
        pltpu.VMEM((SIDE, BLOCK, 2048), jnp.bfloat16),
        pltpu.VMEM((SIDE, BLOCK, 2048), jnp.bfloat16),
        pltpu.VMEM((3, BLOCK, 2048), jnp.bfloat16),
        pltpu.VMEM((3, BLOCK, 2048), jnp.bfloat16),
        pltpu.SemaphoreType.DMA((4,)),
        pltpu.SemaphoreType.DMA((4,)),
        pltpu.SemaphoreType.DMA((4,)),
        pltpu.SemaphoreType.DMA((3,)),
        pltpu.SemaphoreType.DMA((3,)),
    )

    def __init__(self, part, place, scratch):
        x, y, z_hi, z_lo, core = place
        self.own, self.other, self.leaving, self.arrived = scratch[:4]
        own_sem, core_send, core_arrive, x_send, x_arrive = scratch[4:]
        partner = device(x, y, z_hi, z_lo, 1 - core)
        self.across, self.load, self.along = [], [], []
        for step in range(SIDE):
            there = turned(x, step)
            self.across.append(
                remote(row_block(part, 1 - core, there), self.other.at[step], core_send, core_arrive, step, partner)
            )
            self.load.append(
                pltpu.make_async_copy(row_block(part, core, there), self.own.at[step], own_sem.at[step])
            )
        for step in (1, 2, 3):
            self.along.append(
                remote(
                    self.leaving.at[step - 1],
                    self.arrived.at[step - 1],
                    x_send,
                    x_arrive,
                    step - 1,
                    device(turned(x, step), y, z_hi, z_lo, core),
                )
            )

    def start(self):
        for step in (2, 1, 3, 0):
            self.across[step].start()
            self.load[step].start()
        for step in (2, 1, 3):
            self.across[step].wait_recv()
            self.load[step].wait()

            @pl.loop(0, BLOCK, step=16)
            def _(row):
                rows = pl.ds(pl.multiple_of(row, 16), 16)
                both = self.own[step, rows, :].astype(jnp.float32) + self.other[step, rows, :].astype(jnp.float32)
                self.leaving[step - 1, rows, :] = both.astype(jnp.bfloat16)

            self.along[step - 1].start()
        self.across[0].wait_recv()
        self.load[0].wait()

    def finish(self):
        for copy in self.along:
            copy.wait()
        for copy in self.across:
            copy.wait_send()

    def rows(self, rows):
        total = self.own[0, rows, :].astype(jnp.float32) + self.other[0, rows, :].astype(jnp.float32)
        for step in range(3):
            total = total + self.arrived[step, rows, :].astype(jnp.float32)
        return total


class Fetch:
    def __init__(self, weight, filled, quarter, place, sems, index):
        x, y, z_hi, z_lo, core = place
        send, arrive, own_sem = sems
        self.own = pltpu.make_async_copy(weight, filled, own_sem.at[index])
        mine = quarter(filled, y)
        across = device(x, y, 1 - z_hi, 1 - z_lo, z_hi)
        self.across = remote(quarter(weight, y), mine, send, arrive, index * 4, across)
        self.along = [
            remote(mine, mine, send, arrive, index * 4 + k, device(x, turned(y, k), z_hi, z_lo, core))
            for k in (1, 2, 3)
        ]

    def spread(self):
        self.across.wait_recv()
        for copy in self.along:
            copy.start()

    def finish(self):
        self.across.wait_send()
        for copy in self.along:
            copy.wait()


def fetch_scratch(count):
    return (
        pltpu.SemaphoreType.DMA((4 * count,)),
        pltpu.SemaphoreType.DMA((4 * count,)),
        pltpu.SemaphoreType.DMA((count,)),
    )


def fetch_peers(place):
    x, y, z_hi, z_lo, core = place
    return [device(x, y, 1 - z_hi, 1 - z_lo, z_hi)] + [
        device(x, turned(y, k), z_hi, z_lo, core) for k in (1, 2, 3)
    ]


def quarter_qkv(weight, y):
    return weight.at[:, pl.ds(pl.multiple_of(y * 512, 512), 512), :]


def quarter_out(weight, y):
    return weight.at[pl.ds(pl.multiple_of(y * 64, 64), 64), :]


def quarter_down(weight, y):
    return weight.at[pl.ds(pl.multiple_of(y * 176, 16), 176), :]


def quarter_gate_up(weight, y):
    return weight.at[:, pl.ds(pl.multiple_of(y * 176, 16), 176), :]


def moments(values):
    centre = values - jnp.mean(values, axis=-1, keepdims=True)
    return centre, lax.rsqrt(jnp.mean(centre * centre, axis=-1, keepdims=True) + 1e-05)


def tile_rows(body):
    @pl.loop(0, BLOCK, step=16)
    def _(row):
        body(pl.ds(pl.multiple_of(row, 16), 16))


def first_kernel(
    tokens,
    out_grad,
    live,
    gain,
    shift,
    qkv,
    out,
    down,
    tokens_here,
    cot_here,
    normed_full,
    cot_full,
    qkv_here,
    out_here,
    down_here,
    tok_buf,
    grad_buf,
    norm_buf,
    cot_buf,
    swap_send,
    swap_arrive,
    own_sems,
    *sems,
):
    place = here()
    x, y, z_hi, z_lo, core = place
    lacking = core != z_hi
    swap_with = device(x, y, core, z_lo, z_hi)
    fetch_sems = sems[10:]
    fetches = [
        Fetch(weight, filled, cut, place, fetch_sems, index)
        for index, (weight, filled, cut) in enumerate(
            [(qkv, qkv_here, quarter_qkv), (out, out_here, quarter_out), (down, down_here, quarter_down)]
        )
    ]
    swaps = [
        remote(source, target, swap_send, swap_arrive, index, swap_with)
        for index, (source, target) in enumerate([(tokens, tok_buf), (out_grad, grad_buf)])
    ]
    stays = [
        pltpu.make_async_copy(source, target, own_sems.at[index])
        for index, (source, target) in enumerate([(tokens, tok_buf), (out_grad, grad_buf)])
    ]

    @pl.when(lacking)
    def _():
        greet(line_peers(place) + [swap_with] + fetch_peers(place))
        swaps[0].start()
        for fetch in fetches:
            fetch.across.start()
        swaps[1].start()
        swaps[0].wait()

    @pl.when(jnp.logical_not(lacking))
    def _():
        greet(line_peers(place))
        for copy in stays:
            copy.start()
        for fetch in fetches:
            fetch.own.start()
        stays[0].wait()

    def norm(rows):
        centre, scale = moments(tok_buf[rows, :].astype(jnp.float32))
        norm_buf[rows, :] = (centre * scale * gain[...] + shift[...]).astype(jnp.bfloat16)

    tile_rows(norm)
    gather = Gather(norm_buf, normed_full, place, sems[:5])
    gather.start()
    tokens_out = pltpu.make_async_copy(tok_buf, tokens_here, own_sems.at[2])
    tokens_out.start()

    @pl.when(lacking)
    def _():
        fetches[0].spread()
        swaps[1].wait()

    @pl.when(jnp.logical_not(lacking))
    def _():
        stays[1].wait()

    def mask(rows):
        cot_buf[rows, :] = (grad_buf[rows, :].astype(jnp.float32) * live[rows, :]).astype(jnp.bfloat16)

    tile_rows(mask)
    gather_cot = Gather(cot_buf, cot_full, place, sems[5:10])
    gather_cot.start()
    cot_out = pltpu.make_async_copy(cot_buf, cot_here, own_sems.at[3])
    cot_out.start()

    @pl.when(lacking)
    def _():
        fetches[1].spread()
        fetches[2].spread()

    gather.finish()
    gather_cot.finish()
    tokens_out.wait()
    cot_out.wait()

    @pl.when(lacking)
    def _():
        for fetch in fetches:
            fetch.finish()

    @pl.when(jnp.logical_not(lacking))
    def _():
        for fetch in fetches:
            fetch.own.wait()


def middle_kernel(
    part, tokens, gain, shift, gate_up, mid, normed_full, gate_up_here, norm_buf, *scratch
):
    place = here()
    lacking = place[4] != place[2]
    scatter = Scatter(part, place, scratch[:9])
    gather = Gather(norm_buf, normed_full, place, scratch[9:14])
    fetch = Fetch(gate_up, gate_up_here, quarter_gate_up, place, scratch[14:], 0)

    @pl.when(lacking)
    def _():
        greet(line_peers(place) + fetch_peers(place))
        fetch.across.start()

    @pl.when(jnp.logical_not(lacking))
    def _():
        greet(line_peers(place))
        fetch.own.start()

    scatter.start()
    scatter.finish()

    def norm(rows):
        stream = tokens[rows, :].astype(jnp.float32) + scatter.rows(rows)
        mid[rows, :] = stream
        centre, scale = moments(stream)
        norm_buf[rows, :] = (centre * scale * gain[...] + shift[...]).astype(jnp.bfloat16)

    tile_rows(norm)
    gather.start()

    @pl.when(lacking)
    def _():
        fetch.spread()

    gather.finish()

    @pl.when(lacking)
    def _():
        fetch.finish()

    @pl.when(jnp.logical_not(lacking))
    def _():
        fetch.own.wait()


def back_kernel(part, mid, cot, gain, d_mid, d_full, gain_part, shift_part, low_buf, *scratch):
    place = here()
    scatter = Scatter(part, place, scratch[:9])
    gather = Gather(low_buf, d_full, place, scratch[9:])
    greet(line_peers(place))
    scatter.start()
    gain_part[...] = jnp.zeros_like(gain_part)
    shift_part[...] = jnp.zeros_like(shift_part)
    scatter.finish()

    def back(rows):
        grad = scatter.rows(rows)
        centre, scale = moments(mid[rows, :])
        unit = centre * scale
        gain_part[...] += jnp.sum(grad * unit, axis=0, keepdims=True)
        shift_part[...] += jnp.sum(grad, axis=0, keepdims=True)
        scaled = grad * gain[...]
        total = cot[rows, :].astype(jnp.float32) + scale * (
            scaled
            - jnp.mean(scaled, axis=-1, keepdims=True)
            - unit * jnp.mean(scaled * unit, axis=-1, keepdims=True)
        )
        d_mid[rows, :] = total
        low_buf[rows, :] = total.astype(jnp.bfloat16)

    tile_rows(back)
    gather.start()
    gather.finish()


def last_kernel(part, tokens, d_mid, gain, d_in, gain_part, shift_part, *scratch):
    place = here()
    scatter = Scatter(part, place, scratch)
    greet(line_peers(place))
    scatter.start()
    gain_part[...] = jnp.zeros_like(gain_part)
    shift_part[...] = jnp.zeros_like(shift_part)
    scatter.finish()

    def back(rows):
        grad = scatter.rows(rows)
        centre, scale = moments(tokens[rows, :].astype(jnp.float32))
        unit = centre * scale
        gain_part[...] += jnp.sum(grad * unit, axis=0, keepdims=True)
        shift_part[...] += jnp.sum(grad, axis=0, keepdims=True)
        scaled = grad * gain[...]
        d_in[rows, :] = d_mid[rows, :] + scale * (
            scaled
            - jnp.mean(scaled, axis=-1, keepdims=True)
            - unit * jnp.mean(scaled * unit, axis=-1, keepdims=True)
        )

    tile_rows(back)


ANY = pl.BlockSpec(memory_space=pl.ANY)
HELD = pl.BlockSpec(memory_space=pltpu.VMEM)


def call(kernel, collective_id, args, in_specs, outs, out_specs, scratch):
    return pl.pallas_call(
        kernel,
        out_shape=[jax.ShapeDtypeStruct(shape, kind) for shape, kind in outs],
        in_specs=in_specs,
        out_specs=out_specs,
        scratch_shapes=list(scratch),
        compiler_params=pltpu.CompilerParams(
            collective_id=collective_id, has_side_effects=True, vmem_limit_bytes=VMEM_LIMIT
        ),
    )(*args)


def member_layout(seq_length, seq_owner, member, row_total):
    entry_total = seq_length.shape[0]
    row_ids = jnp.arange(row_total, dtype=jnp.int32)
    entry_ids = jnp.arange(entry_total, dtype=jnp.int32)
    earlier = (entry_ids[:, None] < entry_ids[None, :]).astype(jnp.int32)
    sharing = (seq_owner[:, None] == seq_owner[None, :]).astype(jnp.int32)
    starts = jnp.sum(seq_length[:, None] * sharing * earlier, axis=0)
    owned_now = (seq_owner == member).astype(jnp.int32)
    inside = (
        owned_now[None, :]
        * (row_ids[:, None] >= starts[None, :]).astype(jnp.int32)
        * (row_ids[:, None] < (starts + seq_length)[None, :]).astype(jnp.int32)
    )
    live_rows = jnp.sum(inside, axis=1)
    segment = jnp.sum(inside * entry_ids[None, :], axis=1) + (1 - live_rows) * (
        entry_total + row_ids
    )
    position = jnp.sum(inside * (row_ids[:, None] - starts[None, :]), axis=1)
    return (segment, position, live_rows)


def rotary_tables(position):
    half_rot = ROT // 2
    frequency = jnp.power(
        jnp.float32(10000.0), -2.0 * jnp.arange(half_rot, dtype=jnp.float32) / ROT
    )
    angles = position.astype(jnp.float32)[:, None] * frequency[None, :]
    return (jnp.cos(angles)[:, None, :], jnp.sin(angles)[:, None, :])


def rotate(values, cosine, sine_table):
    half_rot = ROT // 2
    first_half = values[..., :half_rot]
    second_half = values[..., half_rot:ROT]
    return jnp.concatenate(
        [
            first_half * cosine - second_half * sine_table,
            second_half * cosine + first_half * sine_table,
            values[..., ROT:],
        ],
        axis=-1,
    )


def contract_rows(left_rows, right_rows):
    return lax.dot_general(
        left_rows, right_rows, (((0,), (0,)), ((), ())), preferred_element_type=jnp.float32
    )


def times_transposed(left_rows, right_rows):
    return lax.dot_general(
        left_rows, right_rows, (((1,), (1,)), ((), ())), preferred_element_type=jnp.float32
    )


def block_mask(segment, row_ids, begin_row, end_row):
    return (segment[begin_row:end_row, None] == segment[None, :end_row]) & (
        row_ids[None, :end_row] <= row_ids[begin_row:end_row, None]
    )


def owns(x, y, z_hi, z_lo, core):
    return core == z_hi


def sum_over_lines(parts):
    x, y, z_hi, z_lo, core = here()
    quarter = parts.shape[1] // SIDE

    def cut(k):
        return lax.dynamic_slice_in_dim(parts, turned(y, k) * quarter, quarter, 1)

    def along(k, held, only=lambda *place: True):
        return permute(
            held,
            lambda x, y, z_hi, z_lo, core: (x, (y + k) % 4, z_hi, z_lo, core)
            if only(x, y, z_hi, z_lo, core)
            else None,
        )

    arrived = [along(k, cut(k)) for k in (1, 2, 3)]
    total = cut(0).astype(jnp.float32)
    for piece in arrived:
        total = total + piece.astype(jnp.float32)
    total = total.astype(jnp.bfloat16)
    arrived = permute(
        total,
        lambda x, y, z_hi, z_lo, core: None
        if core == z_hi
        else (x, y, 1 - z_hi, 1 - z_lo, core),
    )
    total = (total.astype(jnp.float32) + arrived.astype(jnp.float32)).astype(jnp.bfloat16)
    arrived = permute(
        total,
        lambda x, y, z_hi, z_lo, core: (x, y, z_hi, 1 - z_lo, core) if core == z_hi else None,
    )
    total = (total.astype(jnp.float32) + arrived.astype(jnp.float32)).astype(jnp.bfloat16)
    pieces = [total] + [along(k, total, owns) for k in (1, 2, 3)]
    full = jnp.zeros_like(parts)
    for k, piece in enumerate(pieces):
        full = lax.dynamic_update_slice_in_dim(full, piece, turned(y, SIDE - k) * quarter, 1)
    arrived = permute(
        full,
        lambda x, y, z_hi, z_lo, core: (x, y, z_hi, z_lo, 1 - core) if core == z_hi else None,
    )
    return jnp.where(core == z_hi, full, arrived).astype(jnp.float32)


def body(
    tokens,
    seq_length,
    seq_owner,
    ln1_gain,
    ln1_bias,
    qkv_weight,
    qkv_bias,
    out_weight,
    ln2_gain,
    ln2_bias,
    gate_up_weight,
    down_weight,
    out_grad,
):
    bf16, f32 = jnp.bfloat16, jnp.float32
    x, y, z_hi, z_lo, core = here()
    row_total = BLOCK * 8
    rows_here, rows_all = (BLOCK, 2048), (row_total, 2048)
    local_heads = qkv_weight.shape[2] // HEAD_DIM
    member = (y * 2 + z_lo) * 2 + z_hi
    shard = core * SIDE + x
    score_scale = HEAD_DIM ** (-0.5)
    segment, position, live_rows = member_layout(seq_length, seq_owner, member, row_total)
    row_ids = jnp.arange(row_total, dtype=jnp.int32)
    live = lax.dynamic_slice_in_dim(live_rows, shard * BLOCK, BLOCK, 0)[:, None].astype(f32)
    bias = permute(qkv_bias, swap_rows)

    dma = pltpu.SemaphoreType.DMA
    tokens_here, cot, normed1, cot_rows, qkv, out, down = call(
        first_kernel,
        1,
        (tokens, out_grad, live, ln1_gain[None], ln1_bias[None], qkv_weight, out_weight, down_weight),
        [ANY, ANY, HELD, HELD, HELD, ANY, ANY, ANY],
        [
            (rows_here, bf16),
            (rows_here, bf16),
            (rows_all, bf16),
            (rows_all, bf16),
            (qkv_weight.shape, bf16),
            (out_weight.shape, bf16),
            (down_weight.shape, bf16),
        ],
        [ANY] * 4 + [HELD] * 3,
        (pltpu.VMEM(rows_here, bf16),) * 4
        + (dma((2,)), dma((2,)), dma((4,)))
        + Gather.scratch * 2
        + fetch_scratch(3),
    )

    cosine, sine_table = rotary_tables(position)
    projected = [
        jnp.dot(normed1, qkv[channel], preferred_element_type=jnp.float32) + bias[channel]
        for channel in range(3)
    ]
    queries = rotate(
        projected[0].reshape(row_total, local_heads, HEAD_DIM), cosine, sine_table
    ).astype(bf16)
    keys_low = rotate(
        projected[1].reshape(row_total, local_heads, HEAD_DIM), cosine, sine_table
    ).astype(bf16)
    values_low = projected[2].reshape(row_total, local_heads, HEAD_DIM).astype(bf16)
    block_size = min(512, row_total)
    block_count = row_total // block_size
    out_blocks = []
    log_norms = []
    for block_index in range(block_count):
        begin_row = block_index * block_size
        end_row = begin_row + block_size
        allowed = block_mask(segment, row_ids, begin_row, end_row)
        scores = (
            jnp.einsum(
                "qhd,khd->hqk",
                queries[begin_row:end_row],
                keys_low[:end_row],
                preferred_element_type=jnp.float32,
            )
            * score_scale
        )
        scores = jnp.where(allowed[None], scores, -1e30)
        row_max = jnp.max(scores, axis=-1, keepdims=True)
        exp_scores = jnp.exp(scores - row_max)
        exp_sum = jnp.sum(exp_scores, axis=-1, keepdims=True)
        attn_prob = (exp_scores / exp_sum).astype(bf16)
        out_blocks.append(
            jnp.einsum(
                "hqk,khd->qhd", attn_prob, values_low[:end_row], preferred_element_type=jnp.float32
            ).astype(bf16)
        )
        log_norms.append(row_max + jnp.log(exp_sum))
    attended = jnp.concatenate(out_blocks, axis=0).reshape(row_total, local_heads * HEAD_DIM)
    attn_part = jnp.dot(attended, out, preferred_element_type=jnp.float32).astype(bf16)

    gate_up_t = jnp.swapaxes(gate_up_weight, 1, 2)
    mid_stream, normed2, gate_up = call(
        middle_kernel,
        2,
        (attn_part, tokens_here, ln2_gain[None], ln2_bias[None], gate_up_t),
        [ANY, HELD, HELD, HELD, ANY],
        [(rows_here, f32), (rows_all, bf16), (gate_up_t.shape, bf16)],
        [HELD, ANY, HELD],
        (pltpu.VMEM(rows_here, bf16),) + Scatter.scratch + Gather.scratch + fetch_scratch(1),
    )

    gate_act = times_transposed(normed2, gate_up[0])
    up_act = times_transposed(normed2, gate_up[1])
    hidden = (jax.nn.silu(gate_act) * up_act).astype(bf16)
    d_hidden = times_transposed(cot_rows, down)
    sigmoid_g = jax.nn.sigmoid(gate_act)
    d_gate = (d_hidden * up_act * sigmoid_g * (1.0 + gate_act * (1.0 - sigmoid_g))).astype(bf16)
    d_up = (d_hidden * jax.nn.silu(gate_act)).astype(bf16)
    d_norm_part = (
        jnp.dot(d_gate, gate_up[0], preferred_element_type=f32)
        + jnp.dot(d_up, gate_up[1], preferred_element_type=f32)
    ).astype(bf16)

    d_mid, d_rows, gain2_part, shift2_part = call(
        back_kernel,
        3,
        (d_norm_part, mid_stream, cot, ln2_gain[None]),
        [ANY, HELD, HELD, HELD],
        [(rows_here, f32), (rows_all, bf16), ((1, 2048), f32), ((1, 2048), f32)],
        [HELD, ANY, HELD, HELD],
        (pltpu.VMEM(rows_here, bf16),) + Scatter.scratch + Gather.scratch,
    )

    ffn_part = jnp.dot(hidden, down, preferred_element_type=jnp.float32).astype(bf16)
    ffn_part = ffn_part.reshape(2, SIDE, BLOCK, 2048)
    kept = lax.dynamic_index_in_dim(ffn_part, core, 0, False)
    given = lax.dynamic_index_in_dim(ffn_part, 1 - core, 0, False)
    arrived = permute(given, lambda x, y, z_hi, z_lo, core: (x, y, z_hi, z_lo, 1 - core))
    both = (kept.astype(f32) + arrived.astype(f32)).astype(bf16)
    mixed = mid_stream + lax.dynamic_index_in_dim(both, x, 0, False).astype(f32)
    for k in (1, 2, 3):
        arrived = permute(
            lax.dynamic_index_in_dim(both, turned(x, k), 0, False),
            lambda x, y, z_hi, z_lo, core, k=k: ((x + k) % 4, y, z_hi, z_lo, core),
        )
        mixed = mixed + arrived.astype(f32)
    mixed = permute(mixed.astype(bf16), swap_rows)

    ffn_grad = jnp.stack(
        [contract_rows(d_gate, normed2), contract_rows(d_up, normed2), contract_rows(hidden, cot_rows)]
    ).astype(bf16)
    ffn_grad = sum_over_lines(ffn_grad)
    gate_up_grad, down_grad = jnp.swapaxes(ffn_grad[:2], 1, 2), ffn_grad[2]

    out_grad_t = contract_rows(d_rows, attended)
    d_attended = (
        times_transposed(d_rows, out).astype(bf16).reshape(row_total, local_heads, HEAD_DIM)
    )
    query_grads = []
    d_key = jnp.zeros((row_total, local_heads, HEAD_DIM), f32)
    d_value = jnp.zeros((row_total, local_heads, HEAD_DIM), f32)
    for block_index in range(block_count):
        begin_row = block_index * block_size
        end_row = begin_row + block_size
        allowed = block_mask(segment, row_ids, begin_row, end_row)
        query_block = queries[begin_row:end_row]
        key_block = keys_low[:end_row]
        grad_block = d_attended[begin_row:end_row]
        scores = (
            jnp.einsum("qhd,khd->hqk", query_block, key_block, preferred_element_type=jnp.float32)
            * score_scale
        )
        scores = jnp.where(allowed[None], scores, -1e30)
        attn_full = jnp.exp(scores - log_norms[block_index])
        attn_prob = attn_full.astype(bf16)
        d_prob = jnp.einsum(
            "qhd,khd->hqk", grad_block, values_low[:end_row], preferred_element_type=jnp.float32
        )
        row_dots = jnp.sum(attn_full * d_prob, axis=-1, keepdims=True)
        d_score = (attn_full * (d_prob - row_dots)).astype(bf16)
        query_grads.append(
            jnp.einsum("hqk,khd->qhd", d_score, key_block, preferred_element_type=jnp.float32)
            * score_scale
        )
        d_key = d_key.at[:end_row].add(
            jnp.einsum("hqk,qhd->khd", d_score, query_block, preferred_element_type=jnp.float32)
            * score_scale
        )
        d_value = d_value.at[:end_row].add(
            jnp.einsum("hqk,qhd->khd", attn_prob, grad_block, preferred_element_type=jnp.float32)
        )
    d_query = jnp.concatenate(query_grads, axis=0)
    d_proj = [
        rotate(d_query, cosine, -sine_table).reshape(row_total, -1).astype(bf16),
        rotate(d_key, cosine, -sine_table).reshape(row_total, -1).astype(bf16),
        d_value.reshape(row_total, -1).astype(bf16),
    ]
    summed = times_transposed(d_proj[0], qkv[0])
    summed = summed + times_transposed(d_proj[1], qkv[1])
    d_norm_part = (summed + times_transposed(d_proj[2], qkv[2])).astype(bf16)

    d_in, gain1_part, shift1_part = call(
        last_kernel,
        4,
        (d_norm_part, tokens_here, d_mid, ln1_gain[None]),
        [ANY, HELD, HELD, HELD],
        [(rows_here, f32), ((1, 2048), f32), ((1, 2048), f32)],
        [HELD, HELD, HELD],
        Scatter.scratch,
    )
    input_grad = permute(d_in, swap_rows)

    attn_grad = jnp.stack(
        [contract_rows(normed1, d_proj[channel]) for channel in range(3)] + [out_grad_t]
    ).astype(bf16)
    attn_grad = sum_over_lines(attn_grad)
    qkv_weight_grad, out_weight_grad = attn_grad[:3], attn_grad[3].T

    bias_part = jnp.stack([jnp.sum(d.astype(f32), axis=0) for d in d_proj])
    spread = jnp.zeros((8, 3, bias_part.shape[1]), f32)
    spread = lax.dynamic_update_slice_in_dim(spread, bias_part[None], shard, 0)
    norm_grads, bias_all = lax.psum(
        (jnp.concatenate([gain1_part, shift1_part, gain2_part, shift2_part]), spread), AXES
    )
    qkv_bias_grad = lax.dynamic_index_in_dim(bias_all, z_hi * SIDE + x, 0, False)
    return (
        mixed,
        input_grad,
        norm_grads[0],
        norm_grads[1],
        qkv_weight_grad,
        qkv_bias_grad,
        out_weight_grad,
        norm_grads[2],
        norm_grads[3],
        gate_up_grad,
        down_grad,
    )


def solution(mesh):
    placed = (
        P(("dp", "tensor"), None),
        P(),
        P(),
        P(),
        P(),
        P(None, None, "tensor"),
        P(None, "tensor"),
        P("tensor", None),
        P(),
        P(),
        P(None, None, "tensor"),
        P("tensor", None),
        P(("dp", "tensor"), None),
    )
    return jax.shard_map(
        body,
        mesh=mesh,
        in_specs=placed,
        out_specs=(
            P(("dp", "tensor"), None),
            P(("dp", "tensor"), None),
            P(),
            P(),
            P(None, None, "tensor"),
            P(None, "tensor"),
            P("tensor", None),
            P(),
            P(),
            P(None, None, "tensor"),
            P("tensor", None),
        ),
        check_vma=False,
    )
```

```python
import functools

import jax
import jax.numpy as jnp
from jax import lax
from jax.experimental import pallas as pl
from jax.experimental.pallas import tpu as pltpu
from jax.sharding import PartitionSpec as P

HEAD_DIM = 64
ROT = 16
SIDE = 4
BLOCK = 128
AXES = ("dp", "tensor")
MESH = pl.DeviceIdType.MESH
VMEM_LIMIT = 50 * 2**20


def here():
    dp, tensor = lax.axis_index("dp"), lax.axis_index("tensor")
    x, z_hi = lax.rem(tensor, SIDE), lax.div(tensor, SIDE)
    y, z_lo, core = lax.div(dp, SIDE), lax.rem(lax.div(dp, 2), 2), lax.rem(dp, 2)
    return x, y, z_hi, z_lo, core


def device(x, y, z_hi, z_lo, core):
    return ((y * 2 + z_lo) * 2 + core, z_hi * SIDE + x)


def turned(value, by):
    return lax.rem(value + by, SIDE)


def pairs(move):
    found = []
    for dp in range(16):
        for tensor in range(8):
            goal = move(tensor % 4, dp // 4, tensor // 4, (dp // 2) % 2, dp % 2)
            if goal is not None:
                to_dp, to_tensor = device(*goal)
                found.append((dp * 8 + tensor, to_dp * 8 + to_tensor))
    return found


def permute(array, move):
    return lax.ppermute(array, AXES, pairs(move))


def swap_rows(x, y, z_hi, z_lo, core):
    return (x, y, core, z_lo, z_hi)


def remote(source, target, sends, arrives, index, device_id):
    return pltpu.make_async_remote_copy(
        src_ref=source,
        dst_ref=target,
        send_sem=sends.at[index],
        recv_sem=arrives.at[index],
        device_id=device_id,
        device_id_type=MESH,
    )


def greet(peers):
    barrier = pltpu.get_barrier_semaphore()
    for peer in peers:
        pl.semaphore_signal(barrier, inc=1, device_id=peer, device_id_type=MESH)
    pl.semaphore_wait(barrier, len(peers))


def line_peers(place):
    x, y, z_hi, z_lo, core = place
    found = [device(turned(x, k), y, z_hi, z_lo, core) for k in (1, 2, 3)]
    return found + [device(x, y, z_hi, z_lo, 1 - core)]


def row_block(full, core, x):
    return full.at[pl.ds(pl.multiple_of((core * SIDE + x) * BLOCK, BLOCK), BLOCK)]


class ByRow:
    def __init__(self, full, place):
        self.full, self.x, self.core = full, place[0], place[4]

    def at(self, step, other):
        core = 1 - self.core if other else self.core
        return row_block(self.full, core, turned(self.x, SIDE - step))

    def landing(self, step, other, by, across):
        return self.at(step, other)


class ByStep:
    def __init__(self, full):
        self.full = full

    def at(self, step, other):
        return self.full.at[pl.ds((step * 2 + other) * BLOCK, BLOCK)]

    def landing(self, step, other, by, across):
        return self.at((step + by) % SIDE, 1 - other if across else other)


class Gather:
    scratch = (
        pltpu.SemaphoreType.DMA((4,)),
        pltpu.SemaphoreType.DMA((4,)),
        pltpu.SemaphoreType.DMA((4,)),
        pltpu.SemaphoreType.DMA((4,)),
    )

    def __init__(self, block, layout, place, sems):
        x, y, z_hi, z_lo, core = place
        x_send, x_arrive, core_send, core_arrive = sems
        half = BLOCK // 2
        right = device(turned(x, 1), y, z_hi, z_lo, core)
        left = device(turned(x, 3), y, z_hi, z_lo, core)
        partner = device(x, y, z_hi, z_lo, 1 - core)

        def passed(step, first, by, index, to):
            part = pl.ds(first, half)
            return remote(
                layout.at(step, 0).at[part],
                layout.landing(step, 0, by, False).at[part],
                x_send,
                x_arrive,
                index,
                to,
            )

        self.right = remote(block, layout.landing(0, 0, 1, False), x_send, x_arrive, 0, right)
        self.left = remote(block, layout.landing(0, 0, 3, False), x_send, x_arrive, 1, left)
        self.right_on = passed(1, 0, 1, 2, right)
        self.left_on = passed(3, half, 3, 3, left)
        self.across = [
            remote(
                block if step == 0 else layout.at(step, 0),
                layout.landing(step, 0, 0, True),
                core_send,
                core_arrive,
                step,
                partner,
            )
            for step in range(SIDE)
        ]

    def start(self):
        self.right.start()
        self.left.start()
        self.across[0].start()

    def arrive(self, step):
        if step == 1:
            self.right.wait_recv()
            self.right_on.start()
        elif step == 3:
            self.left.wait_recv()
            self.left_on.start()
        else:
            self.right_on.wait_recv()
            self.left_on.wait_recv()
        self.across[step].start()

    def finish(self):
        for copy in (self.right, self.left, self.right_on, self.left_on, *self.across):
            copy.wait_send()

    def take(self):
        for copy in self.across:
            copy.wait_recv()


class Scatter:
    buffers = (
        pltpu.VMEM((SIDE, BLOCK, 2048), jnp.bfloat16),
        pltpu.VMEM((3, BLOCK, 2048), jnp.bfloat16),
        pltpu.VMEM((3, BLOCK, 2048), jnp.bfloat16),
    )
    sems = (
        pltpu.SemaphoreType.DMA((SIDE,)),
        pltpu.SemaphoreType.DMA((SIDE,)),
        pltpu.SemaphoreType.DMA((3,)),
        pltpu.SemaphoreType.DMA((3,)),
    )
    scratch = buffers + sems

    def __init__(self, own, given, place, scratch):
        x, y, z_hi, z_lo, core = place
        self.own, (self.other, self.leaving, self.arrived) = own, scratch[:3]
        core_send, core_arrive, x_send, x_arrive = scratch[3:]
        partner = device(x, y, z_hi, z_lo, 1 - core)
        self.across = [
            remote(given(step), self.other.at[step], core_send, core_arrive, step, partner)
            for step in range(SIDE)
        ]
        self.along = [
            remote(
                self.leaving.at[step - 1],
                self.arrived.at[step - 1],
                x_send,
                x_arrive,
                step - 1,
                device(turned(x, SIDE - step), y, z_hi, z_lo, core),
            )
            for step in (1, 2, 3)
        ]

    def merge(self, step):
        self.across[step].wait_recv()

        def add(rows):
            both = self.own(step, rows).astype(jnp.float32) + self.other[step, rows, :].astype(jnp.float32)
            self.leaving[step - 1, rows, :] = both.astype(jnp.bfloat16)

        tile_rows(add)
        self.along[step - 1].start()

    def finish(self):
        self.across[0].wait_recv()
        for copy in self.along:
            copy.wait()
        for copy in self.across:
            copy.wait_send()

    def rows(self, rows):
        total = self.own(0, rows).astype(jnp.float32) + self.other[0, rows, :].astype(jnp.float32)
        for step in range(3):
            total = total + self.arrived[step, rows, :].astype(jnp.float32)
        return total


class Loaded:
    def __init__(self, full, held, place, sems):
        there, here_ = ByRow(full, place), ByStep(held)
        self.copies = [
            pltpu.make_async_copy(there.at(step, other), here_.at(step, other), sems.at[step * 2 + other])
            for step in range(SIDE)
            for other in range(2)
        ]

    def start(self):
        for copy in self.copies:
            copy.start()

    def wait(self):
        for copy in self.copies:
            copy.wait()


class Fetch:
    def __init__(self, weight, filled, cut, place, sems, index):
        x, y, z_hi, z_lo, core = place
        send, arrive, own_sem = sems
        self.own = pltpu.make_async_copy(weight, filled, own_sem.at[index])
        across = device(x, y, 1 - z_hi, 1 - z_lo, z_hi)
        up = device(x, turned(y, 1), z_hi, z_lo, core)
        down = device(x, turned(y, 3), z_hi, z_lo, core)
        base = index * 5

        def moved(ref, quarter, half, slot, to):
            source = cut(ref, quarter, half)
            return remote(source, cut(filled, quarter, half), send, arrive, base + slot, to)

        self.across = moved(weight, y, None, 0, across)
        self.up = moved(filled, y, None, 1, up)
        self.down = moved(filled, y, None, 2, down)
        self.up_on = moved(filled, turned(y, 3), 0, 3, up)
        self.down_on = moved(filled, turned(y, 1), 1, 4, down)

    def spread(self):
        self.across.wait_recv()
        self.up.start()
        self.down.start()

    def pass_on(self):
        self.up.wait_recv()
        self.up_on.start()
        self.down.wait_recv()
        self.down_on.start()

    def finish(self):
        self.up_on.wait_recv()
        self.down_on.wait_recv()
        for copy in (self.across, self.up, self.down, self.up_on, self.down_on):
            copy.wait_send()


def fetch_scratch(count):
    return (
        pltpu.SemaphoreType.DMA((5 * count,)),
        pltpu.SemaphoreType.DMA((5 * count,)),
        pltpu.SemaphoreType.DMA((count,)),
    )


def fetch_peers(place):
    x, y, z_hi, z_lo, core = place
    return [device(x, y, 1 - z_hi, 1 - z_lo, z_hi)] + [
        device(x, turned(y, k), z_hi, z_lo, core) for k in (1, 3)
    ]


def quarter_rows(size, *before):
    quarter_size = size // SIDE
    split = -(-quarter_size // 32) * 16

    def cut(weight, quarter, half):
        first = pl.multiple_of(quarter * quarter_size, 16)
        if half is None:
            rows = pl.ds(first, quarter_size)
        elif half == 0:
            rows = pl.ds(first, split)
        else:
            rows = pl.ds(first + split, quarter_size - split)
        return weight.at[(*before, rows)]

    return cut


QKV_CUT = quarter_rows(2048, slice(None))
OUT_CUT = quarter_rows(256)
FF_CUT = quarter_rows(704)


def moments(values):
    centre = values - jnp.mean(values, axis=-1, keepdims=True)
    return centre, lax.rsqrt(jnp.mean(centre * centre, axis=-1, keepdims=True) + 1e-05)


def tile_rows(body):
    @pl.loop(0, BLOCK, step=16)
    def _(row):
        body(pl.ds(pl.multiple_of(row, 16), 16))


def first_kernel(
    tokens,
    out_grad,
    live,
    gain,
    shift,
    qkv,
    out,
    down,
    tokens_here,
    cot_here,
    normed_full,
    cot_full,
    qkv_here,
    out_here,
    down_here,
    tok_buf,
    grad_buf,
    norm_buf,
    cot_buf,
    swap_send,
    swap_arrive,
    own_sems,
    *sems,
):
    place = here()
    x, y, z_hi, z_lo, core = place
    lacking = core != z_hi
    swap_with = device(x, y, core, z_lo, z_hi)
    fetch_sems = sems[8:]
    fetches = [
        Fetch(weight, filled, cut, place, fetch_sems, index)
        for index, (weight, filled, cut) in enumerate(
            [(qkv, qkv_here, QKV_CUT), (out, out_here, OUT_CUT), (down, down_here, FF_CUT)]
        )
    ]
    swaps = [
        remote(source, target, swap_send, swap_arrive, index, swap_with)
        for index, (source, target) in enumerate([(tokens, tok_buf), (out_grad, grad_buf)])
    ]
    stays = [
        pltpu.make_async_copy(source, target, own_sems.at[index])
        for index, (source, target) in enumerate([(tokens, tok_buf), (out_grad, grad_buf)])
    ]

    @pl.when(lacking)
    def _():
        greet(line_peers(place) + [swap_with] + fetch_peers(place))
        swaps[0].start()
        swaps[0].wait_recv()
        fetches[0].across.start()
        swaps[1].start()
        fetches[1].across.start()
        fetches[2].across.start()

    @pl.when(jnp.logical_not(lacking))
    def _():
        greet(line_peers(place))
        for copy in stays:
            copy.start()
        for fetch in fetches:
            fetch.own.start()
        stays[0].wait()

    def norm(rows):
        centre, scale = moments(tok_buf[rows, :].astype(jnp.float32))
        norm_buf[rows, :] = (centre * scale * gain[...] + shift[...]).astype(jnp.bfloat16)

    tile_rows(norm)
    gather = Gather(norm_buf, ByRow(normed_full, place), place, sems[:4])
    gather_cot = Gather(cot_buf, ByRow(cot_full, place), place, sems[4:8])
    stored = [
        pltpu.make_async_copy(source, target, own_sems.at[2 + index])
        for index, (source, target) in enumerate(
            [
                (norm_buf, row_block(normed_full, core, x)),
                (tok_buf, tokens_here),
                (cot_buf, cot_here),
                (cot_buf, row_block(cot_full, core, x)),
            ]
        )
    ]
    gather.start()
    stored[0].start()
    stored[1].start()

    @pl.when(lacking)
    def _():
        fetches[0].spread()
        swaps[0].wait_send()
        swaps[1].wait()

    @pl.when(jnp.logical_not(lacking))
    def _():
        stays[1].wait()

    def mask(rows):
        cot_buf[rows, :] = (grad_buf[rows, :].astype(jnp.float32) * live[rows, :]).astype(jnp.bfloat16)

    tile_rows(mask)
    gather_cot.start()
    stored[2].start()
    stored[3].start()
    gather.arrive(1)
    gather.arrive(3)

    @pl.when(lacking)
    def _():
        fetches[1].spread()
        fetches[2].spread()
        fetches[0].pass_on()

    gather.arrive(2)
    gather_cot.arrive(1)
    gather_cot.arrive(3)

    @pl.when(lacking)
    def _():
        fetches[1].pass_on()
        fetches[2].pass_on()

    gather_cot.arrive(2)
    for each in (gather, gather_cot):
        each.take()
        each.finish()
    for copy in stored:
        copy.wait()

    @pl.when(lacking)
    def _():
        for fetch in fetches:
            fetch.finish()

    @pl.when(jnp.logical_not(lacking))
    def _():
        for fetch in fetches:
            fetch.own.wait()


def matmul(left, right, contract):
    return lax.dot_general(left, right, ((contract, ((), ()))), preferred_element_type=jnp.float32)


NN, NT, TN = ((1,), (0,)), ((1,), (1,)), ((0,), (0,))
PAIR = 2 * BLOCK


def middle_kernel(
    part,
    tokens,
    gain,
    shift,
    gate_up_own,
    down_held,
    cot_full,
    attended_full,
    out_held,
    cot,
    mid,
    d_mid,
    gain_part,
    shift_part,
    grads,
    ffn_part,
    d_attended,
    out_grad,
    gate_up,
    down,
    out,
    normed,
    cot_rows,
    d_rows,
    attended,
    hidden,
    d_gate,
    d_up,
    d_hidden,
    own_rows,
    given_terms,
    ffn_tile,
    grad_tile,
    load_sems,
    att_sems,
    own_sems,
    ffn_sem,
    grad_sems,
    *scratch,
):
    bf16 = jnp.bfloat16
    place = here()
    x, y, z_hi, z_lo, core = place
    lacking = core != z_hi
    attn = ByRow(part, place)
    first = Scatter(
        lambda step, rows: own_rows[step, rows, :], lambda step: attn.at(step, 1), place, scratch[:7]
    )
    second = Scatter(
        lambda step, rows: own_rows[step, rows, :],
        lambda step: given_terms.at[step],
        place,
        scratch[:3] + scratch[7:11],
    )
    gather = Gather(normed.at[pl.ds(0, BLOCK)], ByStep(normed), place, scratch[11:15])
    gather_d = Gather(d_rows.at[pl.ds(0, BLOCK)], ByStep(d_rows), place, scratch[15:19])
    fetches = [
        Fetch(gate_up_own.at[index], gate_up.at[index], FF_CUT, place, scratch[19:], index) for index in range(2)
    ]
    load_cot = Loaded(cot_full, cot_rows, place, load_sems)
    load_att = Loaded(attended_full, attended, place, att_sems)
    load_own = [
        pltpu.make_async_copy(attn.at(step, 0), own_rows.at[step], own_sems.at[step]) for step in range(SIDE)
    ]
    load_down = pltpu.make_async_copy(down_held, down, own_sems.at[4])
    load_out = pltpu.make_async_copy(out_held, out, own_sems.at[5])

    for copy in load_own:
        copy.start()
    load_down.start()
    load_cot.start()
    load_att.start()
    load_out.start()

    @pl.when(lacking)
    def _():
        greet(line_peers(place) + fetch_peers(place))

    @pl.when(jnp.logical_not(lacking))
    def _():
        greet(line_peers(place))

    for step in (2, 1, 3, 0):
        first.across[step].start()

    @pl.when(lacking)
    def _():
        for fetch in fetches:
            fetch.across.start()

    @pl.when(jnp.logical_not(lacking))
    def _():
        for fetch in fetches:
            fetch.own.start()

    for copy in load_own:
        copy.wait()
    for step in (2, 1, 3):
        first.merge(step)
    load_down.wait()
    load_cot.wait()

    @pl.loop(0, 2)
    def _(index):
        rows = pl.ds(pl.multiple_of(index * PAIR, PAIR), PAIR)
        d_hidden[rows, :] = matmul(cot_rows[rows, :], down[...], NT)

    @pl.when(lacking)
    def _():
        for fetch in fetches:
            fetch.spread()

    @pl.loop(2, 4)
    def _(index):
        rows = pl.ds(pl.multiple_of(index * PAIR, PAIR), PAIR)
        d_hidden[rows, :] = matmul(cot_rows[rows, :], down[...], NT)

    first.finish()

    def norm(rows):
        stream = tokens[rows, :].astype(jnp.float32) + first.rows(rows)
        mid[rows, :] = stream
        centre, scale = moments(stream)
        normed[rows, :] = (centre * scale * gain[...] + shift[...]).astype(bf16)

    tile_rows(norm)
    gather.start()

    @pl.when(lacking)
    def _():
        for fetch in fetches:
            fetch.pass_on()
        for fetch in fetches:
            fetch.finish()

    @pl.when(jnp.logical_not(lacking))
    def _():
        for fetch in fetches:
            fetch.own.wait()

    order = (0, 1, 3, 2)

    @pl.loop(0, 4)
    def _(turn):
        step = turn + lax.div(turn, 2) * (5 - 2 * turn)
        for index in range(4):

            @pl.when(turn == index)
            def _(index=index):
                for arrived in ((), (1, 3), (), (2,))[index]:
                    gather.arrive(arrived)
                gather.across[order[index]].wait_recv()

        rows = pl.ds(pl.multiple_of(step * PAIR, PAIR), PAIR)
        gate = matmul(normed[rows, :], gate_up[0], NT)
        up = matmul(normed[rows, :], gate_up[1], NT)
        sigmoid = jax.nn.sigmoid(gate)
        silu = gate * sigmoid
        hidden[rows, :] = (silu * up).astype(bf16)
        d_hid = d_hidden[rows, :]
        d_gate[rows, :] = (d_hid * up * sigmoid * (1.0 + gate * (1.0 - sigmoid))).astype(bf16)
        d_up[rows, :] = (d_hid * silu).astype(bf16)
        for index in (2, 3):

            @pl.when(turn == index)
            def _(index=index):
                second.merge(order[index - 1])

        @pl.loop(0, 2048, step=512)
        def _(column):
            columns = pl.ds(pl.multiple_of(column, 512), 512)
            terms = matmul(d_gate[rows, :], gate_up[0, :, columns], NN) + matmul(
                d_up[rows, :], gate_up[1, :, columns], NN
            )
            terms = terms.astype(bf16)
            own_rows[step, :, columns] = terms[:BLOCK]
            given_terms[step, :, columns] = terms[BLOCK:]

        for index in range(4):

            @pl.when(turn == index)
            def _(index=index):
                second.across[order[index]].start()

    second.merge(2)
    load_att.wait()
    load_out.wait()

    @pl.loop(0, 4)
    def _(index):
        rows = pl.ds(pl.multiple_of(index * PAIR, PAIR), PAIR)

        @pl.when(index > 0)
        def _():
            pltpu.make_async_copy(ffn_tile, ffn_part.at[rows], ffn_sem).wait()

        @pl.loop(0, 2048, step=512)
        def _(column):
            columns = pl.ds(pl.multiple_of(column, 512), 512)
            ffn_tile[:, columns] = matmul(hidden[rows, :], down[:, columns], NN).astype(bf16)

        pltpu.make_async_copy(ffn_tile, ffn_part.at[rows], ffn_sem).start()

    def weight_grad(index, left, right):
        @pl.loop(0, 4)
        def _(tile):
            columns = pl.ds(pl.multiple_of(tile * 512, 512), 512)
            target = grads.at[index, :, columns]
            slot = lax.rem(tile, 2)
            copy = pltpu.make_async_copy(grad_tile.at[slot], target, grad_sems.at[slot])

            @pl.when(jnp.logical_or(index > 0, tile > 1))
            def _():
                copy.wait()

            grad_tile[slot] = matmul(left[...], right[:, columns], TN).astype(bf16)
            copy.start()

    weight_grad(0, d_gate, normed)
    second.finish()
    gain_part[...] = jnp.zeros_like(gain_part)
    shift_part[...] = jnp.zeros_like(shift_part)

    def back(rows):
        grad = second.rows(rows)
        centre, scale = moments(mid[rows, :])
        unit = centre * scale
        gain_part[...] += jnp.sum(grad * unit, axis=0, keepdims=True)
        shift_part[...] += jnp.sum(grad, axis=0, keepdims=True)
        scaled = grad * gain[...]
        total = cot[rows, :].astype(jnp.float32) + scale * (
            scaled
            - jnp.mean(scaled, axis=-1, keepdims=True)
            - unit * jnp.mean(scaled * unit, axis=-1, keepdims=True)
        )
        d_mid[rows, :] = total
        d_rows[rows, :] = total.astype(bf16)

    tile_rows(back)
    gather_d.start()
    weight_grad(1, d_up, normed)
    gather_d.arrive(1)
    gather_d.arrive(3)
    weight_grad(2, hidden, cot_rows)
    gather_d.arrive(2)
    for step in range(SIDE):
        gather_d.across[step].wait_recv()
        terms = matmul(d_rows[pl.ds(step * PAIR, PAIR), :], out[...], NT).astype(bf16)
        behind = turned(x, SIDE - step)
        for other in range(2):
            whose = (1 - core) if other else core
            first_row = pl.multiple_of((whose * SIDE + behind) * BLOCK, BLOCK)
            d_attended[pl.ds(first_row, BLOCK), :] = terms[other * BLOCK : (other + 1) * BLOCK]

    @pl.loop(0, 2048, step=512)
    def _(column):
        columns = pl.ds(pl.multiple_of(column, 512), 512)
        out_grad[:, columns] = matmul(attended[...], d_rows[:, columns], TN).astype(bf16)

    gather.finish()
    gather_d.finish()
    pltpu.make_async_copy(ffn_tile, ffn_part.at[pl.ds(0, PAIR)], ffn_sem).wait()
    for slot in range(2):
        pltpu.make_async_copy(grad_tile.at[slot], grads.at[0, :, pl.ds(0, 512)], grad_sems.at[slot]).wait()


class Links:
    def __init__(self, sends, arrives):
        self.sends, self.arrives, self.used = sends, arrives, 0

    def to(self, source, target, device_id):
        self.used += 1
        return remote(source, target, self.sends, self.arrives, self.used - 1, device_id)


class Locals:
    def __init__(self, sems):
        self.sems, self.used = sems, 0

    def of(self, source, target):
        self.used += 1
        return pltpu.make_async_copy(source, target, self.sems.at[self.used - 1])


def each_rows(count, step, body):
    if count == step:
        body(pl.ds(0, count))
        return

    @pl.loop(0, count, step=step)
    def _(row):
        body(pl.ds(pl.multiple_of(row, 16), step))


def add_into(target, *terms, count, step):
    def body(rows):
        total = terms[0](rows).astype(jnp.float32)
        for term in terms[1:]:
            total = total + term(rows).astype(jnp.float32)
        target[rows, :] = total.astype(jnp.bfloat16)

    each_rows(count, step, body)


def of(ref, first=0):
    return lambda rows: ref[pl.ds(rows.start + first, rows.size), :]


class Around:
    def __init__(self, place):
        x, y, z_hi, z_lo, core = place
        self.y, self.z_lo = y, z_lo
        self.up = device(x, turned(y, 1), z_hi, z_lo, core)
        self.down = device(x, turned(y, 3), z_hi, z_lo, core)
        self.beyond = device(x, y, 1 - z_hi, 1 - z_lo, core)
        self.twin = device(x, y, z_hi, 1 - z_lo, core)
        self.partner = device(x, y, z_hi, z_lo, 1 - core)
        self.keeps = core == z_hi
        self.gives = jnp.logical_not(self.keeps)


class RowRing:
    def __init__(self, size, width, step):
        self.size, self.width, self.step = size, width, step
        self.split = -(-size // 32) * 16

    def scratch(self):
        kind = jnp.bfloat16
        return (
            pltpu.VMEM((self.split, self.width), kind),
            pltpu.VMEM((self.size - self.split, self.width), kind),
            pltpu.VMEM((self.size, self.width), kind),
            pltpu.VMEM((self.size, self.width), kind),
            pltpu.VMEM((self.size, self.width), kind),
        )

    def quarter(self, ref, index, first=0):
        return ref.at[pl.ds(pl.multiple_of(first + index * self.size, 16), self.size)]

    def halves(self, ref):
        return ref.at[pl.ds(0, self.split)], ref.at[pl.ds(self.split, self.size - self.split)]

    def bind(self, links, around, scratch, far, up_terms, down_terms, own_terms):
        self.from_below, self.from_above, self.got_up, self.got_down, self.total = scratch
        self.up_terms, self.down_terms, self.own_terms = up_terms, down_terms, own_terms
        first, second = self.halves(far)
        self.first = (
            links.to(first, self.from_below, around.up),
            links.to(second, self.from_above, around.down),
        )
        self.second = (
            links.to(up_terms, self.got_up, around.up),
            links.to(down_terms, self.got_down, around.down),
        )

    def begin(self):
        for copy in self.first:
            copy.start()

    def merge(self):
        self.first[0].wait_recv()
        low, high = self.split, self.size - self.split
        up_low, _ = self.halves(self.up_terms)
        _, down_high = self.halves(self.down_terms)
        add_into(up_low, of(up_low), of(self.from_below), count=low, step=low)
        self.second[0].start()
        self.first[1].wait_recv()
        add_into(down_high, of(down_high), of(self.from_above), count=high, step=high)
        self.second[1].start()

    def sum(self):
        for copy in self.second:
            copy.wait_recv()
        add_into(
            self.total,
            of(self.own_terms),
            of(self.got_up),
            of(self.got_down),
            count=self.size,
            step=self.step,
        )

    def sent(self):
        for copy in (*self.first, *self.second):
            copy.wait_send()


class RowSpread:
    def __init__(self, ring, links, locals_, around, total, full, first=0):
        y = around.y
        mine = ring.quarter(full, y, first)
        below, above = ring.quarter(full, turned(y, 3), first), ring.quarter(full, turned(y, 1), first)
        self.own = locals_.of(total, mine)
        self.direct = (links.to(total, mine, around.up), links.to(total, mine, around.down))
        low, high = ring.halves(below)[0], ring.halves(above)[1]
        self.passed = (links.to(low, low, around.up), links.to(high, high, around.down))

    def begin(self):
        self.own.start()
        for copy in self.direct:
            copy.start()

    def pass_on(self):
        for copy, onward in zip(self.direct, self.passed):
            copy.wait_recv()
            onward.start()

    def end(self):
        self.own.wait()
        for copy in self.passed:
            copy.wait_recv()

    def sent(self):
        for copy in (*self.direct, *self.passed):
            copy.wait_send()


WIDE = 512
FF_RING = (528, 256, 176)
ATTN_UNITS = (((768, 256, 96), 0), ((768, 256, 96), 3072), ((64, 2048, 16), 0))
FF_STEPS, ATTN_STEPS = 9, 8
FF_LINKS, ATTN_LINKS = 12, 11


def ff_scratch(rows):
    kind = jnp.bfloat16
    return (
        pltpu.VMEM((rows, WIDE), kind),
        pltpu.VMEM((rows, WIDE // 2), kind),
    ) + RowRing(*FF_RING).scratch()


def attn_scratch(unit):
    ring = RowRing(*unit[0])
    held = pltpu.VMEM((ring.size, ring.width), jnp.bfloat16)
    return (held,) * 5 + ring.scratch()


def ff_sum(part, full, column, links, locals_, around, mine, scratch):
    got, half = scratch[:2]
    rows = got.shape[0]
    width = WIDE // 2
    ring = RowRing(*FF_RING)
    stretch = lambda ref: ref.at[:, pl.ds(column, WIDE)]
    side = lambda z_lo: pl.ds(pl.multiple_of(z_lo * width, 128), width)
    placed = lambda z_lo: full.at[:, pl.ds(pl.multiple_of(column + z_lo * width, 128), width)]
    load = locals_.of(stretch(part), mine)
    over = links.to(stretch(part), got, around.beyond)
    kept, sent_on = side(around.z_lo), side(1 - around.z_lo)
    twin = links.to(got.at[:, sent_on], half, around.twin)
    y = around.y
    quarter = lambda k: ring.quarter(half, turned(y, k))
    ring.bind(links, around, scratch[2:], quarter(2), quarter(1), quarter(3), quarter(0))
    own_side = placed(around.z_lo)
    spread = RowSpread(ring, links, locals_, around, ring.total, own_side)
    both = links.to(own_side, own_side, around.twin)
    core = links.to(stretch(full), stretch(full), around.partner)

    @pl.when(around.gives)
    def _():
        over.start()

    @pl.when(around.keeps)
    def _():
        load.start()

    yield

    @pl.when(around.keeps)
    def _():
        load.wait()
        over.wait_recv()
        add_into(got, of(got), of(mine), count=rows, step=96)
        twin.start()

    yield

    @pl.when(around.keeps)
    def _():
        twin.wait_recv()
        add_into(half, of(half), lambda rows: got[rows, kept], count=rows, step=96)
        ring.begin()

    yield

    @pl.when(around.keeps)
    def _():
        ring.merge()

    yield

    @pl.when(around.keeps)
    def _():
        ring.sum()
        spread.begin()

    yield

    @pl.when(around.keeps)
    def _():
        spread.pass_on()

    yield

    @pl.when(around.keeps)
    def _():
        spread.end()
        both.start()

    yield

    @pl.when(around.keeps)
    def _():
        both.wait_recv()
        core.start()

    yield

    @pl.when(around.keeps)
    def _():
        twin.wait_send()
        ring.sent()
        spread.sent()
        both.wait_send()
        core.wait_send()

    @pl.when(around.gives)
    def _():
        over.wait_send()
        core.wait_recv()

    yield


def attn_sum(part, full, unit, links, locals_, around, scratch):
    own_terms, up_terms, down_terms, from_beyond, from_twin = scratch[:5]
    sizes, first = unit
    ring = RowRing(*sizes)
    y = around.y
    quarter = lambda k: ring.quarter(part, turned(y, k), first)
    loads = [
        locals_.of(quarter(k), held) for k, held in ((1, up_terms), (3, down_terms), (0, own_terms))
    ]
    ring.bind(links, around, scratch[5:], quarter(2), up_terms, down_terms, own_terms)
    total = ring.total
    over = links.to(total, from_beyond, around.beyond)
    twin = links.to(total, from_twin, around.twin)
    spread = RowSpread(ring, links, locals_, around, own_terms, full, first)
    span = full.at[pl.ds(first, SIDE * ring.size)]
    core = links.to(span, span, around.partner)

    for copy in loads:
        copy.start()
    ring.begin()
    yield
    for copy in loads:
        copy.wait()
    ring.merge()
    yield
    ring.sum()

    @pl.when(around.gives)
    def _():
        over.start()

    yield

    @pl.when(around.keeps)
    def _():
        over.wait_recv()
        add_into(total, of(total), of(from_beyond), count=ring.size, step=ring.step)
        twin.start()

    yield

    @pl.when(around.keeps)
    def _():
        twin.wait_recv()
        add_into(own_terms, of(total), of(from_twin), count=ring.size, step=ring.step)
        spread.begin()

    yield

    @pl.when(around.keeps)
    def _():
        spread.pass_on()

    yield

    @pl.when(around.keeps)
    def _():
        spread.end()
        core.start()

    yield
    ring.sent()

    @pl.when(around.keeps)
    def _():
        twin.wait_send()
        spread.sent()
        core.wait_send()

    @pl.when(around.gives)
    def _():
        over.wait_send()
        core.wait_recv()

    yield


def sum_everywhere(values, places, links, place):
    x, y, z_hi, z_lo, core = place
    by_x, by_core, by_y, by_z = places
    z = z_hi * 2 + z_lo
    rounds = (
        (by_x, x, [device(turned(x, k), y, z_hi, z_lo, core) for k in (1, 2, 3)]),
        (by_core, core, [device(x, y, z_hi, z_lo, 1 - core)]),
        (by_y, y, [device(x, turned(y, k), z_hi, z_lo, core) for k in (1, 2, 3)]),
        (by_z, z, [z_device(x, y, turned(z, k), core) for k in (1, 2, 3)]),
    )
    for slots, mine, peers in rounds:
        slots[mine] = values[...]
        copies = [links.to(slots.at[mine], slots.at[mine], peer) for peer in peers]
        for copy in copies:
            copy.start()
        for copy in copies:
            copy.wait()
        total = slots[0]
        for slot in range(1, slots.shape[0]):
            total = total + slots[slot]
        values[...] = total


def z_device(x, y, z, core):
    return device(x, y, lax.div(z, 2), lax.rem(z, 2), core)


def last_kernel(
    part,
    tokens,
    d_mid,
    gain,
    ffn_part,
    mid,
    ff_part,
    qkv_part,
    out_part,
    norm_part,
    mixed,
    input_grad,
    ff_full,
    qkv_full,
    out_full,
    sums,
    d_in,
    mixed_rows,
    own_rows,
    ffn_rows,
    own_sems,
    sends,
    arrives,
    local_sems,
    by_x,
    by_core,
    by_y,
    by_z,
    *scratch,
):
    place = here()
    x, y, z_hi, z_lo, core = place
    z = z_hi * 2 + z_lo
    around = Around(place)
    links, locals_ = Links(sends, arrives), Locals(local_sems)
    swap_with = device(x, y, core, z_lo, z_hi)
    terms, ffn_terms = ByRow(part, place), ByStep(ffn_part)
    scatter = Scatter(
        lambda step, rows: own_rows[step, rows, :], lambda step: terms.at(step, 1), place, scratch[:7]
    )
    scatter_ffn = Scatter(
        lambda step, rows: ffn_rows[step, rows, :], lambda step: ffn_terms.at(step, 1), place, scratch[7:14]
    )
    scratch = scratch[14:]
    ff_units, attn_units = [], []
    ff_own, scratch = scratch[:2], scratch[2:]
    for index in range(2048 // WIDE):
        mine = ff_own[index % 2]
        ff_units.append(ff_sum(ff_part, ff_full, index * WIDE, links, locals_, around, mine, scratch[:7]))
        scratch = scratch[7:]
    for index, unit in enumerate(ATTN_UNITS):
        refs = (out_part, out_full) if index == 2 else (qkv_part, qkv_full)
        attn_units.append(attn_sum(*refs, unit, links, locals_, around, scratch[:10]))
        scratch = scratch[10:]
    load_own = [locals_.of(terms.at(step, 0), own_rows.at[step]) for step in range(SIDE)]
    load_ffn = [locals_.of(ffn_terms.at(step, 0), ffn_rows.at[step]) for step in range(SIDE)]
    swaps = [links.to(mixed_rows, mixed, swap_with), links.to(d_in, input_grad, swap_with)]
    stays = [locals_.of(mixed_rows, mixed), locals_.of(d_in, input_grad)]

    def ff(*indices):
        for index in indices:
            next(ff_units[index])

    def attn(*indices):
        for index in indices:
            next(attn_units[index])

    def give(index):
        @pl.when(around.gives)
        def _():
            swaps[index].start()

        @pl.when(around.keeps)
        def _():
            stays[index].start()

    for copy in load_own + load_ffn:
        copy.start()
    peers = line_peers(place) + [device(x, turned(y, k), z_hi, z_lo, core) for k in (1, 2, 3)]
    peers += [z_device(x, y, turned(z, k), core) for k in (1, 2, 3)]

    @pl.when(around.gives)
    def _():
        greet(peers + [swap_with])

    @pl.when(around.keeps)
    def _():
        greet(peers)

    for step in (2, 1, 3, 0):
        scatter.across[step].start()
    ff(0, 1)
    attn(0, 1, 2)
    for copy in load_own + load_ffn:
        copy.wait()
    for step in (2, 1, 3):
        scatter.merge(step)
    for step in (2, 1, 3, 0):
        scatter_ffn.across[step].start()
    attn(0, 1, 2)
    for step in (2, 1, 3):
        scatter_ffn.merge(step)
    ff(0, 2)
    attn(0, 1, 2)
    scatter.finish()
    sums[...] = norm_part[...]

    def back(rows):
        grad = scatter.rows(rows)
        centre, scale = moments(tokens[rows, :].astype(jnp.float32))
        unit = centre * scale
        sums[0:1, :] += jnp.sum(grad * unit, axis=0, keepdims=True)
        sums[1:2, :] += jnp.sum(grad, axis=0, keepdims=True)
        scaled = grad * gain[...]
        d_in[rows, :] = d_mid[rows, :] + scale * (
            scaled
            - jnp.mean(scaled, axis=-1, keepdims=True)
            - unit * jnp.mean(scaled * unit, axis=-1, keepdims=True)
        )

    tile_rows(back)
    give(1)
    ff(0)
    attn(0, 1, 2)
    ff(0, 1, 3)
    attn(0, 1, 2)
    scatter_ffn.finish()

    def mix(rows):
        mixed_rows[rows, :] = (mid[rows, :] + scatter_ffn.rows(rows)).astype(jnp.bfloat16)

    tile_rows(mix)
    give(0)
    ff(0, 1, 0)
    attn(0, 1, 2)
    sum_everywhere(sums, (by_x, by_core, by_y, by_z), links, place)
    ff(1, 2, 0, 1, 2)
    attn(0, 1, 2)
    ff(0, 1, 2, 3, 1, 2, 3, 2, 1, 3, 2, 3, 2, 3, 3, 3)
    attn(0, 1, 2)
    ff(0, 1, 2, 3)

    @pl.when(around.gives)
    def _():
        for copy in swaps:
            copy.wait()

    @pl.when(around.keeps)
    def _():
        for copy in stays:
            copy.wait()


ANY = pl.BlockSpec(memory_space=pl.ANY)
HELD = pl.BlockSpec(memory_space=pltpu.VMEM)


def call(kernel, collective_id, args, in_specs, outs, out_specs, scratch):
    return pl.pallas_call(
        kernel,
        out_shape=[jax.ShapeDtypeStruct(shape, kind) for shape, kind in outs],
        in_specs=in_specs,
        out_specs=out_specs,
        scratch_shapes=list(scratch),
        compiler_params=pltpu.CompilerParams(
            collective_id=collective_id, has_side_effects=True, vmem_limit_bytes=VMEM_LIMIT
        ),
    )(*args)


def member_layout(seq_length, seq_owner, member, row_total):
    entry_total = seq_length.shape[0]
    row_ids = jnp.arange(row_total, dtype=jnp.int32)
    entry_ids = jnp.arange(entry_total, dtype=jnp.int32)
    earlier = (entry_ids[:, None] < entry_ids[None, :]).astype(jnp.int32)
    sharing = (seq_owner[:, None] == seq_owner[None, :]).astype(jnp.int32)
    starts = jnp.sum(seq_length[:, None] * sharing * earlier, axis=0)
    owned_now = (seq_owner == member).astype(jnp.int32)
    inside = (
        owned_now[None, :]
        * (row_ids[:, None] >= starts[None, :]).astype(jnp.int32)
        * (row_ids[:, None] < (starts + seq_length)[None, :]).astype(jnp.int32)
    )
    live_rows = jnp.sum(inside, axis=1)
    segment = jnp.sum(inside * entry_ids[None, :], axis=1) + (1 - live_rows) * (
        entry_total + row_ids
    )
    position = jnp.sum(inside * (row_ids[:, None] - starts[None, :]), axis=1)
    return (segment, position, live_rows)


def rotary_tables(position):
    half_rot = ROT // 2
    frequency = jnp.power(
        jnp.float32(10000.0), -2.0 * jnp.arange(half_rot, dtype=jnp.float32) / ROT
    )
    angles = position.astype(jnp.float32)[:, None] * frequency[None, :]
    return (jnp.cos(angles)[:, None, :], jnp.sin(angles)[:, None, :])


def rotate(values, cosine, sine_table):
    half_rot = ROT // 2
    first_half = values[..., :half_rot]
    second_half = values[..., half_rot:ROT]
    return jnp.concatenate(
        [
            first_half * cosine - second_half * sine_table,
            second_half * cosine + first_half * sine_table,
            values[..., ROT:],
        ],
        axis=-1,
    )


def contract_rows(left_rows, right_rows):
    return lax.dot_general(
        left_rows, right_rows, (((0,), (0,)), ((), ())), preferred_element_type=jnp.float32
    )


def times_transposed(left_rows, right_rows):
    return lax.dot_general(
        left_rows, right_rows, (((1,), (1,)), ((), ())), preferred_element_type=jnp.float32
    )


def block_mask(segment, row_ids, begin_row, end_row):
    return (segment[begin_row:end_row, None] == segment[None, :end_row]) & (
        row_ids[None, :end_row] <= row_ids[begin_row:end_row, None]
    )


def body(
    tokens,
    seq_length,
    seq_owner,
    ln1_gain,
    ln1_bias,
    qkv_weight,
    qkv_bias,
    out_weight,
    ln2_gain,
    ln2_bias,
    gate_up_weight,
    down_weight,
    out_grad,
):
    bf16, f32 = jnp.bfloat16, jnp.float32
    x, y, z_hi, z_lo, core = here()
    row_total = BLOCK * 8
    rows_here, rows_all = (BLOCK, 2048), (row_total, 2048)
    local_heads = qkv_weight.shape[2] // HEAD_DIM
    member = (y * 2 + z_lo) * 2 + z_hi
    shard = core * SIDE + x
    score_scale = HEAD_DIM ** (-0.5)
    segment, position, live_rows = member_layout(seq_length, seq_owner, member, row_total)
    row_ids = jnp.arange(row_total, dtype=jnp.int32)
    live = lax.dynamic_slice_in_dim(live_rows, shard * BLOCK, BLOCK, 0)[:, None].astype(f32)
    bias = permute(qkv_bias, swap_rows)

    dma = pltpu.SemaphoreType.DMA
    tokens_here, cot, normed1, cot_rows, qkv, out, down = call(
        first_kernel,
        1,
        (tokens, out_grad, live, ln1_gain[None], ln1_bias[None], qkv_weight, out_weight, down_weight),
        [ANY, ANY, HELD, HELD, HELD, ANY, ANY, ANY],
        [
            (rows_here, bf16),
            (rows_here, bf16),
            (rows_all, bf16),
            (rows_all, bf16),
            (qkv_weight.shape, bf16),
            (out_weight.shape, bf16),
            (down_weight.shape, bf16),
        ],
        [ANY] * 4 + [HELD] * 3,
        (pltpu.VMEM(rows_here, bf16),) * 4
        + (dma((2,)), dma((2,)), dma((6,)))
        + Gather.scratch * 2
        + fetch_scratch(3),
    )

    cosine, sine_table = rotary_tables(position)
    projected = [
        jnp.dot(normed1, qkv[channel], preferred_element_type=jnp.float32) + bias[channel]
        for channel in range(3)
    ]
    queries = rotate(
        projected[0].reshape(row_total, local_heads, HEAD_DIM), cosine, sine_table
    ).astype(bf16)
    keys_low = rotate(
        projected[1].reshape(row_total, local_heads, HEAD_DIM), cosine, sine_table
    ).astype(bf16)
    values_low = projected[2].reshape(row_total, local_heads, HEAD_DIM).astype(bf16)
    block_size = min(512, row_total)
    block_count = row_total // block_size
    out_blocks = []
    log_norms = []
    for block_index in range(block_count):
        begin_row = block_index * block_size
        end_row = begin_row + block_size
        allowed = block_mask(segment, row_ids, begin_row, end_row)
        scores = (
            jnp.einsum(
                "qhd,khd->hqk",
                queries[begin_row:end_row],
                keys_low[:end_row],
                preferred_element_type=jnp.float32,
            )
            * score_scale
        )
        scores = jnp.where(allowed[None], scores, -1e30)
        row_max = jnp.max(scores, axis=-1, keepdims=True)
        exp_scores = jnp.exp(scores - row_max)
        exp_sum = jnp.sum(exp_scores, axis=-1, keepdims=True)
        attn_prob = (exp_scores / exp_sum).astype(bf16)
        out_blocks.append(
            jnp.einsum(
                "hqk,khd->qhd", attn_prob, values_low[:end_row], preferred_element_type=jnp.float32
            ).astype(bf16)
        )
        log_norms.append(row_max + jnp.log(exp_sum))
    attended = jnp.concatenate(out_blocks, axis=0).reshape(row_total, local_heads * HEAD_DIM)
    attn_part = jnp.dot(attended, out, preferred_element_type=jnp.float32).astype(bf16)

    gate_up_t = jnp.swapaxes(gate_up_weight, 1, 2)
    ff = down_weight.shape[0]
    vmem = pltpu.VMEM
    mid_stream, d_mid, gain2_part, shift2_part, ffn_grad, ffn_part, d_attended, out_grad = call(
        middle_kernel,
        2,
        (
            attn_part,
            tokens_here,
            ln2_gain[None],
            ln2_bias[None],
            gate_up_t,
            down,
            cot_rows,
            attended,
            out,
            cot,
        ),
        [ANY, HELD, HELD, HELD, ANY, ANY, ANY, ANY, ANY, HELD],
        [
            (rows_here, f32),
            (rows_here, f32),
            ((1, 2048), f32),
            ((1, 2048), f32),
            ((3, ff, 2048), bf16),
            (rows_all, bf16),
            (attended.shape, bf16),
            (out.shape, bf16),
        ],
        [HELD, HELD, HELD, HELD, ANY, ANY, HELD, HELD],
        (
            vmem((2, ff, 2048), bf16),
            vmem((ff, 2048), bf16),
            vmem(out.shape, bf16),
            vmem(rows_all, bf16),
            vmem(rows_all, bf16),
            vmem(rows_all, bf16),
            vmem(attended.shape, bf16),
            vmem((row_total, ff), bf16),
            vmem((row_total, ff), bf16),
            vmem((row_total, ff), bf16),
            vmem((row_total, ff), f32),
            vmem((SIDE, BLOCK, 2048), bf16),
            vmem((SIDE, BLOCK, 2048), bf16),
            vmem((PAIR, 2048), bf16),
            vmem((2, ff, 512), bf16),
            dma((8,)),
            dma((8,)),
            dma((6,)),
            dma,
            dma((2,)),
        )
        + Scatter.scratch
        + Scatter.sems
        + Gather.scratch * 2
        + fetch_scratch(2),
    )

    d_attended = d_attended.reshape(row_total, local_heads, HEAD_DIM)
    query_grads = []
    d_key = jnp.zeros((row_total, local_heads, HEAD_DIM), f32)
    d_value = jnp.zeros((row_total, local_heads, HEAD_DIM), f32)
    for block_index in range(block_count):
        begin_row = block_index * block_size
        end_row = begin_row + block_size
        allowed = block_mask(segment, row_ids, begin_row, end_row)
        query_block = queries[begin_row:end_row]
        key_block = keys_low[:end_row]
        grad_block = d_attended[begin_row:end_row]
        scores = (
            jnp.einsum("qhd,khd->hqk", query_block, key_block, preferred_element_type=jnp.float32)
            * score_scale
        )
        scores = jnp.where(allowed[None], scores, -1e30)
        attn_full = jnp.exp(scores - log_norms[block_index])
        attn_prob = attn_full.astype(bf16)
        d_prob = jnp.einsum(
            "qhd,khd->hqk", grad_block, values_low[:end_row], preferred_element_type=jnp.float32
        )
        row_dots = jnp.sum(attn_full * d_prob, axis=-1, keepdims=True)
        d_score = (attn_full * (d_prob - row_dots)).astype(bf16)
        query_grads.append(
            jnp.einsum("hqk,khd->qhd", d_score, key_block, preferred_element_type=jnp.float32)
            * score_scale
        )
        d_key = d_key.at[:end_row].add(
            jnp.einsum("hqk,qhd->khd", d_score, query_block, preferred_element_type=jnp.float32)
            * score_scale
        )
        d_value = d_value.at[:end_row].add(
            jnp.einsum("hqk,qhd->khd", attn_prob, grad_block, preferred_element_type=jnp.float32)
        )
    d_query = jnp.concatenate(query_grads, axis=0)
    d_proj = [
        rotate(d_query, cosine, -sine_table).reshape(row_total, -1).astype(bf16),
        rotate(d_key, cosine, -sine_table).reshape(row_total, -1).astype(bf16),
        d_value.reshape(row_total, -1).astype(bf16),
    ]
    summed = times_transposed(d_proj[0], qkv[0])
    summed = summed + times_transposed(d_proj[1], qkv[1])
    d_norm_part = (summed + times_transposed(d_proj[2], qkv[2])).astype(bf16)

    qkv_part = jnp.concatenate(
        [contract_rows(normed1, d_proj[channel]).astype(bf16) for channel in range(3)]
    )
    bias_part = jnp.stack([jnp.sum(d.astype(f32), axis=0) for d in d_proj])
    bias_part = lax.dynamic_update_slice_in_dim(
        jnp.zeros((3, 2048), f32), bias_part, shard * bias_part.shape[1], 1
    )
    norm_part = jnp.concatenate(
        [jnp.zeros((2, 2048), f32), gain2_part, shift2_part, bias_part, jnp.zeros((1, 2048), f32)]
    )
    ff_part = ffn_grad.reshape(3 * ff, 2048)
    unit_count = 2048 // WIDE
    small = (8, 2048)
    mixed, input_grad, ff_full, qkv_full, out_full, sums = call(
        last_kernel,
        4,
        (
            d_norm_part,
            tokens_here,
            d_mid,
            ln1_gain[None],
            ffn_part,
            mid_stream,
            ff_part,
            qkv_part,
            out_grad,
            norm_part,
        ),
        [ANY, HELD, HELD, HELD, ANY, HELD, ANY, ANY, ANY, HELD],
        [
            (rows_here, bf16),
            (rows_here, f32),
            (ff_part.shape, bf16),
            (qkv_part.shape, bf16),
            (out.shape, bf16),
            (small, f32),
        ],
        [ANY, ANY, ANY, ANY, ANY, HELD],
        (
            vmem(rows_here, f32),
            vmem(rows_here, bf16),
            vmem((SIDE, BLOCK, 2048), bf16),
            vmem((SIDE, BLOCK, 2048), bf16),
            dma((8,)),
            dma((FF_LINKS * unit_count + ATTN_LINKS * 3 + 12,)),
            dma((FF_LINKS * unit_count + ATTN_LINKS * 3 + 12,)),
            dma((2 * unit_count + 4 * 3 + 10,)),
            vmem((SIDE, *small), f32),
            vmem((2, *small), f32),
            vmem((SIDE, *small), f32),
            vmem((SIDE, *small), f32),
        )
        + Scatter.scratch * 2
        + (vmem((3 * ff, WIDE), bf16),) * 2
        + ff_scratch(3 * ff) * unit_count
        + sum((attn_scratch(unit) for unit in ATTN_UNITS), ()),
    )
    ff_grads = ff_full.reshape(3, ff, 2048)
    gate_up_grad = jnp.swapaxes(ff_grads[:2], 1, 2).astype(f32)
    down_grad = ff_grads[2].astype(f32)
    qkv_weight_grad = qkv_full.reshape(3, 2048, -1).astype(f32)
    out_weight_grad = out_full.astype(f32)
    width = qkv_bias.shape[1]
    qkv_bias_grad = lax.dynamic_slice_in_dim(sums[4:7], (z_hi * SIDE + x) * width, width, 1)
    return (
        mixed,
        input_grad,
        sums[0],
        sums[1],
        qkv_weight_grad,
        qkv_bias_grad,
        out_weight_grad,
        sums[2],
        sums[3],
        gate_up_grad,
        down_grad,
    )


def solution(mesh):
    placed = (
        P(("dp", "tensor"), None),
        P(),
        P(),
        P(),
        P(),
        P(None, None, "tensor"),
        P(None, "tensor"),
        P("tensor", None),
        P(),
        P(),
        P(None, None, "tensor"),
        P("tensor", None),
        P(("dp", "tensor"), None),
    )
    return jax.shard_map(
        body,
        mesh=mesh,
        in_specs=placed,
        out_specs=(
            P(("dp", "tensor"), None),
            P(("dp", "tensor"), None),
            P(),
            P(),
            P(None, None, "tensor"),
            P(None, "tensor"),
            P("tensor", None),
            P(),
            P(),
            P(None, None, "tensor"),
            P("tensor", None),
        ),
        check_vma=False,
    )
```

```python
import functools

import jax
import jax.numpy as jnp
from jax import lax
from jax.experimental import pallas as pl
from jax.experimental.pallas import tpu as pltpu
from jax.sharding import PartitionSpec as P

HEAD_DIM = 64
ROT = 16
SIDE = 4
BLOCK = 128
AXES = ("dp", "tensor")
MESH = pl.DeviceIdType.MESH
VMEM_LIMIT = 54 * 2**20


def here():
    dp, tensor = lax.axis_index("dp"), lax.axis_index("tensor")
    x, z_hi = lax.rem(tensor, SIDE), lax.div(tensor, SIDE)
    y, z_lo, core = lax.div(dp, SIDE), lax.rem(lax.div(dp, 2), 2), lax.rem(dp, 2)
    return x, y, z_hi, z_lo, core


def device(x, y, z_hi, z_lo, core):
    return ((y * 2 + z_lo) * 2 + core, z_hi * SIDE + x)


def turned(value, by):
    return lax.rem(value + by, SIDE)


def pairs(move):
    found = []
    for dp in range(16):
        for tensor in range(8):
            goal = move(tensor % 4, dp // 4, tensor // 4, (dp // 2) % 2, dp % 2)
            if goal is not None:
                to_dp, to_tensor = device(*goal)
                found.append((dp * 8 + tensor, to_dp * 8 + to_tensor))
    return found


def permute(array, move):
    return lax.ppermute(array, AXES, pairs(move))


def swap_rows(x, y, z_hi, z_lo, core):
    return (x, y, core, z_lo, z_hi)


def remote(source, target, sends, arrives, index, device_id):
    return pltpu.make_async_remote_copy(
        src_ref=source,
        dst_ref=target,
        send_sem=sends.at[index],
        recv_sem=arrives.at[index],
        device_id=device_id,
        device_id_type=MESH,
    )


def greet(peers):
    barrier = pltpu.get_barrier_semaphore()
    for peer in peers:
        pl.semaphore_signal(barrier, inc=1, device_id=peer, device_id_type=MESH)
    pl.semaphore_wait(barrier, len(peers))


def line_peers(place):
    x, y, z_hi, z_lo, core = place
    found = [device(turned(x, k), y, z_hi, z_lo, core) for k in (1, 2, 3)]
    return found + [device(x, y, z_hi, z_lo, 1 - core)]


def row_block(full, core, x):
    return full.at[pl.ds(pl.multiple_of((core * SIDE + x) * BLOCK, BLOCK), BLOCK)]


class ByRow:
    def __init__(self, full, place):
        self.full, self.x, self.core = full, place[0], place[4]

    def at(self, step, other):
        core = 1 - self.core if other else self.core
        return row_block(self.full, core, turned(self.x, SIDE - step))

    def landing(self, step, other, by, across):
        return self.at(step, other)


class ByStep:
    def __init__(self, full):
        self.full = full

    def at(self, step, other):
        return self.full.at[pl.ds((step * 2 + other) * BLOCK, BLOCK)]

    def landing(self, step, other, by, across):
        return self.at((step + by) % SIDE, 1 - other if across else other)


class Gather:
    scratch = (
        pltpu.SemaphoreType.DMA((4,)),
        pltpu.SemaphoreType.DMA((4,)),
        pltpu.SemaphoreType.DMA((4,)),
        pltpu.SemaphoreType.DMA((4,)),
    )

    def __init__(self, block, layout, place, sems):
        x, y, z_hi, z_lo, core = place
        x_send, x_arrive, core_send, core_arrive = sems
        half = BLOCK // 2
        right = device(turned(x, 1), y, z_hi, z_lo, core)
        left = device(turned(x, 3), y, z_hi, z_lo, core)
        partner = device(x, y, z_hi, z_lo, 1 - core)

        def passed(step, first, by, index, to):
            part = pl.ds(first, half)
            return remote(
                layout.at(step, 0).at[part],
                layout.landing(step, 0, by, False).at[part],
                x_send,
                x_arrive,
                index,
                to,
            )

        self.right = remote(block, layout.landing(0, 0, 1, False), x_send, x_arrive, 0, right)
        self.left = remote(block, layout.landing(0, 0, 3, False), x_send, x_arrive, 1, left)
        self.right_on = passed(1, 0, 1, 2, right)
        self.left_on = passed(3, half, 3, 3, left)
        self.across = [
            remote(
                block if step == 0 else layout.at(step, 0),
                layout.landing(step, 0, 0, True),
                core_send,
                core_arrive,
                step,
                partner,
            )
            for step in range(SIDE)
        ]

    def start(self):
        self.right.start()
        self.left.start()
        self.across[0].start()

    def arrive(self, step):
        if step == 1:
            self.right.wait_recv()
            self.right_on.start()
        elif step == 3:
            self.left.wait_recv()
            self.left_on.start()
        else:
            self.right_on.wait_recv()
            self.left_on.wait_recv()
        self.across[step].start()

    def finish(self):
        for copy in (self.right, self.left, self.right_on, self.left_on, *self.across):
            copy.wait_send()

    def take(self):
        for copy in self.across:
            copy.wait_recv()


class Scatter:
    buffers = (
        pltpu.VMEM((SIDE, BLOCK, 2048), jnp.bfloat16),
        pltpu.VMEM((3, BLOCK, 2048), jnp.bfloat16),
        pltpu.VMEM((3, BLOCK, 2048), jnp.bfloat16),
    )
    sems = (
        pltpu.SemaphoreType.DMA((SIDE,)),
        pltpu.SemaphoreType.DMA((SIDE,)),
        pltpu.SemaphoreType.DMA((3,)),
        pltpu.SemaphoreType.DMA((3,)),
    )
    scratch = buffers + sems

    def __init__(self, own, given, place, scratch):
        x, y, z_hi, z_lo, core = place
        self.own, (self.other, self.leaving, self.arrived) = own, scratch[:3]
        core_send, core_arrive, x_send, x_arrive = scratch[3:]
        partner = device(x, y, z_hi, z_lo, 1 - core)
        self.across = [
            remote(given(step), self.other.at[step], core_send, core_arrive, step, partner)
            for step in range(SIDE)
        ]
        self.along = [
            remote(
                self.leaving.at[step - 1],
                self.arrived.at[step - 1],
                x_send,
                x_arrive,
                step - 1,
                device(turned(x, SIDE - step), y, z_hi, z_lo, core),
            )
            for step in (1, 2, 3)
        ]

    def merge(self, step):
        self.across[step].wait_recv()

        def add(rows):
            both = self.own(step, rows).astype(jnp.float32) + self.other[step, rows, :].astype(jnp.float32)
            self.leaving[step - 1, rows, :] = both.astype(jnp.bfloat16)

        tile_rows(add)
        self.along[step - 1].start()

    def finish(self):
        self.across[0].wait_recv()
        for copy in self.along:
            copy.wait()
        for copy in self.across:
            copy.wait_send()

    def rows(self, rows):
        total = self.own(0, rows).astype(jnp.float32) + self.other[0, rows, :].astype(jnp.float32)
        for step in range(3):
            total = total + self.arrived[step, rows, :].astype(jnp.float32)
        return total


class Loaded:
    def __init__(self, full, held, place, sems):
        there, here_ = ByRow(full, place), ByStep(held)
        self.copies = [
            pltpu.make_async_copy(there.at(step, other), here_.at(step, other), sems.at[step * 2 + other])
            for step in range(SIDE)
            for other in range(2)
        ]

    def start(self):
        for copy in self.copies:
            copy.start()

    def wait(self):
        for copy in self.copies:
            copy.wait()


class Fetch:
    def __init__(self, weight, filled, cut, place, sems, index):
        x, y, z_hi, z_lo, core = place
        send, arrive, own_sem = sems
        self.own = pltpu.make_async_copy(weight, filled, own_sem.at[index])
        across = device(x, y, 1 - z_hi, 1 - z_lo, z_hi)
        up = device(x, turned(y, 1), z_hi, z_lo, core)
        down = device(x, turned(y, 3), z_hi, z_lo, core)
        base = index * 5

        def moved(ref, quarter, half, slot, to):
            source = cut(ref, quarter, half)
            return remote(source, cut(filled, quarter, half), send, arrive, base + slot, to)

        self.across = moved(weight, y, None, 0, across)
        self.up = moved(filled, y, None, 1, up)
        self.down = moved(filled, y, None, 2, down)
        self.up_on = moved(filled, turned(y, 3), 0, 3, up)
        self.down_on = moved(filled, turned(y, 1), 1, 4, down)

    def spread(self):
        self.across.wait_recv()
        self.up.start()
        self.down.start()

    def pass_on(self):
        self.up.wait_recv()
        self.up_on.start()
        self.down.wait_recv()
        self.down_on.start()

    def finish(self):
        self.up_on.wait_recv()
        self.down_on.wait_recv()
        for copy in (self.across, self.up, self.down, self.up_on, self.down_on):
            copy.wait_send()


def fetch_scratch(count):
    return (
        pltpu.SemaphoreType.DMA((5 * count,)),
        pltpu.SemaphoreType.DMA((5 * count,)),
        pltpu.SemaphoreType.DMA((count,)),
    )


def fetch_peers(place):
    x, y, z_hi, z_lo, core = place
    return [device(x, y, 1 - z_hi, 1 - z_lo, z_hi)] + [
        device(x, turned(y, k), z_hi, z_lo, core) for k in (1, 3)
    ]


def quarter_rows(size, *before):
    quarter_size = size // SIDE
    split = -(-quarter_size // 32) * 16

    def cut(weight, quarter, half):
        first = pl.multiple_of(quarter * quarter_size, 16)
        if half is None:
            rows = pl.ds(first, quarter_size)
        elif half == 0:
            rows = pl.ds(first, split)
        else:
            rows = pl.ds(first + split, quarter_size - split)
        return weight.at[(*before, rows)]

    return cut


QKV_CUT = quarter_rows(2048, slice(None))
OUT_CUT = quarter_rows(256)
FF_CUT = quarter_rows(704)


def moments(values):
    centre = values - jnp.mean(values, axis=-1, keepdims=True)
    return centre, lax.rsqrt(jnp.mean(centre * centre, axis=-1, keepdims=True) + 1e-05)


def tile_rows(body):
    @pl.loop(0, BLOCK, step=16)
    def _(row):
        body(pl.ds(pl.multiple_of(row, 16), 16))


def matmul(left, right, contract):
    return lax.dot_general(left, right, ((contract, ((), ()))), preferred_element_type=jnp.float32)


NN, NT, TN = ((1,), (0,)), ((1,), (1,)), ((0,), (0,))
PAIR = 2 * BLOCK
TILE = 256


class Locals:
    def __init__(self, sems):
        self.sems, self.used = sems, 0

    def of(self, source, target):
        self.used += 1
        return pltpu.make_async_copy(source, target, self.sems.at[self.used - 1])


def attention(queries, keys, values, row_info, segments, segment_row, attended, score_scale):
    bf16 = jnp.bfloat16
    lane = lax.broadcasted_iota(jnp.int32, (1, 128), 1)
    row_info[...] = jnp.where(lane == 4, segments[...], 0.0)
    for block in range(4):
        first, end = block * PAIR, (block + 1) * PAIR
        rows, before = pl.ds(first, PAIR), pl.ds(0, end)
        places = first + lax.broadcasted_iota(jnp.int32, (PAIR, end), 0)
        allowed = (segments[rows, :] == segment_row[:, 0:end]) & (
            lax.broadcasted_iota(jnp.int32, (PAIR, end), 1) <= places
        )

        @pl.loop(0, 2)
        def _(pair):
            lanes = pl.ds(pl.multiple_of(pair * 128, 128), 128)
            query, key, value = queries[rows, lanes], keys[before, lanes], values[before, lanes]
            mixed = jnp.zeros((PAIR, 128), jnp.float32)
            for head in range(2):
                inside = (lane >= head * HEAD_DIM) & (lane < (head + 1) * HEAD_DIM)
                query_h = jnp.where(inside, query, jnp.zeros_like(query))
                value_h = jnp.where(inside, value, jnp.zeros_like(value))
                scores = jnp.where(allowed, matmul(query_h, key, NT) * score_scale, -1e30)
                top = jnp.max(scores, axis=1, keepdims=True)
                raised = jnp.exp(scores - top)
                total = jnp.sum(raised, axis=1, keepdims=True)
                mixed = mixed + matmul((raised / total).astype(bf16), value_h, NN)
                row_info[rows, :] = jnp.where(
                    lane == pair * 2 + head, top + jnp.log(total), row_info[rows, :]
                )
            attended[rows, lanes] = mixed.astype(bf16)

        yield


def first_kernel(
    tokens,
    out_grad,
    live,
    gain,
    shift,
    qkv,
    out,
    down,
    bias,
    segments,
    segment_row,
    keep,
    from_after,
    from_before,
    tokens_here,
    cot_here,
    normed_full,
    cot_full,
    part,
    qkv_here,
    out_here,
    down_here,
    queries,
    keys,
    values,
    attended,
    row_info,
    tok_buf,
    grad_buf,
    cot_buf,
    bias_buf,
    normed,
    part_tile,
    swap_send,
    swap_arrive,
    own_sems,
    *sems,
):
    bf16 = jnp.bfloat16
    place = here()
    x, y, z_hi, z_lo, core = place
    lacking = core != z_hi
    swap_with = device(x, y, core, z_lo, z_hi)
    fetch_sems = sems[8:]
    fetches = [
        Fetch(weight, filled, cut, place, fetch_sems, index)
        for index, (weight, filled, cut) in enumerate(
            [(qkv, qkv_here, QKV_CUT), (out, out_here, OUT_CUT), (down, down_here, FF_CUT)]
        )
    ]
    moved = [(tokens, tok_buf), (out_grad, grad_buf), (bias, bias_buf)]
    swaps = [
        remote(source, target, swap_send, swap_arrive, index, swap_with)
        for index, (source, target) in enumerate(moved)
    ]
    locals_ = Locals(own_sems)
    stays = [locals_.of(source, target) for source, target in moved]
    gather = Gather(normed.at[pl.ds(0, BLOCK)], ByStep(normed), place, sems[:4])
    gather_cot = Gather(cot_buf, ByRow(cot_full, place), place, sems[4:8])
    by_step, by_row = ByStep(normed), ByRow(normed_full, place)
    normed_out = [
        locals_.of(by_step.at(step, other), by_row.at(step, other)) for step in range(SIDE) for other in range(2)
    ]
    stored = [
        locals_.of(tok_buf, tokens_here),
        locals_.of(cot_buf, cot_here),
        locals_.of(cot_buf, row_block(cot_full, core, x)),
    ]
    part_sem = own_sems.at[locals_.used]

    @pl.when(lacking)
    def _():
        greet(line_peers(place) + [swap_with] + fetch_peers(place))
        swaps[0].start()
        swaps[2].start()
        fetches[0].across.start()
        swaps[1].start()
        fetches[1].across.start()
        fetches[2].across.start()
        swaps[0].wait_recv()

    @pl.when(jnp.logical_not(lacking))
    def _():
        greet(line_peers(place))
        for copy in stays:
            copy.start()
        for fetch in fetches:
            fetch.own.start()
        stays[0].wait()

    def norm(rows):
        centre, scale = moments(tok_buf[rows, :].astype(jnp.float32))
        normed[rows, :] = (centre * scale * gain[...] + shift[...]).astype(bf16)

    tile_rows(norm)
    gather.start()
    stored[0].start()

    @pl.when(lacking)
    def _():
        fetches[0].spread()
        for copy in swaps:
            copy.wait_send()
        swaps[1].wait_recv()
        swaps[2].wait_recv()

    @pl.when(jnp.logical_not(lacking))
    def _():
        stays[1].wait()
        stays[2].wait()

    def mask(rows):
        cot_buf[rows, :] = (grad_buf[rows, :].astype(jnp.float32) * live[rows, :]).astype(bf16)

    tile_rows(mask)
    gather.arrive(1)
    gather.arrive(3)
    gather_cot.start()
    stored[1].start()
    stored[2].start()

    @pl.when(lacking)
    def _():
        fetches[0].pass_on()
        fetches[1].spread()
        fetches[2].spread()

    gather.arrive(2)
    gather.take()
    for copy in normed_out:
        copy.start()

    @pl.when(lacking)
    def _():
        fetches[0].finish()

    @pl.when(jnp.logical_not(lacking))
    def _():
        fetches[0].own.wait()

    gather_cot.arrive(1)
    gather_cot.arrive(3)

    @pl.loop(0, 8)
    def _(index):
        step, other = lax.div(index, 2), lax.rem(index, 2)
        whose = core + other * (1 - 2 * core)
        first = pl.multiple_of((whose * SIDE + turned(x, SIDE - step)) * BLOCK, BLOCK)
        rows = pl.ds(first, BLOCK)
        block = normed[pl.ds(pl.multiple_of(index * BLOCK, BLOCK), BLOCK), :]
        for channel, target in enumerate((queries, keys, values)):
            projected = matmul(block, qkv_here[channel], NN) + bias_buf[channel : channel + 1, :]
            for pair in range(2):
                lanes = projected[:, pair * 128 : (pair + 1) * 128]
                if channel < 2:
                    lanes = (
                        lanes * keep[rows, :]
                        - pltpu.roll(lanes, 120, 1) * from_after[rows, :]
                        - pltpu.roll(lanes, 8, 1) * from_before[rows, :]
                    )
                target[rows, pair * 128 : (pair + 1) * 128] = lanes.astype(bf16)

    @pl.when(lacking)
    def _():
        fetches[1].pass_on()
        fetches[2].pass_on()

    gather_cot.arrive(2)
    blocks = attention(
        queries, keys, values, row_info, segments, segment_row, attended, HEAD_DIM ** (-0.5)
    )
    for block in range(4):
        next(blocks)
        rows = pl.ds(block * PAIR, PAIR)
        if block == 0:

            @pl.when(lacking)
            def _():
                fetches[1].finish()

            @pl.when(jnp.logical_not(lacking))
            def _():
                fetches[1].own.wait()

        else:
            pltpu.make_async_copy(part_tile, part.at[rows], part_sem).wait()

        @pl.loop(0, 2048, step=512)
        def _(column):
            columns = pl.ds(pl.multiple_of(column, 512), 512)
            part_tile[:, columns] = matmul(attended[rows, :], out_here[:, columns], NN).astype(bf16)

        pltpu.make_async_copy(part_tile, part.at[rows], part_sem).start()

    gather_cot.take()
    for each in (gather, gather_cot):
        each.finish()
    for copy in normed_out + stored:
        copy.wait()
    pltpu.make_async_copy(part_tile, part.at[pl.ds(0, PAIR)], part_sem).wait()

    @pl.when(lacking)
    def _():
        fetches[2].finish()

    @pl.when(jnp.logical_not(lacking))
    def _():
        fetches[2].own.wait()


def middle_kernel(
    part,
    tokens,
    gain,
    shift,
    gate_up_own,
    down_held,
    cot_full,
    attended_full,
    out_held,
    cot,
    mid,
    d_mid,
    gain_part,
    shift_part,
    gate_grad,
    up_grad,
    down_grad,
    gate_beyond,
    down_sum,
    ffn_part,
    d_attended,
    out_grad,
    gate_up,
    down,
    out,
    normed,
    cot_rows,
    d_rows,
    attended,
    hidden,
    d_gate,
    d_up,
    d_hidden,
    own_rows,
    given_terms,
    ffn_tile,
    grad_tile,
    load_sems,
    att_sems,
    own_sems,
    ffn_sem,
    grad_sems,
    *scratch,
):
    bf16 = jnp.bfloat16
    place = here()
    x, y, z_hi, z_lo, core = place
    lacking = core != z_hi
    attn = ByRow(part, place)
    first = Scatter(
        lambda step, rows: own_rows[step, rows, :], lambda step: attn.at(step, 1), place, scratch[:7]
    )
    second = Scatter(
        lambda step, rows: own_rows[step, rows, :],
        lambda step: given_terms.at[step],
        place,
        scratch[:3] + scratch[7:11],
    )
    gather = Gather(normed.at[pl.ds(0, BLOCK)], ByStep(normed), place, scratch[11:15])
    gather_d = Gather(d_rows.at[pl.ds(0, BLOCK)], ByStep(d_rows), place, scratch[15:19])
    fetches = [
        Fetch(gate_up_own.at[index], gate_up.at[index], FF_CUT, place, scratch[19:22], index) for index in range(2)
    ]
    around = Around(place)
    links = Links(*scratch[22:24])
    over = links.to(gate_grad, gate_beyond, around.beyond)
    ring = RowRing(*DOWN_RING)
    ring_terms = scratch[24:27]
    ring_loads = [
        pltpu.make_async_copy(ring.quarter(down_grad, turned(y, k)), held, load_sems.at[index])
        for index, (k, held) in enumerate(zip((1, 3, 0), ring_terms))
    ]
    ring.bind(links, around, scratch[27:], ring.quarter(down_grad, turned(y, 2)), *ring_terms)
    load_cot = Loaded(cot_full, cot_rows, place, load_sems)
    load_att = Loaded(attended_full, attended, place, att_sems)
    load_own = [
        pltpu.make_async_copy(attn.at(step, 0), own_rows.at[step], own_sems.at[step]) for step in range(SIDE)
    ]
    load_down = pltpu.make_async_copy(down_held, down, own_sems.at[4])
    load_out = pltpu.make_async_copy(out_held, out, own_sems.at[5])

    for copy in load_own:
        copy.start()
    load_down.start()
    load_cot.start()
    load_att.start()
    load_out.start()

    @pl.when(lacking)
    def _():
        greet(line_peers(place) + fetch_peers(place) + [around.beyond])

    @pl.when(jnp.logical_not(lacking))
    def _():
        greet(line_peers(place) + [around.up, around.down, around.beyond])

    for step in (2, 1, 3, 0):
        first.across[step].start()

    @pl.when(lacking)
    def _():
        for fetch in fetches:
            fetch.across.start()

    @pl.when(jnp.logical_not(lacking))
    def _():
        for fetch in fetches:
            fetch.own.start()

    for copy in load_own:
        copy.wait()
    for step in (2, 1, 3):
        first.merge(step)
    load_down.wait()
    load_cot.wait()

    @pl.loop(0, 2)
    def _(index):
        rows = pl.ds(pl.multiple_of(index * PAIR, PAIR), PAIR)
        d_hidden[rows, :] = matmul(cot_rows[rows, :], down[...], NT)

    @pl.when(lacking)
    def _():
        for fetch in fetches:
            fetch.spread()

    @pl.loop(2, 4)
    def _(index):
        rows = pl.ds(pl.multiple_of(index * PAIR, PAIR), PAIR)
        d_hidden[rows, :] = matmul(cot_rows[rows, :], down[...], NT)

    first.finish()

    def norm(rows):
        stream = tokens[rows, :].astype(jnp.float32) + first.rows(rows)
        mid[rows, :] = stream
        centre, scale = moments(stream)
        normed[rows, :] = (centre * scale * gain[...] + shift[...]).astype(bf16)

    tile_rows(norm)
    gather.start()

    @pl.when(lacking)
    def _():
        for fetch in fetches:
            fetch.pass_on()
        for fetch in fetches:
            fetch.finish()

    @pl.when(jnp.logical_not(lacking))
    def _():
        for fetch in fetches:
            fetch.own.wait()

    order = (0, 1, 3, 2)

    @pl.loop(0, 4)
    def _(turn):
        step = turn + lax.div(turn, 2) * (5 - 2 * turn)
        for index in range(4):

            @pl.when(turn == index)
            def _(index=index):
                for arrived in ((), (1, 3), (), (2,))[index]:
                    gather.arrive(arrived)
                gather.across[order[index]].wait_recv()

        rows = pl.ds(pl.multiple_of(step * PAIR, PAIR), PAIR)
        gate = matmul(normed[rows, :], gate_up[0], NT)
        up = matmul(normed[rows, :], gate_up[1], NT)
        sigmoid = jax.nn.sigmoid(gate)
        silu = gate * sigmoid
        hidden[rows, :] = (silu * up).astype(bf16)
        d_hid = d_hidden[rows, :]
        d_gate[rows, :] = (d_hid * up * sigmoid * (1.0 + gate * (1.0 - sigmoid))).astype(bf16)
        d_up[rows, :] = (d_hid * silu).astype(bf16)
        for index in (2, 3):

            @pl.when(turn == index)
            def _(index=index):
                second.merge(order[index - 1])

        @pl.loop(0, 2048, step=512)
        def _(column):
            columns = pl.ds(pl.multiple_of(column, 512), 512)
            terms = matmul(d_gate[rows, :], gate_up[0, :, columns], NN) + matmul(
                d_up[rows, :], gate_up[1, :, columns], NN
            )
            terms = terms.astype(bf16)
            own_rows[step, :, columns] = terms[:BLOCK]
            given_terms[step, :, columns] = terms[BLOCK:]

        for index in range(4):

            @pl.when(turn == index)
            def _(index=index):
                second.across[order[index]].start()

    second.merge(2)
    load_att.wait()
    load_out.wait()

    def ffn_terms():
        @pl.loop(0, 4)
        def _(index):
            rows = pl.ds(pl.multiple_of(index * PAIR, PAIR), PAIR)

            @pl.when(index > 0)
            def _():
                pltpu.make_async_copy(ffn_tile, ffn_part.at[rows], ffn_sem).wait()

            @pl.loop(0, 2048, step=512)
            def _(column):
                columns = pl.ds(pl.multiple_of(column, 512), 512)
                ffn_tile[:, columns] = matmul(hidden[rows, :], down[:, columns], NN).astype(bf16)

            pltpu.make_async_copy(ffn_tile, ffn_part.at[rows], ffn_sem).start()

    def weight_grad(target, left, right):
        def stored(tile, slot):
            columns = pl.ds(pl.multiple_of(tile * TILE, TILE), TILE)
            return pltpu.make_async_copy(grad_tile.at[slot], target.at[:, columns], grad_sems.at[slot])

        @pl.loop(0, 8)
        def _(tile):
            slot = lax.rem(tile, 2)

            @pl.when(tile > 1)
            def _():
                stored(tile, slot).wait()

            columns = pl.ds(pl.multiple_of(tile * TILE, TILE), TILE)
            grad_tile[slot] = matmul(left[...], right[:, columns], TN).astype(bf16)
            stored(tile, slot).start()

        for slot in range(2):
            stored(slot, slot).wait()

    weight_grad(gate_grad, d_gate, normed)

    @pl.when(lacking)
    def _():
        over.start()

    weight_grad(down_grad, hidden, cot_rows)
    ring.begin()
    for copy in ring_loads:
        copy.start()
    second.finish()
    gain_part[...] = jnp.zeros_like(gain_part)
    shift_part[...] = jnp.zeros_like(shift_part)

    def back(rows):
        grad = second.rows(rows)
        centre, scale = moments(mid[rows, :])
        unit = centre * scale
        gain_part[...] += jnp.sum(grad * unit, axis=0, keepdims=True)
        shift_part[...] += jnp.sum(grad, axis=0, keepdims=True)
        scaled = grad * gain[...]
        total = cot[rows, :].astype(jnp.float32) + scale * (
            scaled
            - jnp.mean(scaled, axis=-1, keepdims=True)
            - unit * jnp.mean(scaled * unit, axis=-1, keepdims=True)
        )
        d_mid[rows, :] = total
        d_rows[rows, :] = total.astype(bf16)

    tile_rows(back)
    gather_d.start()
    for copy in ring_loads:
        copy.wait()
    ring.merge()
    ffn_terms()
    gather_d.arrive(1)
    gather_d.arrive(3)
    weight_grad(up_grad, d_up, normed)
    gather_d.arrive(2)
    for step in range(SIDE):
        gather_d.across[step].wait_recv()
        terms = matmul(d_rows[pl.ds(step * PAIR, PAIR), :], out[...], NT).astype(bf16)
        behind = turned(x, SIDE - step)
        for other in range(2):
            whose = (1 - core) if other else core
            first_row = pl.multiple_of((whose * SIDE + behind) * BLOCK, BLOCK)
            d_attended[pl.ds(first_row, BLOCK), :] = terms[other * BLOCK : (other + 1) * BLOCK]

    @pl.loop(0, 2048, step=512)
    def _(column):
        columns = pl.ds(pl.multiple_of(column, 512), 512)
        out_grad[:, columns] = matmul(attended[...], d_rows[:, columns], TN).astype(bf16)

    gather.finish()
    gather_d.finish()
    pltpu.make_async_copy(ffn_tile, ffn_part.at[pl.ds(0, PAIR)], ffn_sem).wait()
    ring.sum()
    down_stored = pltpu.make_async_copy(ring.total, down_sum, own_sems.at[0])
    down_stored.start()
    ring.sent()
    down_stored.wait()

    @pl.when(lacking)
    def _():
        over.wait_send()

    @pl.when(jnp.logical_not(lacking))
    def _():
        over.wait_recv()


class Links:
    def __init__(self, sends, arrives):
        self.sends, self.arrives, self.used = sends, arrives, 0

    def to(self, source, target, device_id):
        self.used += 1
        return remote(source, target, self.sends, self.arrives, self.used - 1, device_id)


def each_rows(count, step, body):
    if count == step:
        body(pl.ds(0, count))
        return

    @pl.loop(0, count, step=step)
    def _(row):
        body(pl.ds(pl.multiple_of(row, 16), step))


def add_into(target, *terms, count, step):
    def body(rows):
        total = terms[0](rows).astype(jnp.float32)
        for term in terms[1:]:
            total = total + term(rows).astype(jnp.float32)
        target[rows, :] = total.astype(jnp.bfloat16)

    each_rows(count, step, body)


def of(ref, first=0):
    return lambda rows: ref[pl.ds(rows.start + first, rows.size), :]


class Around:
    def __init__(self, place):
        x, y, z_hi, z_lo, core = place
        self.y, self.z_lo = y, z_lo
        self.up = device(x, turned(y, 1), z_hi, z_lo, core)
        self.down = device(x, turned(y, 3), z_hi, z_lo, core)
        self.beyond = device(x, y, 1 - z_hi, 1 - z_lo, core)
        self.twin = device(x, y, z_hi, 1 - z_lo, core)
        self.partner = device(x, y, z_hi, z_lo, 1 - core)
        self.keeps = core == z_hi
        self.gives = jnp.logical_not(self.keeps)


class RowRing:
    def __init__(self, size, width, step):
        self.size, self.width, self.step = size, width, step
        self.split = -(-size // 32) * 16

    def scratch(self):
        kind = jnp.bfloat16
        return (
            pltpu.VMEM((self.split, self.width), kind),
            pltpu.VMEM((self.size - self.split, self.width), kind),
            pltpu.VMEM((self.size, self.width), kind),
            pltpu.VMEM((self.size, self.width), kind),
            pltpu.VMEM((self.size, self.width), kind),
        )

    def quarter(self, ref, index, first=0):
        return ref.at[pl.ds(pl.multiple_of(first + index * self.size, 16), self.size)]

    def halves(self, ref):
        return ref.at[pl.ds(0, self.split)], ref.at[pl.ds(self.split, self.size - self.split)]

    def bind(self, links, around, scratch, far, up_terms, down_terms, own_terms):
        self.from_below, self.from_above, self.got_up, self.got_down, self.total = scratch
        self.up_terms, self.down_terms, self.own_terms = up_terms, down_terms, own_terms
        first, second = self.halves(far)
        self.first = (
            links.to(first, self.from_below, around.up),
            links.to(second, self.from_above, around.down),
        )
        self.second = (
            links.to(up_terms, self.got_up, around.up),
            links.to(down_terms, self.got_down, around.down),
        )

    def begin(self):
        for copy in self.first:
            copy.start()

    def merge(self):
        self.first[0].wait_recv()
        low, high = self.split, self.size - self.split
        up_low, _ = self.halves(self.up_terms)
        _, down_high = self.halves(self.down_terms)
        add_into(up_low, of(up_low), of(self.from_below), count=low, step=low)
        self.second[0].start()
        self.first[1].wait_recv()
        add_into(down_high, of(down_high), of(self.from_above), count=high, step=high)
        self.second[1].start()

    def sum(self):
        for copy in self.second:
            copy.wait_recv()
        add_into(
            self.total,
            of(self.own_terms),
            of(self.got_up),
            of(self.got_down),
            count=self.size,
            step=self.step,
        )

    def sent(self):
        for copy in (*self.first, *self.second):
            copy.wait_send()


class RowSpread:
    def __init__(self, ring, links, locals_, around, total, full, first=0):
        y = around.y
        mine = ring.quarter(full, y, first)
        below, above = ring.quarter(full, turned(y, 3), first), ring.quarter(full, turned(y, 1), first)
        self.own = locals_.of(total, mine)
        self.direct = (links.to(total, mine, around.up), links.to(total, mine, around.down))
        low, high = ring.halves(below)[0], ring.halves(above)[1]
        self.passed = (links.to(low, low, around.up), links.to(high, high, around.down))

    def begin(self):
        self.own.start()
        for copy in self.direct:
            copy.start()

    def pass_on(self):
        for copy, onward in zip(self.direct, self.passed):
            copy.wait_recv()
            onward.start()

    def end(self):
        self.own.wait()
        for copy in self.passed:
            copy.wait_recv()

    def sent(self):
        for copy in (*self.direct, *self.passed):
            copy.wait_send()


WIDE = 1024
DOWN_RING = (176, 2048, 16)
ATTN_UNITS = ((768, 256, 96, 0), (768, 256, 96, 3072), (64, 2048, 16, 0))
LINK_COUNT, LOCAL_COUNT = 112, 64


def left_ring():
    return RowRing(176, WIDE // 2, 176)


def right_ring():
    return RowRing(176, WIDE, 16)


def left_scratch(rows, count):
    kind = jnp.bfloat16
    half = pltpu.VMEM((rows, WIDE // 2), kind)
    return (pltpu.VMEM((rows, WIDE), kind),) * 3 + ((half,) + left_ring().scratch()) * count


def right_scratch(count):
    return (pltpu.VMEM((176, WIDE), jnp.bfloat16),) * (4 * count)


def attn_scratch():
    found = ()
    for size, width, step, _ in ATTN_UNITS:
        ring = RowRing(size, width, step)
        found += (pltpu.VMEM((size, width), jnp.bfloat16),) * 2 + ring.scratch()
    return found


def left_sum(part, beyond, full, column, fetch, links, locals_, around, mine, got, scratch):
    half = scratch[0]
    rows, width = got.shape[0], WIDE // 2
    ring = left_ring()
    side = lambda z_lo: pl.ds(pl.multiple_of(z_lo * width, 128), width)
    columns = pl.ds(column, WIDE)
    stretch = full.at[:, columns]
    own_side = full.at[:, pl.ds(pl.multiple_of(column + around.z_lo * width, 128), width)]
    loads = (locals_.of(part.at[:, columns], mine), locals_.of(beyond.at[:, columns], got))
    if fetch:
        over = links.to(part.at[:, columns], beyond.at[:, columns], around.beyond)
    kept, sent_on = side(around.z_lo), side(1 - around.z_lo)
    twin = links.to(got.at[:, sent_on], half, around.twin)
    quarter = lambda k: ring.quarter(half, turned(around.y, k))
    ring.bind(links, around, scratch[1:], quarter(2), quarter(1), quarter(3), quarter(0))
    spread = RowSpread(ring, links, locals_, around, ring.total, own_side)
    both = links.to(own_side, own_side, around.twin)
    core = links.to(stretch, stretch, around.partner)

    if fetch:

        @pl.when(around.gives)
        def _():
            over.start()

        yield

    @pl.when(around.keeps)
    def _():
        if fetch:
            over.wait_recv()
        for copy in loads:
            copy.start()

    yield

    @pl.when(around.keeps)
    def _():
        for copy in loads:
            copy.wait()
        add_into(got, of(got), of(mine), count=rows, step=64)
        twin.start()

    yield

    @pl.when(around.keeps)
    def _():
        twin.wait_recv()
        add_into(half, of(half), lambda rows: got[rows, kept], count=rows, step=64)
        ring.begin()
        twin.wait_send()

    yield

    @pl.when(around.keeps)
    def _():
        ring.merge()

    yield

    @pl.when(around.keeps)
    def _():
        ring.sum()
        spread.begin()

    yield

    @pl.when(around.keeps)
    def _():
        spread.pass_on()

    yield

    @pl.when(around.keeps)
    def _():
        spread.end()
        both.start()

    yield

    @pl.when(around.keeps)
    def _():
        both.wait_recv()
        core.start()

    yield

    @pl.when(around.keeps)
    def _():
        ring.sent()
        spread.sent()
        both.wait_send()
        core.wait_send()

    @pl.when(around.gives)
    def _():
        if fetch:
            over.wait_send()
        core.wait_recv()

    yield


def across_and_back(ring, total, spare, from_beyond, from_twin, full, first, links, locals_, around):
    over = links.to(total, from_beyond, around.beyond)
    twin = links.to(total, from_twin, around.twin)
    spread = RowSpread(ring, links, locals_, around, spare, full, first)
    span = full.at[pl.ds(first, SIDE * ring.size)]
    core = links.to(span, span, around.partner)

    @pl.when(around.gives)
    def _():
        over.start()

    yield

    @pl.when(around.keeps)
    def _():
        over.wait_recv()
        add_into(total, of(total), of(from_beyond), count=ring.size, step=ring.step)
        twin.start()

    yield

    @pl.when(around.keeps)
    def _():
        twin.wait_recv()
        add_into(spare, of(total), of(from_twin), count=ring.size, step=ring.step)
        spread.begin()

    yield

    @pl.when(around.keeps)
    def _():
        spread.pass_on()

    yield

    @pl.when(around.keeps)
    def _():
        spread.end()
        core.start()

    yield

    @pl.when(around.keeps)
    def _():
        twin.wait_send()
        spread.sent()
        core.wait_send()

    @pl.when(around.gives)
    def _():
        over.wait_send()
        core.wait_recv()

    yield


def right_sum(summed, full, unit, links, locals_, around, scratch):
    stretch = full.at[:, pl.ds(unit, WIDE)]
    total, spare, from_beyond, from_twin = scratch
    ring = right_ring()
    load = locals_.of(summed.at[:, pl.ds(unit, WIDE)], total)
    load.start()
    yield
    load.wait()
    yield from across_and_back(
        ring, total, spare, from_beyond, from_twin, stretch, 0, links, locals_, around
    )


def attn_sum(part, full, unit, links, locals_, around, held_terms, scratch):
    own_terms, up_terms, down_terms = held_terms
    from_beyond, from_twin = scratch[:2]
    *sizes, first = unit
    ring = RowRing(*sizes)
    quarter = lambda k: ring.quarter(part, turned(around.y, k), first)
    loads = [
        locals_.of(quarter(k), held) for k, held in ((1, up_terms), (3, down_terms), (0, own_terms))
    ]
    ring.bind(links, around, scratch[2:], quarter(2), up_terms, down_terms, own_terms)
    ring.begin()
    for copy in loads:
        copy.start()
    yield
    for copy in loads:
        copy.wait()
    ring.merge()
    yield
    ring.sum()
    yield from across_and_back(
        ring, ring.total, own_terms, from_beyond, from_twin, full, first, links, locals_, around
    )
    ring.sent()
    yield


def sum_everywhere(values, places, links, place):
    x, y, z_hi, z_lo, core = place
    by_x, by_core, by_y, by_z = places
    z = z_hi * 2 + z_lo
    rounds = (
        (by_x, x, [device(turned(x, k), y, z_hi, z_lo, core) for k in (1, 2, 3)]),
        (by_core, core, [device(x, y, z_hi, z_lo, 1 - core)]),
        (by_y, y, [device(x, turned(y, k), z_hi, z_lo, core) for k in (1, 2, 3)]),
        (by_z, z, [z_device(x, y, turned(z, k), core) for k in (1, 2, 3)]),
    )
    for slots, mine, peers in rounds:
        slots[mine] = values[...]
        copies = [links.to(slots.at[mine], slots.at[mine], peer) for peer in peers]
        for copy in copies:
            copy.start()
        yield
        for copy in copies:
            copy.wait()
        total = slots[0]
        for slot in range(1, slots.shape[0]):
            total = total + slots[slot]
        values[...] = total
    yield


def z_device(x, y, z, core):
    return device(x, y, lax.div(z, 2), lax.rem(z, 2), core)


def attention_back(
    queries, keys, values, d_attended, row_info, segment_row, turns, qkv, d_keys, d_values, d_proj, d_normed, score_scale
):
    bf16, f32 = jnp.bfloat16, jnp.float32
    keep, from_after, from_before = turns
    lane = lax.broadcasted_iota(jnp.int32, (1, 128), 1)
    d_keys[...] = jnp.zeros_like(d_keys)
    d_values[...] = jnp.zeros_like(d_values)

    def turned_back(grads, rows):
        return (
            grads * keep[rows, :]
            + pltpu.roll(grads, 120, 1) * from_after[rows, :]
            + pltpu.roll(grads, 8, 1) * from_before[rows, :]
        )

    for block in (3, 2, 1, 0):
        first, end = block * PAIR, (block + 1) * PAIR
        rows, before = pl.ds(first, PAIR), pl.ds(0, end)
        info = row_info[rows, :]
        places = first + lax.broadcasted_iota(jnp.int32, (PAIR, end), 0)
        allowed = (info[:, 4:5] == segment_row[:, 0:end]) & (
            lax.broadcasted_iota(jnp.int32, (PAIR, end), 1) <= places
        )
        info_lane = lax.broadcasted_iota(jnp.int32, info.shape, 1)

        @pl.loop(0, 2)
        def _(pair):
            lanes = pl.ds(pl.multiple_of(pair * 128, 128), 128)
            query, grad = queries[rows, lanes], d_attended[rows, lanes]
            key, value = keys[before, lanes], values[before, lanes]
            d_query = jnp.zeros((PAIR, 128), f32)
            for head in range(2):
                inside = (lane >= head * HEAD_DIM) & (lane < (head + 1) * HEAD_DIM)
                query_h = jnp.where(inside, query, jnp.zeros_like(query))
                grad_h = jnp.where(inside, grad, jnp.zeros_like(grad))
                key_h = jnp.where(inside, key, jnp.zeros_like(key))
                log_norm = jnp.sum(
                    jnp.where(info_lane == pair * 2 + head, info, 0.0), axis=1, keepdims=True
                )
                scores = jnp.where(allowed, matmul(query_h, key, NT) * score_scale, -1e30)
                prob = jnp.exp(scores - log_norm)
                d_prob = matmul(grad_h, value, NT)
                row_dots = jnp.sum(prob * d_prob, axis=1, keepdims=True)
                d_score = (prob * (d_prob - row_dots)).astype(bf16)
                d_query = d_query + matmul(d_score, key_h, NN)
                d_keys[before, lanes] += matmul(d_score, query_h, TN)
                d_values[before, lanes] += matmul(prob.astype(bf16), grad_h, TN)
            d_proj[rows, lanes] = turned_back(d_query * score_scale, rows).astype(bf16)
            key_lanes = pl.ds(pl.multiple_of(256 + pair * 128, 128), 128)
            d_proj[rows, key_lanes] = turned_back(d_keys[rows, lanes] * score_scale, rows).astype(bf16)
            value_lanes = pl.ds(pl.multiple_of(512 + pair * 128, 128), 128)
            d_proj[rows, value_lanes] = d_values[rows, lanes].astype(bf16)

        @pl.loop(0, 2048, step=512)
        def _(column):
            columns = pl.ds(pl.multiple_of(column, 512), 512)
            total = matmul(d_proj[rows, 0:256], qkv[0, columns, :], NT)
            total = total + matmul(d_proj[rows, 256:512], qkv[1, columns, :], NT)
            total = total + matmul(d_proj[rows, 512:768], qkv[2, columns, :], NT)
            d_normed[rows, columns] = total.astype(bf16)

        yield


ORDER = (
    "l3", "l0", "f", "l2", "r0", "a2", "r1", "l0", "l1", "f", "l1", "f", "l0", "f",
    "l0", "l1", "r0", "a2", "f", "l0", "l1", "l2", "f", "l2", "l3", "l1", "l0", "r1",
    "f", "a1", "l3", "a0", "r0", "f", "l0", "l2", "a2", "l1", "r1", "f", "a1", "f",
    "a0", "l3", "l2", "l1", "a2", "r0", "a1", "l0", "a1", "a0", "l3", "r1", "l2", "l0",
    "r0", "f", "l3", "a0", "e", "l1", "f", "r1", "a2", "l2", "r0", "e", "l1", "a1",
    "l3", "r0", "e", "r1", "a0", "a2", "r1", "l2", "a1", "l3", "e", "a0", "a2", "a1",
    "l2", "a2", "a0", "a1", "l2", "l3", "a0", "e", "l3",
)


def last_kernel(
    queries_in,
    keys_in,
    values_in,
    d_attended_in,
    row_info,
    segment_row,
    keep,
    from_after,
    from_before,
    qkv,
    normed,
    tokens,
    d_mid,
    gain,
    ffn_part,
    mid,
    gate_part,
    gate_beyond,
    up_part,
    down_sum,
    out_part,
    gain_part,
    shift_part,
    mixed,
    input_grad,
    gate_full,
    up_full,
    down_full,
    qkv_full,
    out_full,
    sums,
    up_beyond,
    qkv_part,
    queries,
    keys,
    values,
    d_attended,
    d_keys,
    d_values,
    d_proj,
    d_normed,
    normed_tile,
    grad_tile,
    d_in,
    mixed_rows,
    ffn_rows,
    normed_sems,
    grad_sems,
    ready,
    sends,
    arrives,
    local_sems,
    by_x,
    by_core,
    by_y,
    by_z,
    *scratch,
):
    bf16 = jnp.bfloat16
    place = here()
    x, y, z_hi, z_lo, core = place
    z = z_hi * 2 + z_lo
    around = Around(place)
    links, locals_ = Links(sends, arrives), Locals(local_sems)
    swap_with = device(x, y, core, z_lo, z_hi)
    terms, ffn_terms = ByRow(d_normed, place), ByStep(ffn_part)

    def own_terms(step, rows):
        first = (core * SIDE + turned(x, SIDE - step)) * BLOCK
        return d_normed[pl.ds(pl.multiple_of(first + rows.start, 16), rows.size), :]

    scatter_ffn = Scatter(
        lambda step, rows: ffn_rows[step, rows, :], lambda step: ffn_terms.at(step, 1), place, scratch[:7]
    )
    scatter = Scatter(own_terms, lambda step: terms.at(step, 1), place, scratch[:3] + scratch[7:11])
    scratch = scratch[11:]
    units = {}
    mine, *got = scratch[:3]
    scratch = scratch[3:]
    refs_of = ((gate_part, gate_beyond, gate_full), (up_part, up_beyond, up_full))
    for index in range(4):
        units[f"l{index}"] = left_sum(
            *refs_of[index // 2],
            (index % 2) * WIDE,
            index > 1,
            links,
            locals_,
            around,
            mine,
            got[index % 2],
            scratch[:6],
        )
        scratch = scratch[6:]
    for index in range(2):
        units[f"r{index}"] = right_sum(down_sum, down_full, index * WIDE, links, locals_, around, scratch[:4])
        scratch = scratch[4:]
    out_terms, scratch = scratch[:3], scratch[3:]
    held_terms = (
        [ref.at[pl.ds(0, 768)] for ref in (queries, keys, values)],
        [d_proj.at[pl.ds(0, 768), pl.ds(256 * index, 256)] for index in range(3)],
        out_terms,
    )
    for index, unit in enumerate(ATTN_UNITS):
        refs = (out_part, out_full) if index == 2 else (qkv_part, qkv_full)
        units[f"a{index}"] = attn_sum(*refs, unit, links, locals_, around, held_terms[index], scratch[:7])
        scratch = scratch[7:]
    units["e"] = sum_everywhere(sums, (by_x, by_core, by_y, by_z), links, place)
    units["t"] = attention_back(
        queries,
        keys,
        values,
        d_attended,
        row_info,
        segment_row,
        (keep, from_after, from_before),
        qkv,
        d_keys,
        d_values,
        d_proj,
        d_normed,
        HEAD_DIM ** (-0.5),
    )

    def on(*names):
        for name in names:
            next(units[name])

    load_attn = [
        locals_.of(source, held)
        for source, held in (
            (queries_in, queries),
            (keys_in, keys),
            (values_in, values),
            (d_attended_in, d_attended),
        )
    ]
    load_ffn = [locals_.of(ffn_terms.at(step, 0), ffn_rows.at[step]) for step in range(SIDE)]
    swaps = [links.to(mixed_rows, mixed, swap_with), links.to(d_in, input_grad, swap_with)]
    stays = [locals_.of(mixed_rows, mixed), locals_.of(d_in, input_grad)]

    def give(index):
        @pl.when(around.gives)
        def _():
            swaps[index].start()

        @pl.when(around.keeps)
        def _():
            stays[index].start()

    def load_normed(chunk):
        columns = pl.ds(pl.multiple_of(chunk * TILE, TILE), TILE)
        slot = lax.rem(chunk, 2)
        return pltpu.make_async_copy(normed.at[:, columns], normed_tile.at[slot], normed_sems.at[slot])

    def store_grad(chunk):
        slot = lax.rem(chunk, 2)
        return [
            pltpu.make_async_copy(
                grad_tile.at[slot, pl.ds(channel * TILE, TILE)],
                qkv_part.at[pl.ds(pl.multiple_of(channel * 2048 + chunk * TILE, TILE), TILE)],
                grad_sems.at[slot, channel],
            )
            for channel in range(3)
        ]

    def qkv_grads(first, end):
        @pl.loop(first, end)
        def _(chunk):
            slot = lax.rem(chunk, 2)
            load_normed(chunk).wait()

            @pl.when(chunk + 1 < 8)
            def _():
                load_normed(chunk + 1).start()

            @pl.when(chunk > first + 1)
            def _():
                for copy in store_grad(chunk):
                    copy.wait()

            grads = matmul(normed_tile[slot], d_proj[...], TN).astype(bf16)
            for channel in range(3):
                grad_tile[slot, channel * TILE : (channel + 1) * TILE, :] = grads[
                    :, channel * TILE : (channel + 1) * TILE
                ]
            for copy in store_grad(chunk):
                copy.start()

        for chunk in (end - 2, end - 1):
            for copy in store_grad(jnp.int32(chunk)):
                copy.wait()

    for copy in load_ffn + load_attn:
        copy.start()
    load_normed(jnp.int32(0)).start()
    peers = line_peers(place) + [device(x, turned(y, k), z_hi, z_lo, core) for k in (1, 2, 3)]
    peers += [z_device(x, y, turned(z, k), core) for k in (1, 2, 3)]

    @pl.when(around.gives)
    def _():
        greet(peers + [swap_with])

    @pl.when(around.keeps)
    def _():
        greet(peers)

    def mix(rows):
        mixed_rows[rows, :] = (mid[rows, :] + scatter_ffn.rows(rows)).astype(bf16)

    def bias_grads():
        width = d_proj.shape[1] // 3
        mine_columns = pl.ds(pl.multiple_of((core * SIDE + x) * width, width), width)
        for channel in range(3):
            grads = d_proj[:, channel * width : (channel + 1) * width].astype(jnp.float32)
            sums[4 + channel : 5 + channel, mine_columns] = jnp.sum(grads, axis=0, keepdims=True)

    def back(rows):
        grad = scatter.rows(rows)
        centre, scale = moments(tokens[rows, :].astype(jnp.float32))
        unit = centre * scale
        sums[0:1, :] += jnp.sum(grad * unit, axis=0, keepdims=True)
        sums[1:2, :] += jnp.sum(grad, axis=0, keepdims=True)
        scaled = grad * gain[...]
        d_in[rows, :] = d_mid[rows, :] + scale * (
            scaled
            - jnp.mean(scaled, axis=-1, keepdims=True)
            - unit * jnp.mean(scaled * unit, axis=-1, keepdims=True)
        )

    def foreground():
        for step in (2, 1, 3, 0):
            scatter_ffn.across[step].start()
        yield
        for copy in load_ffn:
            copy.wait()
        for step in (2, 1, 3):
            scatter_ffn.merge(step)
        yield
        for copy in load_attn:
            copy.wait()
        sums[...] = jnp.zeros_like(sums)
        sums[2:3, :] = gain_part[...]
        sums[3:4, :] = shift_part[...]
        on("t")
        yield
        on("t")
        yield
        on("t")
        yield
        on("t")
        yield
        qkv_grads(0, 8)
        bias_grads()
        yield
        scatter_ffn.finish()
        tile_rows(mix)
        for peer in line_peers(place):
            pl.semaphore_signal(ready, inc=1, device_id=peer, device_id_type=MESH)
        give(0)
        yield
        pl.semaphore_wait(ready, SIDE)
        for step in (2, 1, 3, 0):
            scatter.across[step].start()
        yield
        for step in (2, 1, 3):
            scatter.merge(step)
        yield
        scatter.finish()
        tile_rows(back)
        yield
        give(1)
        yield

    units["f"] = foreground()
    on(*ORDER)
    for unit in units.values():
        for _ in unit:
            pass

    @pl.when(around.gives)
    def _():
        for copy in swaps:
            copy.wait()

    @pl.when(around.keeps)
    def _():
        for copy in stays:
            copy.wait()


ANY = pl.BlockSpec(memory_space=pl.ANY)
HELD = pl.BlockSpec(memory_space=pltpu.VMEM)


def call(kernel, collective_id, args, in_specs, outs, out_specs, scratch):
    return pl.pallas_call(
        kernel,
        out_shape=[jax.ShapeDtypeStruct(shape, kind) for shape, kind in outs],
        in_specs=in_specs,
        out_specs=out_specs,
        scratch_shapes=list(scratch),
        compiler_params=pltpu.CompilerParams(
            collective_id=collective_id, has_side_effects=True, vmem_limit_bytes=VMEM_LIMIT
        ),
    )(*args)


def member_layout(seq_length, seq_owner, member, row_total):
    entry_total = seq_length.shape[0]
    row_ids = jnp.arange(row_total, dtype=jnp.int32)
    entry_ids = jnp.arange(entry_total, dtype=jnp.int32)
    earlier = (entry_ids[:, None] < entry_ids[None, :]).astype(jnp.int32)
    sharing = (seq_owner[:, None] == seq_owner[None, :]).astype(jnp.int32)
    starts = jnp.sum(seq_length[:, None] * sharing * earlier, axis=0)
    owned_now = (seq_owner == member).astype(jnp.int32)
    inside = (
        owned_now[None, :]
        * (row_ids[:, None] >= starts[None, :]).astype(jnp.int32)
        * (row_ids[:, None] < (starts + seq_length)[None, :]).astype(jnp.int32)
    )
    live_rows = jnp.sum(inside, axis=1)
    segment = jnp.sum(inside * entry_ids[None, :], axis=1) + (1 - live_rows) * (
        entry_total + row_ids
    )
    position = jnp.sum(inside * (row_ids[:, None] - starts[None, :]), axis=1)
    return (segment, position, live_rows)


def rotary_tables(position):
    half_rot = ROT // 2
    frequency = jnp.power(
        jnp.float32(10000.0), -2.0 * jnp.arange(half_rot, dtype=jnp.float32) / ROT
    )
    lane = jnp.arange(128) % HEAD_DIM
    frequency = jnp.where(lane < ROT, jnp.tile(frequency, 128 // half_rot), 0.0)
    angles = position.astype(jnp.float32)[:, None] * frequency[None, :]
    sine = jnp.sin(angles)
    from_after = jnp.where(lane < half_rot, sine, 0.0)
    from_before = jnp.where(lane >= half_rot, -sine, 0.0)
    return (jnp.cos(angles), from_after, from_before)


def body(
    tokens,
    seq_length,
    seq_owner,
    ln1_gain,
    ln1_bias,
    qkv_weight,
    qkv_bias,
    out_weight,
    ln2_gain,
    ln2_bias,
    gate_up_weight,
    down_weight,
    out_grad,
):
    bf16, f32 = jnp.bfloat16, jnp.float32
    x, y, z_hi, z_lo, core = here()
    row_total = BLOCK * 8
    rows_here, rows_all = (BLOCK, 2048), (row_total, 2048)
    local_heads = qkv_weight.shape[2] // HEAD_DIM
    member = (y * 2 + z_lo) * 2 + z_hi
    shard = core * SIDE + x
    segment, position, live_rows = member_layout(seq_length, seq_owner, member, row_total)
    live = lax.dynamic_slice_in_dim(live_rows, shard * BLOCK, BLOCK, 0)[:, None].astype(f32)
    segments = segment.astype(f32)[:, None]
    segment_row = segment.astype(f32)[None]
    keep, from_after, from_before = rotary_tables(position)
    flat = (row_total, qkv_weight.shape[2])
    dma, vmem = pltpu.SemaphoreType.DMA, pltpu.VMEM
    tokens_here, cot, normed1, cot_rows, attn_part, qkv, out, down, queries, keys, values, attended, row_info = call(
        first_kernel,
        1,
        (
            tokens,
            out_grad,
            live,
            ln1_gain[None],
            ln1_bias[None],
            qkv_weight,
            out_weight,
            down_weight,
            qkv_bias,
            segments,
            segment_row,
            keep,
            from_after,
            from_before,
        ),
        [ANY, ANY, HELD, HELD, HELD, ANY, ANY, ANY] + [HELD] * 6,
        [
            (rows_here, bf16),
            (rows_here, bf16),
            (rows_all, bf16),
            (rows_all, bf16),
            (rows_all, bf16),
            (qkv_weight.shape, bf16),
            (out_weight.shape, bf16),
            (down_weight.shape, bf16),
            (flat, bf16),
            (flat, bf16),
            (flat, bf16),
            (flat, bf16),
            ((row_total, 128), f32),
        ],
        [ANY] * 5 + [HELD] * 8,
        (
            vmem(rows_here, bf16),
            vmem(rows_here, bf16),
            vmem(rows_here, bf16),
            vmem(qkv_bias.shape, f32),
            vmem(rows_all, bf16),
            vmem((PAIR, 2048), bf16),
            dma((3,)),
            dma((3,)),
            dma((16,)),
        )
        + Gather.scratch * 2
        + fetch_scratch(3),
    )

    gate_up_t = jnp.swapaxes(gate_up_weight, 1, 2)
    ff = down_weight.shape[0]
    mid_stream, d_mid, gain2_part, shift2_part, *ff_parts, ffn_part, d_attended, out_grad = call(
        middle_kernel,
        2,
        (
            attn_part,
            tokens_here,
            ln2_gain[None],
            ln2_bias[None],
            gate_up_t,
            down,
            cot_rows,
            attended,
            out,
            cot,
        ),
        [ANY, HELD, HELD, HELD, ANY, ANY, ANY, ANY, ANY, HELD],
        [
            (rows_here, f32),
            (rows_here, f32),
            ((1, 2048), f32),
            ((1, 2048), f32),
            (down_weight.shape, bf16),
            (down_weight.shape, bf16),
            (down_weight.shape, bf16),
            (down_weight.shape, bf16),
            ((ff // SIDE, 2048), bf16),
            (rows_all, bf16),
            (attended.shape, bf16),
            (out.shape, bf16),
        ],
        [HELD] * 4 + [ANY] * 6 + [HELD, HELD],
        (
            vmem((2, ff, 2048), bf16),
            vmem((ff, 2048), bf16),
            vmem(out.shape, bf16),
            vmem(rows_all, bf16),
            vmem(rows_all, bf16),
            vmem(rows_all, bf16),
            vmem(attended.shape, bf16),
            vmem((row_total, ff), bf16),
            vmem((row_total, ff), bf16),
            vmem((row_total, ff), bf16),
            vmem((row_total, ff), f32),
            vmem((SIDE, BLOCK, 2048), bf16),
            vmem((SIDE, BLOCK, 2048), bf16),
            vmem((PAIR, 2048), bf16),
            vmem((2, ff, TILE), bf16),
            dma((8,)),
            dma((8,)),
            dma((6,)),
            dma,
            dma((2,)),
        )
        + Scatter.scratch
        + Scatter.sems
        + Gather.scratch * 2
        + fetch_scratch(2)
        + (dma((5,)), dma((5,)))
        + (vmem((ff // SIDE, 2048), bf16),) * 3
        + RowRing(*DOWN_RING).scratch(),
    )

    gate_part, up_part, _, gate_beyond, down_sum = ff_parts
    small = (8, 2048)
    qkv_rows = (3 * 2048, flat[1])
    mixed, input_grad, gate_full, up_full, down_full, qkv_full, out_full, sums, _, _ = call(
        last_kernel,
        4,
        (
            queries,
            keys,
            values,
            d_attended,
            row_info,
            segment_row,
            keep,
            from_after,
            from_before,
            qkv,
            normed1,
            tokens_here,
            d_mid,
            ln1_gain[None],
            ffn_part,
            mid_stream,
            gate_part,
            gate_beyond,
            up_part,
            down_sum,
            out_grad,
            gain2_part,
            shift2_part,
        ),
        [ANY] * 4 + [HELD] * 6 + [ANY] + [HELD] * 3 + [ANY, HELD] + [ANY] * 5 + [HELD] * 2,
        [
            (rows_here, bf16),
            (rows_here, f32),
            (down_weight.shape, bf16),
            (down_weight.shape, bf16),
            (down_weight.shape, bf16),
            (qkv_rows, bf16),
            (out.shape, bf16),
            (small, f32),
            (down_weight.shape, bf16),
            (qkv_rows, bf16),
        ],
        [ANY] * 7 + [HELD] + [ANY] * 2,
        (
            vmem(flat, bf16),
            vmem(flat, bf16),
            vmem(flat, bf16),
            vmem(flat, bf16),
            vmem(flat, f32),
            vmem(flat, f32),
            vmem((row_total, 3 * flat[1]), bf16),
            vmem(rows_all, bf16),
            vmem((2, row_total, TILE), bf16),
            vmem((2, 3 * TILE, flat[1]), bf16),
            vmem(rows_here, f32),
            vmem(rows_here, bf16),
            vmem((SIDE, BLOCK, 2048), bf16),
            dma((2,)),
            dma((2, 3)),
            pltpu.SemaphoreType.REGULAR,
            dma((LINK_COUNT,)),
            dma((LINK_COUNT,)),
            dma((LOCAL_COUNT,)),
            vmem((SIDE, *small), f32),
            vmem((2, *small), f32),
            vmem((SIDE, *small), f32),
            vmem((SIDE, *small), f32),
        )
        + Scatter.scratch
        + Scatter.sems
        + left_scratch(ff, 4)
        + right_scratch(2)
        + (vmem((64, 2048), bf16),) * 3
        + attn_scratch(),
    )
    gate_up_grad = jnp.swapaxes(jnp.stack([gate_full.astype(f32), up_full.astype(f32)]), 1, 2)
    down_grad = down_full.astype(f32)
    qkv_weight_grad = qkv_full.reshape(3, 2048, -1).astype(f32)
    out_weight_grad = out_full.astype(f32)
    width = qkv_bias.shape[1]
    qkv_bias_grad = lax.dynamic_slice_in_dim(sums[4:7], (z_hi * SIDE + x) * width, width, 1)
    return (
        mixed,
        input_grad,
        sums[0],
        sums[1],
        qkv_weight_grad,
        qkv_bias_grad,
        out_weight_grad,
        sums[2],
        sums[3],
        gate_up_grad,
        down_grad,
    )


def solution(mesh):
    placed = (
        P(("dp", "tensor"), None),
        P(),
        P(),
        P(),
        P(),
        P(None, None, "tensor"),
        P(None, "tensor"),
        P("tensor", None),
        P(),
        P(),
        P(None, None, "tensor"),
        P("tensor", None),
        P(("dp", "tensor"), None),
    )
    return jax.shard_map(
        body,
        mesh=mesh,
        in_specs=placed,
        out_specs=(
            P(("dp", "tensor"), None),
            P(("dp", "tensor"), None),
            P(),
            P(),
            P(None, None, "tensor"),
            P(None, "tensor"),
            P("tensor", None),
            P(),
            P(),
            P(None, None, "tensor"),
            P("tensor", None),
        ),
        check_vma=False,
    )
```

```python
import functools

import jax
import jax.numpy as jnp
from jax import lax
from jax.experimental import pallas as pl
from jax.experimental.pallas import tpu as pltpu
from jax.sharding import PartitionSpec as P

HEAD_DIM = 64
ROT = 16
SIDE = 4
BLOCK = 128
AXES = ("dp", "tensor")
MESH = pl.DeviceIdType.MESH
VMEM_LIMIT = 54 * 2**20


def here():
    dp, tensor = lax.axis_index("dp"), lax.axis_index("tensor")
    x, z_hi = lax.rem(tensor, SIDE), lax.div(tensor, SIDE)
    y, z_lo, core = lax.div(dp, SIDE), lax.rem(lax.div(dp, 2), 2), lax.rem(dp, 2)
    return x, y, z_hi, z_lo, core


def device(x, y, z_hi, z_lo, core):
    return ((y * 2 + z_lo) * 2 + core, z_hi * SIDE + x)


def turned(value, by):
    return lax.rem(value + by, SIDE)


def pairs(move):
    found = []
    for dp in range(16):
        for tensor in range(8):
            goal = move(tensor % 4, dp // 4, tensor // 4, (dp // 2) % 2, dp % 2)
            if goal is not None:
                to_dp, to_tensor = device(*goal)
                found.append((dp * 8 + tensor, to_dp * 8 + to_tensor))
    return found


def permute(array, move):
    return lax.ppermute(array, AXES, pairs(move))


def swap_rows(x, y, z_hi, z_lo, core):
    return (x, y, core, z_lo, z_hi)


def remote(source, target, sends, arrives, index, device_id):
    return pltpu.make_async_remote_copy(
        src_ref=source,
        dst_ref=target,
        send_sem=sends.at[index],
        recv_sem=arrives.at[index],
        device_id=device_id,
        device_id_type=MESH,
    )


def greet(peers):
    barrier = pltpu.get_barrier_semaphore()
    for peer in peers:
        pl.semaphore_signal(barrier, inc=1, device_id=peer, device_id_type=MESH)
    pl.semaphore_wait(barrier, len(peers))


def line_peers(place):
    x, y, z_hi, z_lo, core = place
    found = [device(turned(x, k), y, z_hi, z_lo, core) for k in (1, 2, 3)]
    return found + [device(x, y, z_hi, z_lo, 1 - core)]


def row_block(full, core, x):
    return full.at[pl.ds(pl.multiple_of((core * SIDE + x) * BLOCK, BLOCK), BLOCK)]


class ByRow:
    def __init__(self, full, place):
        self.full, self.x, self.core = full, place[0], place[4]

    def at(self, step, other):
        core = 1 - self.core if other else self.core
        return row_block(self.full, core, turned(self.x, SIDE - step))

    def landing(self, step, other, by, across):
        return self.at(step, other)


class ByStep:
    def __init__(self, full):
        self.full = full

    def at(self, step, other):
        return self.full.at[pl.ds((step * 2 + other) * BLOCK, BLOCK)]

    def landing(self, step, other, by, across):
        return self.at((step + by) % SIDE, 1 - other if across else other)


class Gather:
    scratch = (
        pltpu.SemaphoreType.DMA((4,)),
        pltpu.SemaphoreType.DMA((4,)),
        pltpu.SemaphoreType.DMA((4,)),
        pltpu.SemaphoreType.DMA((4,)),
    )

    def __init__(self, block, layout, place, sems):
        x, y, z_hi, z_lo, core = place
        x_send, x_arrive, core_send, core_arrive = sems
        half = BLOCK // 2
        right = device(turned(x, 1), y, z_hi, z_lo, core)
        left = device(turned(x, 3), y, z_hi, z_lo, core)
        partner = device(x, y, z_hi, z_lo, 1 - core)

        def passed(step, first, by, index, to):
            part = pl.ds(first, half)
            return remote(
                layout.at(step, 0).at[part],
                layout.landing(step, 0, by, False).at[part],
                x_send,
                x_arrive,
                index,
                to,
            )

        self.right = remote(block, layout.landing(0, 0, 1, False), x_send, x_arrive, 0, right)
        self.left = remote(block, layout.landing(0, 0, 3, False), x_send, x_arrive, 1, left)
        self.right_on = passed(1, 0, 1, 2, right)
        self.left_on = passed(3, half, 3, 3, left)
        self.across = [
            remote(
                block if step == 0 else layout.at(step, 0),
                layout.landing(step, 0, 0, True),
                core_send,
                core_arrive,
                step,
                partner,
            )
            for step in range(SIDE)
        ]

    def start(self):
        self.right.start()
        self.left.start()
        self.across[0].start()

    def arrive(self, step):
        if step == 1:
            self.right.wait_recv()
            self.right_on.start()
        elif step == 3:
            self.left.wait_recv()
            self.left_on.start()
        else:
            self.right_on.wait_recv()
            self.left_on.wait_recv()
        self.across[step].start()

    def finish(self):
        for copy in (self.right, self.left, self.right_on, self.left_on, *self.across):
            copy.wait_send()

    def take(self):
        for copy in self.across:
            copy.wait_recv()


class Scatter:
    buffers = (
        pltpu.VMEM((SIDE, BLOCK, 2048), jnp.bfloat16),
        pltpu.VMEM((3, BLOCK, 2048), jnp.bfloat16),
        pltpu.VMEM((3, BLOCK, 2048), jnp.bfloat16),
    )
    sems = (
        pltpu.SemaphoreType.DMA((SIDE,)),
        pltpu.SemaphoreType.DMA((SIDE,)),
        pltpu.SemaphoreType.DMA((3,)),
        pltpu.SemaphoreType.DMA((3,)),
    )
    scratch = buffers + sems

    def __init__(self, own, given, place, scratch):
        x, y, z_hi, z_lo, core = place
        self.own, (self.other, self.leaving, self.arrived) = own, scratch[:3]
        core_send, core_arrive, x_send, x_arrive = scratch[3:]
        partner = device(x, y, z_hi, z_lo, 1 - core)
        self.across = [
            remote(given(step), self.other.at[step], core_send, core_arrive, step, partner)
            for step in range(SIDE)
        ]
        self.along = [
            remote(
                self.leaving.at[step - 1],
                self.arrived.at[step - 1],
                x_send,
                x_arrive,
                step - 1,
                device(turned(x, SIDE - step), y, z_hi, z_lo, core),
            )
            for step in (1, 2, 3)
        ]

    def merge(self, step):
        self.across[step].wait_recv()

        def add(rows):
            both = self.own(step, rows).astype(jnp.float32) + self.other[step, rows, :].astype(jnp.float32)
            self.leaving[step - 1, rows, :] = both.astype(jnp.bfloat16)

        tile_rows(add)
        self.along[step - 1].start()

    def finish(self):
        self.across[0].wait_recv()
        for copy in self.along:
            copy.wait()
        for copy in self.across:
            copy.wait_send()

    def rows(self, rows):
        total = self.own(0, rows).astype(jnp.float32) + self.other[0, rows, :].astype(jnp.float32)
        for step in range(3):
            total = total + self.arrived[step, rows, :].astype(jnp.float32)
        return total


class Loaded:
    def __init__(self, full, held, place, sems):
        there, here_ = ByRow(full, place), ByStep(held)
        self.copies = [
            pltpu.make_async_copy(there.at(step, other), here_.at(step, other), sems.at[step * 2 + other])
            for step in range(SIDE)
            for other in range(2)
        ]

    def start(self):
        for copy in self.copies:
            copy.start()

    def wait(self):
        for copy in self.copies:
            copy.wait()


class Fetch:
    def __init__(self, weight, filled, cut, place, sems, index):
        x, y, z_hi, z_lo, core = place
        send, arrive, own_sem = sems
        self.own = pltpu.make_async_copy(weight, filled, own_sem.at[index])
        across = device(x, y, 1 - z_hi, 1 - z_lo, z_hi)
        up = device(x, turned(y, 1), z_hi, z_lo, core)
        down = device(x, turned(y, 3), z_hi, z_lo, core)
        base = index * 5

        def moved(ref, quarter, half, slot, to):
            source = cut(ref, quarter, half)
            return remote(source, cut(filled, quarter, half), send, arrive, base + slot, to)

        self.across = moved(weight, y, None, 0, across)
        self.up = moved(filled, y, None, 1, up)
        self.down = moved(filled, y, None, 2, down)
        self.up_on = moved(filled, turned(y, 3), 0, 3, up)
        self.down_on = moved(filled, turned(y, 1), 1, 4, down)

    def spread(self):
        self.across.wait_recv()
        self.up.start()
        self.down.start()

    def pass_on(self):
        self.up.wait_recv()
        self.up_on.start()
        self.down.wait_recv()
        self.down_on.start()

    def finish(self):
        self.up_on.wait_recv()
        self.down_on.wait_recv()
        for copy in (self.across, self.up, self.down, self.up_on, self.down_on):
            copy.wait_send()


def fetch_scratch(count):
    return (
        pltpu.SemaphoreType.DMA((5 * count,)),
        pltpu.SemaphoreType.DMA((5 * count,)),
        pltpu.SemaphoreType.DMA((count,)),
    )


def fetch_peers(place):
    x, y, z_hi, z_lo, core = place
    return [device(x, y, 1 - z_hi, 1 - z_lo, z_hi)] + [
        device(x, turned(y, k), z_hi, z_lo, core) for k in (1, 3)
    ]


def quarter_rows(size, *before):
    quarter_size = size // SIDE
    split = -(-quarter_size // 32) * 16

    def cut(weight, quarter, half):
        first = pl.multiple_of(quarter * quarter_size, 16)
        if half is None:
            rows = pl.ds(first, quarter_size)
        elif half == 0:
            rows = pl.ds(first, split)
        else:
            rows = pl.ds(first + split, quarter_size - split)
        return weight.at[(*before, rows)]

    return cut


QKV_CUT = quarter_rows(2048, slice(None))
OUT_CUT = quarter_rows(256)
FF_CUT = quarter_rows(704)


def moments(values):
    centre = values - jnp.mean(values, axis=-1, keepdims=True)
    return centre, lax.rsqrt(jnp.mean(centre * centre, axis=-1, keepdims=True) + 1e-05)


def tile_rows(body):
    @pl.loop(0, BLOCK, step=16)
    def _(row):
        body(pl.ds(pl.multiple_of(row, 16), 16))


def matmul(left, right, contract):
    return lax.dot_general(left, right, ((contract, ((), ()))), preferred_element_type=jnp.float32)


NN, NT, TN = ((1,), (0,)), ((1,), (1,)), ((0,), (0,))
PAIR = 2 * BLOCK
TILE = 256


class Locals:
    def __init__(self, sems):
        self.sems, self.used = sems, 0

    def of(self, source, target):
        self.used += 1
        return pltpu.make_async_copy(source, target, self.sems.at[self.used - 1])


def attention(queries, keys, values, row_info, segments, segment_row, attended, score_scale):
    bf16 = jnp.bfloat16
    lane = lax.broadcasted_iota(jnp.int32, (1, 128), 1)
    row_info[...] = jnp.where(lane == 4, segments[...], 0.0)
    for block in range(4):
        first, end = block * PAIR, (block + 1) * PAIR
        rows, before = pl.ds(first, PAIR), pl.ds(0, end)
        places = first + lax.broadcasted_iota(jnp.int32, (PAIR, end), 0)
        allowed = (segments[rows, :] == segment_row[:, 0:end]) & (
            lax.broadcasted_iota(jnp.int32, (PAIR, end), 1) <= places
        )

        @pl.loop(0, 2)
        def _(pair):
            lanes = pl.ds(pl.multiple_of(pair * 128, 128), 128)
            query, key, value = queries[rows, lanes], keys[before, lanes], values[before, lanes]
            mixed = jnp.zeros((PAIR, 128), jnp.float32)
            for head in range(2):
                inside = (lane >= head * HEAD_DIM) & (lane < (head + 1) * HEAD_DIM)
                query_h = jnp.where(inside, query, jnp.zeros_like(query))
                value_h = jnp.where(inside, value, jnp.zeros_like(value))
                scores = jnp.where(allowed, matmul(query_h, key, NT) * score_scale, -1e30)
                top = jnp.max(scores, axis=1, keepdims=True)
                raised = jnp.exp(scores - top)
                total = jnp.sum(raised, axis=1, keepdims=True)
                mixed = mixed + matmul((raised / total).astype(bf16), value_h, NN)
                row_info[rows, :] = jnp.where(
                    lane == pair * 2 + head, top + jnp.log(total), row_info[rows, :]
                )
            attended[rows, lanes] = mixed.astype(bf16)

        yield


def first_kernel(
    tokens,
    out_grad,
    live,
    gain,
    shift,
    qkv,
    out,
    down,
    gate_up,
    gain_mid,
    shift_mid,
    bias,
    segments,
    segment_row,
    keep,
    from_after,
    from_before,
    tokens_here,
    cot_here,
    normed_full,
    cot_full,
    mid,
    normed_mid,
    qkv_here,
    out_here,
    down_here,
    gate_up_here,
    queries,
    keys,
    values,
    attended,
    row_info,
    tok_buf,
    grad_buf,
    cot_buf,
    bias_buf,
    normed,
    part,
    swap_send,
    swap_arrive,
    own_sems,
    *sems,
):
    bf16 = jnp.bfloat16
    place = here()
    x, y, z_hi, z_lo, core = place
    lacking = core != z_hi
    swap_with = device(x, y, core, z_lo, z_hi)
    fetch_sems = sems[8:11]
    fetches = [
        Fetch(weight, filled, cut, place, fetch_sems, index)
        for index, (weight, filled, cut) in enumerate(
            [
                (qkv, qkv_here, QKV_CUT),
                (out, out_here, OUT_CUT),
                (down, down_here, FF_CUT),
                (gate_up.at[0], gate_up_here.at[0], FF_CUT),
                (gate_up.at[1], gate_up_here.at[1], FF_CUT),
            ]
        )
    ]

    def own_terms(step, rows):
        first = (core * SIDE + turned(x, SIDE - step)) * BLOCK
        return part[pl.ds(pl.multiple_of(first + rows.start, 16), rows.size), :]

    terms = ByRow(part, place)
    scatter = Scatter(own_terms, lambda step: terms.at(step, 1), place, sems[11:])
    moved = [(tokens, tok_buf), (out_grad, grad_buf), (bias, bias_buf)]
    swaps = [
        remote(source, target, swap_send, swap_arrive, index, swap_with)
        for index, (source, target) in enumerate(moved)
    ]
    locals_ = Locals(own_sems)
    stays = [locals_.of(source, target) for source, target in moved]
    gather = Gather(normed.at[pl.ds(0, BLOCK)], ByStep(normed), place, sems[:4])
    gather_cot = Gather(cot_buf, ByRow(cot_full, place), place, sems[4:8])
    by_step, by_row = ByStep(normed), ByRow(normed_full, place)
    normed_out = [
        locals_.of(by_step.at(step, other), by_row.at(step, other)) for step in range(SIDE) for other in range(2)
    ]
    stored = [
        locals_.of(tok_buf, tokens_here),
        locals_.of(cot_buf, cot_here),
        locals_.of(cot_buf, row_block(cot_full, core, x)),
    ]

    @pl.when(lacking)
    def _():
        greet(line_peers(place) + [swap_with] + fetch_peers(place))
        swaps[0].start()
        swaps[2].start()
        fetches[0].across.start()
        swaps[0].wait_recv()
        swaps[1].start()
        fetches[1].across.start()

    @pl.when(jnp.logical_not(lacking))
    def _():
        greet(line_peers(place))
        for copy in stays:
            copy.start()
        for fetch in fetches:
            fetch.own.start()
        stays[0].wait()

    def norm(rows):
        centre, scale = moments(tok_buf[rows, :].astype(jnp.float32))
        normed[rows, :] = (centre * scale * gain[...] + shift[...]).astype(bf16)

    tile_rows(norm)
    gather.start()
    stored[0].start()

    @pl.when(lacking)
    def _():
        fetches[0].spread()
        fetches[2].across.start()
        for copy in swaps:
            copy.wait_send()
        swaps[1].wait_recv()
        swaps[2].wait_recv()
        fetches[3].across.start()

    @pl.when(jnp.logical_not(lacking))
    def _():
        stays[1].wait()
        stays[2].wait()

    def mask(rows):
        cot_buf[rows, :] = (grad_buf[rows, :].astype(jnp.float32) * live[rows, :]).astype(bf16)

    tile_rows(mask)
    gather.arrive(1)
    gather.arrive(3)
    gather_cot.start()
    stored[1].start()
    stored[2].start()

    @pl.when(lacking)
    def _():
        fetches[0].pass_on()
        fetches[1].spread()
        fetches[2].spread()
        fetches[4].across.start()

    gather.arrive(2)
    gather.take()
    for copy in normed_out:
        copy.start()

    @pl.when(lacking)
    def _():
        fetches[0].finish()

    @pl.when(jnp.logical_not(lacking))
    def _():
        fetches[0].own.wait()

    @pl.loop(0, 8)
    def _(index):
        step, other = lax.div(index, 2), lax.rem(index, 2)
        whose = core + other * (1 - 2 * core)
        first = pl.multiple_of((whose * SIDE + turned(x, SIDE - step)) * BLOCK, BLOCK)
        rows = pl.ds(first, BLOCK)
        block = normed[pl.ds(pl.multiple_of(index * BLOCK, BLOCK), BLOCK), :]
        for channel, target in enumerate((queries, keys, values)):
            projected = matmul(block, qkv_here[channel], NN) + bias_buf[channel : channel + 1, :]
            for pair in range(2):
                lanes = projected[:, pair * 128 : (pair + 1) * 128]
                if channel < 2:
                    lanes = (
                        lanes * keep[rows, :]
                        - pltpu.roll(lanes, 120, 1) * from_after[rows, :]
                        - pltpu.roll(lanes, 8, 1) * from_before[rows, :]
                    )
                target[rows, pair * 128 : (pair + 1) * 128] = lanes.astype(bf16)

    @pl.when(lacking)
    def _():
        fetches[1].pass_on()
        fetches[2].pass_on()
        fetches[3].spread()

    gather_cot.arrive(1)
    gather_cot.arrive(3)
    blocks = attention(
        queries, keys, values, row_info, segments, segment_row, attended, HEAD_DIM ** (-0.5)
    )
    for block in range(4):
        next(blocks)
        rows = pl.ds(block * PAIR, PAIR)
        if block == 0:

            @pl.when(lacking)
            def _():
                fetches[1].finish()

            @pl.when(jnp.logical_not(lacking))
            def _():
                fetches[1].own.wait()

        @pl.loop(0, 2048, step=512)
        def _(column):
            columns = pl.ds(pl.multiple_of(column, 512), 512)
            part[rows, columns] = matmul(attended[rows, :], out_here[:, columns], NN).astype(bf16)

        if block == 0:

            @pl.when(lacking)
            def _():
                fetches[4].spread()

            gather_cot.arrive(2)

        if block == 1:

            @pl.when(core == 1)
            def _():
                for step in (2, 1, 3, 0):
                    scatter.across[step].start()

        if block == 2:

            @pl.when(core == 0)
            def _():
                for step in (2, 1, 3):
                    scatter.merge(step)

    @pl.when(core == 0)
    def _():
        for step in (2, 1, 3, 0):
            scatter.across[step].start()

    @pl.when(core == 1)
    def _():
        for step in (2, 1, 3):
            scatter.merge(step)

    @pl.when(lacking)
    def _():
        fetches[3].pass_on()
        fetches[4].pass_on()

    gather_cot.take()
    for each in (gather, gather_cot):
        each.finish()
    for copy in normed_out + stored:
        copy.wait()

    @pl.when(lacking)
    def _():
        for fetch in fetches[2:]:
            fetch.finish()

    @pl.when(jnp.logical_not(lacking))
    def _():
        for fetch in fetches[2:]:
            fetch.own.wait()

    scatter.finish()

    def norm_mid(rows):
        stream = tok_buf[rows, :].astype(jnp.float32) + scatter.rows(rows)
        mid[rows, :] = stream
        centre, scale = moments(stream)
        normed_mid[rows, :] = (centre * scale * gain_mid[...] + shift_mid[...]).astype(bf16)

    tile_rows(norm_mid)


def middle_kernel(
    normed_mid,
    mid,
    gain,
    gate_up_held,
    down_held,
    cot_full,
    attended_full,
    out_held,
    cot,
    d_mid,
    gain_part,
    shift_part,
    gate_grad,
    up_grad,
    down_grad,
    gate_beyond,
    down_sum,
    ffn_part,
    d_attended,
    out_grad,
    gate_up,
    down,
    out,
    normed,
    cot_rows,
    d_rows,
    attended,
    hidden,
    d_gate,
    d_up,
    d_hidden,
    own_rows,
    given_terms,
    ffn_tile,
    grad_tile,
    load_sems,
    att_sems,
    own_sems,
    ffn_sem,
    grad_sems,
    *scratch,
):
    bf16 = jnp.bfloat16
    place = here()
    x, y, z_hi, z_lo, core = place
    lacking = core != z_hi
    second = Scatter(
        lambda step, rows: own_rows[step, rows, :], lambda step: given_terms.at[step], place, scratch[:7]
    )
    gather = Gather(normed.at[pl.ds(0, BLOCK)], ByStep(normed), place, scratch[7:11])
    gather_d = Gather(d_rows.at[pl.ds(0, BLOCK)], ByStep(d_rows), place, scratch[11:15])
    scratch = scratch[15:]
    around = Around(place)
    links = Links(*scratch[:2])
    over = links.to(gate_grad, gate_beyond, around.beyond)
    ring = RowRing(*DOWN_RING)
    ring_terms = scratch[2:5]
    ring_loads = [
        pltpu.make_async_copy(ring.quarter(down_grad, turned(y, k)), held, load_sems.at[index])
        for index, (k, held) in enumerate(zip((1, 3, 0), ring_terms))
    ]
    ring.bind(links, around, scratch[5:], ring.quarter(down_grad, turned(y, 2)), *ring_terms)
    load_cot = Loaded(cot_full, cot_rows, place, load_sems)
    load_att = Loaded(attended_full, attended, place, att_sems)
    load_normed = pltpu.make_async_copy(normed_mid, normed.at[pl.ds(0, BLOCK)], own_sems.at[0])
    load_gate_up = pltpu.make_async_copy(gate_up_held, gate_up, own_sems.at[1])
    load_down = pltpu.make_async_copy(down_held, down, own_sems.at[2])
    load_out = pltpu.make_async_copy(out_held, out, own_sems.at[3])

    load_normed.start()
    load_down.start()
    load_cot.start()
    load_gate_up.start()
    load_att.start()
    load_out.start()
    greet(line_peers(place) + [around.up, around.down, around.beyond])
    load_normed.wait()
    gather.start()
    load_down.wait()
    load_cot.wait()

    @pl.loop(0, 4)
    def _(index):
        rows = pl.ds(pl.multiple_of(index * PAIR, PAIR), PAIR)
        d_hidden[rows, :] = matmul(cot_rows[rows, :], down[...], NT)

    load_gate_up.wait()
    order = (0, 1, 3, 2)

    @pl.loop(0, 4)
    def _(turn):
        step = turn + lax.div(turn, 2) * (5 - 2 * turn)
        for index in range(4):

            @pl.when(turn == index)
            def _(index=index):
                for arrived in ((), (1, 3), (), (2,))[index]:
                    gather.arrive(arrived)
                gather.across[order[index]].wait_recv()

        rows = pl.ds(pl.multiple_of(step * PAIR, PAIR), PAIR)
        gate = matmul(normed[rows, :], gate_up[0], NT)
        up = matmul(normed[rows, :], gate_up[1], NT)
        sigmoid = jax.nn.sigmoid(gate)
        silu = gate * sigmoid
        hidden[rows, :] = (silu * up).astype(bf16)
        d_hid = d_hidden[rows, :]
        d_gate[rows, :] = (d_hid * up * sigmoid * (1.0 + gate * (1.0 - sigmoid))).astype(bf16)
        d_up[rows, :] = (d_hid * silu).astype(bf16)
        for index in (2, 3):

            @pl.when(turn == index)
            def _(index=index):
                second.merge(order[index - 1])

        @pl.loop(0, 2048, step=512)
        def _(column):
            columns = pl.ds(pl.multiple_of(column, 512), 512)
            terms = matmul(d_gate[rows, :], gate_up[0, :, columns], NN) + matmul(
                d_up[rows, :], gate_up[1, :, columns], NN
            )
            terms = terms.astype(bf16)
            own_rows[step, :, columns] = terms[:BLOCK]
            given_terms[step, :, columns] = terms[BLOCK:]

        for index in range(4):

            @pl.when(turn == index)
            def _(index=index):
                second.across[order[index]].start()

    second.merge(2)
    load_att.wait()
    load_out.wait()

    def ffn_terms():
        @pl.loop(0, 4)
        def _(index):
            rows = pl.ds(pl.multiple_of(index * PAIR, PAIR), PAIR)

            @pl.when(index > 0)
            def _():
                pltpu.make_async_copy(ffn_tile, ffn_part.at[rows], ffn_sem).wait()

            @pl.loop(0, 2048, step=512)
            def _(column):
                columns = pl.ds(pl.multiple_of(column, 512), 512)
                ffn_tile[:, columns] = matmul(hidden[rows, :], down[:, columns], NN).astype(bf16)

            pltpu.make_async_copy(ffn_tile, ffn_part.at[rows], ffn_sem).start()

    def weight_grad(target, left, right):
        def stored(tile, slot):
            columns = pl.ds(pl.multiple_of(tile * TILE, TILE), TILE)
            return pltpu.make_async_copy(grad_tile.at[slot], target.at[:, columns], grad_sems.at[slot])

        @pl.loop(0, 8)
        def _(tile):
            slot = lax.rem(tile, 2)

            @pl.when(tile > 1)
            def _():
                stored(tile, slot).wait()

            columns = pl.ds(pl.multiple_of(tile * TILE, TILE), TILE)
            grad_tile[slot] = matmul(left[...], right[:, columns], TN).astype(bf16)
            stored(tile, slot).start()

        for slot in range(2):
            stored(slot, slot).wait()

    weight_grad(gate_grad, d_gate, normed)

    @pl.when(lacking)
    def _():
        over.start()

    weight_grad(down_grad, hidden, cot_rows)
    ring.begin()
    for copy in ring_loads:
        copy.start()
    second.finish()
    gain_part[...] = jnp.zeros_like(gain_part)
    shift_part[...] = jnp.zeros_like(shift_part)

    def back(rows):
        grad = second.rows(rows)
        centre, scale = moments(mid[rows, :])
        unit = centre * scale
        gain_part[...] += jnp.sum(grad * unit, axis=0, keepdims=True)
        shift_part[...] += jnp.sum(grad, axis=0, keepdims=True)
        scaled = grad * gain[...]
        total = cot[rows, :].astype(jnp.float32) + scale * (
            scaled
            - jnp.mean(scaled, axis=-1, keepdims=True)
            - unit * jnp.mean(scaled * unit, axis=-1, keepdims=True)
        )
        d_mid[rows, :] = total
        d_rows[rows, :] = total.astype(bf16)

    tile_rows(back)
    gather_d.start()
    for copy in ring_loads:
        copy.wait()
    ring.merge()
    ffn_terms()
    gather_d.arrive(1)
    gather_d.arrive(3)
    weight_grad(up_grad, d_up, normed)
    gather_d.arrive(2)
    for step in range(SIDE):
        gather_d.across[step].wait_recv()
        terms = matmul(d_rows[pl.ds(step * PAIR, PAIR), :], out[...], NT).astype(bf16)
        behind = turned(x, SIDE - step)
        for other in range(2):
            whose = (1 - core) if other else core
            first_row = pl.multiple_of((whose * SIDE + behind) * BLOCK, BLOCK)
            d_attended[pl.ds(first_row, BLOCK), :] = terms[other * BLOCK : (other + 1) * BLOCK]

    @pl.loop(0, 2048, step=512)
    def _(column):
        columns = pl.ds(pl.multiple_of(column, 512), 512)
        out_grad[:, columns] = matmul(attended[...], d_rows[:, columns], TN).astype(bf16)

    gather.finish()
    gather_d.finish()
    pltpu.make_async_copy(ffn_tile, ffn_part.at[pl.ds(0, PAIR)], ffn_sem).wait()
    ring.sum()
    down_stored = pltpu.make_async_copy(ring.total, down_sum, own_sems.at[0])
    down_stored.start()
    ring.sent()
    down_stored.wait()

    @pl.when(lacking)
    def _():
        over.wait_send()

    @pl.when(jnp.logical_not(lacking))
    def _():
        over.wait_recv()


class Links:
    def __init__(self, sends, arrives):
        self.sends, self.arrives, self.used = sends, arrives, 0

    def to(self, source, target, device_id):
        self.used += 1
        return remote(source, target, self.sends, self.arrives, self.used - 1, device_id)


def each_rows(count, step, body):
    if count == step:
        body(pl.ds(0, count))
        return

    @pl.loop(0, count, step=step)
    def _(row):
        body(pl.ds(pl.multiple_of(row, 16), step))


def add_into(target, *terms, count, step):
    def body(rows):
        total = terms[0](rows).astype(jnp.float32)
        for term in terms[1:]:
            total = total + term(rows).astype(jnp.float32)
        target[rows, :] = total.astype(jnp.bfloat16)

    each_rows(count, step, body)


def of(ref, first=0):
    return lambda rows: ref[pl.ds(rows.start + first, rows.size), :]


class Around:
    def __init__(self, place):
        x, y, z_hi, z_lo, core = place
        self.y, self.z_lo = y, z_lo
        self.up = device(x, turned(y, 1), z_hi, z_lo, core)
        self.down = device(x, turned(y, 3), z_hi, z_lo, core)
        self.beyond = device(x, y, 1 - z_hi, 1 - z_lo, core)
        self.twin = device(x, y, z_hi, 1 - z_lo, core)
        self.partner = device(x, y, z_hi, z_lo, 1 - core)
        self.keeps = core == z_hi
        self.gives = jnp.logical_not(self.keeps)


class RowRing:
    def __init__(self, size, width, step):
        self.size, self.width, self.step = size, width, step
        self.split = -(-size // 32) * 16

    def scratch(self):
        kind = jnp.bfloat16
        return (
            pltpu.VMEM((self.split, self.width), kind),
            pltpu.VMEM((self.size - self.split, self.width), kind),
            pltpu.VMEM((self.size, self.width), kind),
            pltpu.VMEM((self.size, self.width), kind),
            pltpu.VMEM((self.size, self.width), kind),
        )

    def quarter(self, ref, index, first=0):
        return ref.at[pl.ds(pl.multiple_of(first + index * self.size, 16), self.size)]

    def halves(self, ref):
        return ref.at[pl.ds(0, self.split)], ref.at[pl.ds(self.split, self.size - self.split)]

    def bind(self, links, around, scratch, far, up_terms, down_terms, own_terms):
        self.from_below, self.from_above, self.got_up, self.got_down, self.total = scratch
        self.up_terms, self.down_terms, self.own_terms = up_terms, down_terms, own_terms
        first, second = self.halves(far)
        self.first = (
            links.to(first, self.from_below, around.up),
            links.to(second, self.from_above, around.down),
        )
        self.second = (
            links.to(up_terms, self.got_up, around.up),
            links.to(down_terms, self.got_down, around.down),
        )

    def begin(self):
        for copy in self.first:
            copy.start()

    def merge(self):
        self.first[0].wait_recv()
        low, high = self.split, self.size - self.split
        up_low, _ = self.halves(self.up_terms)
        _, down_high = self.halves(self.down_terms)
        add_into(up_low, of(up_low), of(self.from_below), count=low, step=low)
        self.second[0].start()
        self.first[1].wait_recv()
        add_into(down_high, of(down_high), of(self.from_above), count=high, step=high)
        self.second[1].start()

    def sum(self):
        for copy in self.second:
            copy.wait_recv()
        add_into(
            self.total,
            of(self.own_terms),
            of(self.got_up),
            of(self.got_down),
            count=self.size,
            step=self.step,
        )

    def sent(self):
        for copy in (*self.first, *self.second):
            copy.wait_send()


class RowSpread:
    def __init__(self, ring, links, locals_, around, total, full, first=0):
        y = around.y
        mine = ring.quarter(full, y, first)
        below, above = ring.quarter(full, turned(y, 3), first), ring.quarter(full, turned(y, 1), first)
        self.own = locals_.of(total, mine)
        self.direct = (links.to(total, mine, around.up), links.to(total, mine, around.down))
        low, high = ring.halves(below)[0], ring.halves(above)[1]
        self.passed = (links.to(low, low, around.up), links.to(high, high, around.down))

    def begin(self):
        self.own.start()
        for copy in self.direct:
            copy.start()

    def pass_on(self):
        for copy, onward in zip(self.direct, self.passed):
            copy.wait_recv()
            onward.start()

    def end(self):
        self.own.wait()
        for copy in self.passed:
            copy.wait_recv()

    def sent(self):
        for copy in (*self.direct, *self.passed):
            copy.wait_send()


WIDE = 1024
DOWN_RING = (176, 2048, 16)
ATTN_UNITS = ((768, 256, 96, 0), (768, 256, 96, 3072), (64, 2048, 16, 0))
LINK_COUNT, LOCAL_COUNT = 112, 64


def left_ring():
    return RowRing(176, WIDE // 2, 176)


def right_ring():
    return RowRing(176, WIDE, 16)


def left_scratch(rows, count):
    kind = jnp.bfloat16
    half = pltpu.VMEM((rows, WIDE // 2), kind)
    return (pltpu.VMEM((rows, WIDE), kind),) * 3 + ((half,) + left_ring().scratch()) * count


def right_scratch(count):
    return (pltpu.VMEM((176, WIDE), jnp.bfloat16),) * (4 * count)


def attn_scratch():
    found = ()
    for size, width, step, _ in ATTN_UNITS:
        ring = RowRing(size, width, step)
        found += (pltpu.VMEM((size, width), jnp.bfloat16),) * 2 + ring.scratch()
    return found


def left_sum(part, beyond, full, column, fetch, links, locals_, around, mine, got, scratch):
    half = scratch[0]
    rows, width = got.shape[0], WIDE // 2
    ring = left_ring()
    side = lambda z_lo: pl.ds(pl.multiple_of(z_lo * width, 128), width)
    columns = pl.ds(column, WIDE)
    stretch = full.at[:, columns]
    own_side = full.at[:, pl.ds(pl.multiple_of(column + around.z_lo * width, 128), width)]
    loads = (locals_.of(part.at[:, columns], mine), locals_.of(beyond.at[:, columns], got))
    if fetch:
        over = links.to(part.at[:, columns], beyond.at[:, columns], around.beyond)
    kept, sent_on = side(around.z_lo), side(1 - around.z_lo)
    twin = links.to(got.at[:, sent_on], half, around.twin)
    quarter = lambda k: ring.quarter(half, turned(around.y, k))
    ring.bind(links, around, scratch[1:], quarter(2), quarter(1), quarter(3), quarter(0))
    spread = RowSpread(ring, links, locals_, around, ring.total, own_side)
    both = links.to(own_side, own_side, around.twin)
    core = links.to(stretch, stretch, around.partner)

    if fetch:

        @pl.when(around.gives)
        def _():
            over.start()

        yield

    @pl.when(around.keeps)
    def _():
        if fetch:
            over.wait_recv()
        for copy in loads:
            copy.start()

    yield

    @pl.when(around.keeps)
    def _():
        for copy in loads:
            copy.wait()
        add_into(got, of(got), of(mine), count=rows, step=64)
        twin.start()

    yield

    @pl.when(around.keeps)
    def _():
        twin.wait_recv()
        add_into(half, of(half), lambda rows: got[rows, kept], count=rows, step=64)
        ring.begin()
        twin.wait_send()

    yield

    @pl.when(around.keeps)
    def _():
        ring.merge()

    yield

    @pl.when(around.keeps)
    def _():
        ring.sum()
        spread.begin()

    yield

    @pl.when(around.keeps)
    def _():
        spread.pass_on()

    yield

    @pl.when(around.keeps)
    def _():
        spread.end()
        both.start()

    yield

    @pl.when(around.keeps)
    def _():
        both.wait_recv()
        core.start()

    yield

    @pl.when(around.keeps)
    def _():
        ring.sent()
        spread.sent()
        both.wait_send()
        core.wait_send()

    @pl.when(around.gives)
    def _():
        if fetch:
            over.wait_send()
        core.wait_recv()

    yield


def across_and_back(ring, total, spare, from_beyond, from_twin, full, first, links, locals_, around):
    over = links.to(total, from_beyond, around.beyond)
    twin = links.to(total, from_twin, around.twin)
    spread = RowSpread(ring, links, locals_, around, spare, full, first)
    span = full.at[pl.ds(first, SIDE * ring.size)]
    core = links.to(span, span, around.partner)

    @pl.when(around.gives)
    def _():
        over.start()

    yield

    @pl.when(around.keeps)
    def _():
        over.wait_recv()
        add_into(total, of(total), of(from_beyond), count=ring.size, step=ring.step)
        twin.start()

    yield

    @pl.when(around.keeps)
    def _():
        twin.wait_recv()
        add_into(spare, of(total), of(from_twin), count=ring.size, step=ring.step)
        spread.begin()

    yield

    @pl.when(around.keeps)
    def _():
        spread.pass_on()

    yield

    @pl.when(around.keeps)
    def _():
        spread.end()
        core.start()

    yield

    @pl.when(around.keeps)
    def _():
        twin.wait_send()
        spread.sent()
        core.wait_send()

    @pl.when(around.gives)
    def _():
        over.wait_send()
        core.wait_recv()

    yield


def right_sum(summed, full, unit, links, locals_, around, scratch):
    stretch = full.at[:, pl.ds(unit, WIDE)]
    total, spare, from_beyond, from_twin = scratch
    ring = right_ring()
    load = locals_.of(summed.at[:, pl.ds(unit, WIDE)], total)
    load.start()
    yield
    load.wait()
    yield from across_and_back(
        ring, total, spare, from_beyond, from_twin, stretch, 0, links, locals_, around
    )


def attn_sum(part, full, unit, links, locals_, around, held_terms, scratch):
    own_terms, up_terms, down_terms = held_terms
    from_beyond, from_twin = scratch[:2]
    *sizes, first = unit
    ring = RowRing(*sizes)
    quarter = lambda k: ring.quarter(part, turned(around.y, k), first)
    loads = [
        locals_.of(quarter(k), held) for k, held in ((1, up_terms), (3, down_terms), (0, own_terms))
    ]
    ring.bind(links, around, scratch[2:], quarter(2), up_terms, down_terms, own_terms)
    ring.begin()
    for copy in loads:
        copy.start()
    yield
    for copy in loads:
        copy.wait()
    ring.merge()
    yield
    ring.sum()
    yield from across_and_back(
        ring, ring.total, own_terms, from_beyond, from_twin, full, first, links, locals_, around
    )
    ring.sent()
    yield


def sum_everywhere(values, places, links, place):
    x, y, z_hi, z_lo, core = place
    by_x, by_core, by_y, by_z = places
    z = z_hi * 2 + z_lo
    rounds = (
        (by_x, x, [device(turned(x, k), y, z_hi, z_lo, core) for k in (1, 2, 3)]),
        (by_core, core, [device(x, y, z_hi, z_lo, 1 - core)]),
        (by_y, y, [device(x, turned(y, k), z_hi, z_lo, core) for k in (1, 2, 3)]),
        (by_z, z, [z_device(x, y, turned(z, k), core) for k in (1, 2, 3)]),
    )
    for slots, mine, peers in rounds:
        slots[mine] = values[...]
        copies = [links.to(slots.at[mine], slots.at[mine], peer) for peer in peers]
        for copy in copies:
            copy.start()
        yield
        for copy in copies:
            copy.wait()
        total = slots[0]
        for slot in range(1, slots.shape[0]):
            total = total + slots[slot]
        values[...] = total
    yield


def z_device(x, y, z, core):
    return device(x, y, lax.div(z, 2), lax.rem(z, 2), core)


def attention_back(
    queries, keys, values, d_attended, row_info, segment_row, turns, qkv, d_keys, d_values, d_proj, d_normed, score_scale
):
    bf16, f32 = jnp.bfloat16, jnp.float32
    keep, from_after, from_before = turns
    lane = lax.broadcasted_iota(jnp.int32, (1, 128), 1)
    d_keys[...] = jnp.zeros_like(d_keys)
    d_values[...] = jnp.zeros_like(d_values)

    def turned_back(grads, rows):
        return (
            grads * keep[rows, :]
            + pltpu.roll(grads, 120, 1) * from_after[rows, :]
            + pltpu.roll(grads, 8, 1) * from_before[rows, :]
        )

    for block in (3, 2, 1, 0):
        first, end = block * PAIR, (block + 1) * PAIR
        rows, before = pl.ds(first, PAIR), pl.ds(0, end)
        info = row_info[rows, :]
        places = first + lax.broadcasted_iota(jnp.int32, (PAIR, end), 0)
        allowed = (info[:, 4:5] == segment_row[:, 0:end]) & (
            lax.broadcasted_iota(jnp.int32, (PAIR, end), 1) <= places
        )
        info_lane = lax.broadcasted_iota(jnp.int32, info.shape, 1)

        @pl.loop(0, 2)
        def _(pair):
            lanes = pl.ds(pl.multiple_of(pair * 128, 128), 128)
            query, grad = queries[rows, lanes], d_attended[rows, lanes]
            key, value = keys[before, lanes], values[before, lanes]
            d_query = jnp.zeros((PAIR, 128), f32)
            for head in range(2):
                inside = (lane >= head * HEAD_DIM) & (lane < (head + 1) * HEAD_DIM)
                query_h = jnp.where(inside, query, jnp.zeros_like(query))
                grad_h = jnp.where(inside, grad, jnp.zeros_like(grad))
                key_h = jnp.where(inside, key, jnp.zeros_like(key))
                log_norm = jnp.sum(
                    jnp.where(info_lane == pair * 2 + head, info, 0.0), axis=1, keepdims=True
                )
                scores = jnp.where(allowed, matmul(query_h, key, NT) * score_scale, -1e30)
                prob = jnp.exp(scores - log_norm)
                d_prob = matmul(grad_h, value, NT)
                row_dots = jnp.sum(prob * d_prob, axis=1, keepdims=True)
                d_score = (prob * (d_prob - row_dots)).astype(bf16)
                d_query = d_query + matmul(d_score, key_h, NN)
                d_keys[before, lanes] += matmul(d_score, query_h, TN)
                d_values[before, lanes] += matmul(prob.astype(bf16), grad_h, TN)
            d_proj[rows, lanes] = turned_back(d_query * score_scale, rows).astype(bf16)
            key_lanes = pl.ds(pl.multiple_of(256 + pair * 128, 128), 128)
            d_proj[rows, key_lanes] = turned_back(d_keys[rows, lanes] * score_scale, rows).astype(bf16)
            value_lanes = pl.ds(pl.multiple_of(512 + pair * 128, 128), 128)
            d_proj[rows, value_lanes] = d_values[rows, lanes].astype(bf16)

        @pl.loop(0, 2048, step=512)
        def _(column):
            columns = pl.ds(pl.multiple_of(column, 512), 512)
            total = matmul(d_proj[rows, 0:256], qkv[0, columns, :], NT)
            total = total + matmul(d_proj[rows, 256:512], qkv[1, columns, :], NT)
            total = total + matmul(d_proj[rows, 512:768], qkv[2, columns, :], NT)
            d_normed[rows, columns] = total.astype(bf16)

        yield


ORDER = (
    "l3", "l0", "f", "l2", "a2", "r0", "r1", "l0", "l1", "f", "l1", "f", "l0", "f",
    "l1", "l0", "f", "l1", "l2", "l0", "a2", "l2", "l3", "f", "l3", "l1", "l0", "f",
    "a0", "a1", "l1", "l2", "f", "l0", "l3", "a2", "r0", "f", "r1", "a0", "f", "a1",
    "l1", "l2", "a2", "l3", "r0", "l0", "r1", "a0", "l0", "l1", "a2", "a0", "a1", "l1",
    "l2", "r0", "l3", "f", "r1", "e", "a1", "l2", "a2", "f", "a0", "r0", "e", "l3",
    "e", "a1", "r1", "l2", "a2", "a2", "a0", "r0", "l3", "e", "r0", "a1", "l2", "r1",
    "a0", "l2", "a1", "r1", "l3", "a0", "e", "a1", "l3",
)


def last_kernel(
    queries_in,
    keys_in,
    values_in,
    d_attended_in,
    row_info,
    segment_row,
    keep,
    from_after,
    from_before,
    qkv,
    normed,
    tokens,
    d_mid,
    gain,
    ffn_part,
    mid,
    gate_part,
    gate_beyond,
    up_part,
    down_sum,
    out_part,
    gain_part,
    shift_part,
    mixed,
    input_grad,
    gate_full,
    up_full,
    down_full,
    qkv_full,
    out_full,
    sums,
    up_beyond,
    qkv_part,
    queries,
    keys,
    values,
    d_attended,
    d_keys,
    d_values,
    d_proj,
    d_normed,
    normed_tile,
    grad_tile,
    d_in,
    mixed_rows,
    ffn_rows,
    normed_sems,
    grad_sems,
    ready,
    sends,
    arrives,
    local_sems,
    by_x,
    by_core,
    by_y,
    by_z,
    *scratch,
):
    bf16 = jnp.bfloat16
    place = here()
    x, y, z_hi, z_lo, core = place
    z = z_hi * 2 + z_lo
    around = Around(place)
    links, locals_ = Links(sends, arrives), Locals(local_sems)
    swap_with = device(x, y, core, z_lo, z_hi)
    terms, ffn_terms = ByRow(d_normed, place), ByStep(ffn_part)

    def own_terms(step, rows):
        first = (core * SIDE + turned(x, SIDE - step)) * BLOCK
        return d_normed[pl.ds(pl.multiple_of(first + rows.start, 16), rows.size), :]

    scatter_ffn = Scatter(
        lambda step, rows: ffn_rows[step, rows, :], lambda step: ffn_terms.at(step, 1), place, scratch[:7]
    )
    scatter = Scatter(own_terms, lambda step: terms.at(step, 1), place, scratch[:3] + scratch[7:11])
    scratch = scratch[11:]
    units = {}
    mine, *got = scratch[:3]
    scratch = scratch[3:]
    refs_of = ((gate_part, gate_beyond, gate_full), (up_part, up_beyond, up_full))
    for index in range(4):
        units[f"l{index}"] = left_sum(
            *refs_of[index // 2],
            (index % 2) * WIDE,
            index > 1,
            links,
            locals_,
            around,
            mine,
            got[index % 2],
            scratch[:6],
        )
        scratch = scratch[6:]
    for index in range(2):
        units[f"r{index}"] = right_sum(down_sum, down_full, index * WIDE, links, locals_, around, scratch[:4])
        scratch = scratch[4:]
    out_terms, scratch = scratch[:3], scratch[3:]
    held_terms = (
        [ref.at[pl.ds(0, 768)] for ref in (queries, keys, values)],
        [d_proj.at[pl.ds(0, 768), pl.ds(256 * index, 256)] for index in range(3)],
        out_terms,
    )
    for index, unit in enumerate(ATTN_UNITS):
        refs = (out_part, out_full) if index == 2 else (qkv_part, qkv_full)
        units[f"a{index}"] = attn_sum(*refs, unit, links, locals_, around, held_terms[index], scratch[:7])
        scratch = scratch[7:]
    units["e"] = sum_everywhere(sums, (by_x, by_core, by_y, by_z), links, place)
    units["t"] = attention_back(
        queries,
        keys,
        values,
        d_attended,
        row_info,
        segment_row,
        (keep, from_after, from_before),
        qkv,
        d_keys,
        d_values,
        d_proj,
        d_normed,
        HEAD_DIM ** (-0.5),
    )

    def on(*names):
        for name in names:
            next(units[name])

    load_attn = [
        locals_.of(source, held)
        for source, held in (
            (queries_in, queries),
            (keys_in, keys),
            (values_in, values),
            (d_attended_in, d_attended),
        )
    ]
    load_ffn = [locals_.of(ffn_terms.at(step, 0), ffn_rows.at[step]) for step in range(SIDE)]
    swaps = [links.to(mixed_rows, mixed, swap_with), links.to(d_in, input_grad, swap_with)]
    stays = [locals_.of(mixed_rows, mixed), locals_.of(d_in, input_grad)]

    def give(index):
        @pl.when(around.gives)
        def _():
            swaps[index].start()

        @pl.when(around.keeps)
        def _():
            stays[index].start()

    def load_normed(chunk):
        columns = pl.ds(pl.multiple_of(chunk * TILE, TILE), TILE)
        slot = lax.rem(chunk, 2)
        return pltpu.make_async_copy(normed.at[:, columns], normed_tile.at[slot], normed_sems.at[slot])

    def store_grad(chunk):
        slot = lax.rem(chunk, 2)
        return [
            pltpu.make_async_copy(
                grad_tile.at[slot, pl.ds(channel * TILE, TILE)],
                qkv_part.at[pl.ds(pl.multiple_of(channel * 2048 + chunk * TILE, TILE), TILE)],
                grad_sems.at[slot, channel],
            )
            for channel in range(3)
        ]

    def qkv_grads(first, end):
        @pl.loop(first, end)
        def _(chunk):
            slot = lax.rem(chunk, 2)
            load_normed(chunk).wait()

            @pl.when(chunk + 1 < 8)
            def _():
                load_normed(chunk + 1).start()

            @pl.when(chunk > first + 1)
            def _():
                for copy in store_grad(chunk):
                    copy.wait()

            grads = matmul(normed_tile[slot], d_proj[...], TN).astype(bf16)
            for channel in range(3):
                grad_tile[slot, channel * TILE : (channel + 1) * TILE, :] = grads[
                    :, channel * TILE : (channel + 1) * TILE
                ]
            for copy in store_grad(chunk):
                copy.start()

        for chunk in (end - 2, end - 1):
            for copy in store_grad(jnp.int32(chunk)):
                copy.wait()

    for copy in load_ffn + load_attn:
        copy.start()
    load_normed(jnp.int32(0)).start()
    peers = line_peers(place) + [device(x, turned(y, k), z_hi, z_lo, core) for k in (1, 2, 3)]
    peers += [z_device(x, y, turned(z, k), core) for k in (1, 2, 3)]

    @pl.when(around.gives)
    def _():
        greet(peers + [swap_with])

    @pl.when(around.keeps)
    def _():
        greet(peers)

    def mix(rows):
        mixed_rows[rows, :] = (mid[rows, :] + scatter_ffn.rows(rows)).astype(bf16)

    def bias_grads():
        width = d_proj.shape[1] // 3
        mine_columns = pl.ds(pl.multiple_of((core * SIDE + x) * width, width), width)
        for channel in range(3):
            grads = d_proj[:, channel * width : (channel + 1) * width].astype(jnp.float32)
            sums[4 + channel : 5 + channel, mine_columns] = jnp.sum(grads, axis=0, keepdims=True)

    def back(rows):
        grad = scatter.rows(rows)
        centre, scale = moments(tokens[rows, :].astype(jnp.float32))
        unit = centre * scale
        sums[0:1, :] += jnp.sum(grad * unit, axis=0, keepdims=True)
        sums[1:2, :] += jnp.sum(grad, axis=0, keepdims=True)
        scaled = grad * gain[...]
        d_in[rows, :] = d_mid[rows, :] + scale * (
            scaled
            - jnp.mean(scaled, axis=-1, keepdims=True)
            - unit * jnp.mean(scaled * unit, axis=-1, keepdims=True)
        )

    def foreground():
        for step in (2, 1, 3, 0):
            scatter_ffn.across[step].start()
        yield
        for copy in load_ffn:
            copy.wait()
        for step in (2, 1, 3):
            scatter_ffn.merge(step)
        yield
        for copy in load_attn:
            copy.wait()
        sums[...] = jnp.zeros_like(sums)
        sums[2:3, :] = gain_part[...]
        sums[3:4, :] = shift_part[...]
        on("t")
        yield
        on("t")
        yield
        on("t")
        yield
        on("t")
        yield
        qkv_grads(0, 8)
        bias_grads()
        yield
        scatter_ffn.finish()
        tile_rows(mix)
        for peer in line_peers(place):
            pl.semaphore_signal(ready, inc=1, device_id=peer, device_id_type=MESH)
        give(0)
        yield
        pl.semaphore_wait(ready, SIDE)
        for step in (2, 1, 3, 0):
            scatter.across[step].start()
        yield
        for step in (2, 1, 3):
            scatter.merge(step)
        yield
        scatter.finish()
        tile_rows(back)
        yield
        give(1)
        yield

    units["f"] = foreground()
    on(*ORDER)
    for unit in units.values():
        for _ in unit:
            pass

    @pl.when(around.gives)
    def _():
        for copy in swaps:
            copy.wait()

    @pl.when(around.keeps)
    def _():
        for copy in stays:
            copy.wait()


ANY = pl.BlockSpec(memory_space=pl.ANY)
HELD = pl.BlockSpec(memory_space=pltpu.VMEM)


def call(kernel, collective_id, args, in_specs, outs, out_specs, scratch):
    return pl.pallas_call(
        kernel,
        out_shape=[jax.ShapeDtypeStruct(shape, kind) for shape, kind in outs],
        in_specs=in_specs,
        out_specs=out_specs,
        scratch_shapes=list(scratch),
        compiler_params=pltpu.CompilerParams(
            collective_id=collective_id, has_side_effects=True, vmem_limit_bytes=VMEM_LIMIT
        ),
    )(*args)


def member_layout(seq_length, seq_owner, member, row_total):
    entry_total = seq_length.shape[0]
    row_ids = jnp.arange(row_total, dtype=jnp.int32)
    entry_ids = jnp.arange(entry_total, dtype=jnp.int32)
    earlier = (entry_ids[:, None] < entry_ids[None, :]).astype(jnp.int32)
    sharing = (seq_owner[:, None] == seq_owner[None, :]).astype(jnp.int32)
    starts = jnp.sum(seq_length[:, None] * sharing * earlier, axis=0)
    owned_now = (seq_owner == member).astype(jnp.int32)
    inside = (
        owned_now[None, :]
        * (row_ids[:, None] >= starts[None, :]).astype(jnp.int32)
        * (row_ids[:, None] < (starts + seq_length)[None, :]).astype(jnp.int32)
    )
    live_rows = jnp.sum(inside, axis=1)
    segment = jnp.sum(inside * entry_ids[None, :], axis=1) + (1 - live_rows) * (
        entry_total + row_ids
    )
    position = jnp.sum(inside * (row_ids[:, None] - starts[None, :]), axis=1)
    return (segment, position, live_rows)


def rotary_tables(position):
    half_rot = ROT // 2
    frequency = jnp.power(
        jnp.float32(10000.0), -2.0 * jnp.arange(half_rot, dtype=jnp.float32) / ROT
    )
    lane = jnp.arange(128) % HEAD_DIM
    frequency = jnp.where(lane < ROT, jnp.tile(frequency, 128 // half_rot), 0.0)
    angles = position.astype(jnp.float32)[:, None] * frequency[None, :]
    sine = jnp.sin(angles)
    from_after = jnp.where(lane < half_rot, sine, 0.0)
    from_before = jnp.where(lane >= half_rot, -sine, 0.0)
    return (jnp.cos(angles), from_after, from_before)


def body(
    tokens,
    seq_length,
    seq_owner,
    ln1_gain,
    ln1_bias,
    qkv_weight,
    qkv_bias,
    out_weight,
    ln2_gain,
    ln2_bias,
    gate_up_weight,
    down_weight,
    out_grad,
):
    bf16, f32 = jnp.bfloat16, jnp.float32
    x, y, z_hi, z_lo, core = here()
    row_total = BLOCK * 8
    rows_here, rows_all = (BLOCK, 2048), (row_total, 2048)
    local_heads = qkv_weight.shape[2] // HEAD_DIM
    member = (y * 2 + z_lo) * 2 + z_hi
    shard = core * SIDE + x
    segment, position, live_rows = member_layout(seq_length, seq_owner, member, row_total)
    live = lax.dynamic_slice_in_dim(live_rows, shard * BLOCK, BLOCK, 0)[:, None].astype(f32)
    segments = segment.astype(f32)[:, None]
    segment_row = segment.astype(f32)[None]
    keep, from_after, from_before = rotary_tables(position)
    flat = (row_total, qkv_weight.shape[2])
    dma, vmem = pltpu.SemaphoreType.DMA, pltpu.VMEM
    gate_up_t = jnp.swapaxes(gate_up_weight, 1, 2)
    (
        tokens_here,
        cot,
        normed1,
        cot_rows,
        mid_stream,
        normed2,
        qkv,
        out,
        down,
        gate_up,
        queries,
        keys,
        values,
        attended,
        row_info,
    ) = call(
        first_kernel,
        1,
        (
            tokens,
            out_grad,
            live,
            ln1_gain[None],
            ln1_bias[None],
            qkv_weight,
            out_weight,
            down_weight,
            gate_up_t,
            ln2_gain[None],
            ln2_bias[None],
            qkv_bias,
            segments,
            segment_row,
            keep,
            from_after,
            from_before,
        ),
        [ANY, ANY, HELD, HELD, HELD, ANY, ANY, ANY, ANY] + [HELD] * 8,
        [
            (rows_here, bf16),
            (rows_here, bf16),
            (rows_all, bf16),
            (rows_all, bf16),
            (rows_here, f32),
            (rows_here, bf16),
            (qkv_weight.shape, bf16),
            (out_weight.shape, bf16),
            (down_weight.shape, bf16),
            (gate_up_t.shape, bf16),
            (flat, bf16),
            (flat, bf16),
            (flat, bf16),
            (flat, bf16),
            ((row_total, 128), f32),
        ],
        [ANY] * 4 + [HELD] * 11,
        (
            vmem(rows_here, bf16),
            vmem(rows_here, bf16),
            vmem(rows_here, bf16),
            vmem(qkv_bias.shape, f32),
            vmem(rows_all, bf16),
            vmem(rows_all, bf16),
            dma((3,)),
            dma((3,)),
            dma((16,)),
        )
        + Gather.scratch * 2
        + fetch_scratch(5)
        + Scatter.scratch,
    )

    ff = down_weight.shape[0]
    d_mid, gain2_part, shift2_part, *ff_parts, ffn_part, d_attended, out_grad = call(
        middle_kernel,
        2,
        (
            normed2,
            mid_stream,
            ln2_gain[None],
            gate_up,
            down,
            cot_rows,
            attended,
            out,
            cot,
        ),
        [ANY, HELD, HELD, ANY, ANY, ANY, ANY, ANY, HELD],
        [
            (rows_here, f32),
            ((1, 2048), f32),
            ((1, 2048), f32),
            (down_weight.shape, bf16),
            (down_weight.shape, bf16),
            (down_weight.shape, bf16),
            (down_weight.shape, bf16),
            ((ff // SIDE, 2048), bf16),
            (rows_all, bf16),
            (attended.shape, bf16),
            (out.shape, bf16),
        ],
        [HELD] * 3 + [ANY] * 6 + [HELD, HELD],
        (
            vmem((2, ff, 2048), bf16),
            vmem((ff, 2048), bf16),
            vmem(out.shape, bf16),
            vmem(rows_all, bf16),
            vmem(rows_all, bf16),
            vmem(rows_all, bf16),
            vmem(attended.shape, bf16),
            vmem((row_total, ff), bf16),
            vmem((row_total, ff), bf16),
            vmem((row_total, ff), bf16),
            vmem((row_total, ff), f32),
            vmem((SIDE, BLOCK, 2048), bf16),
            vmem((SIDE, BLOCK, 2048), bf16),
            vmem((PAIR, 2048), bf16),
            vmem((2, ff, TILE), bf16),
            dma((8,)),
            dma((8,)),
            dma((6,)),
            dma,
            dma((2,)),
        )
        + Scatter.scratch
        + Gather.scratch * 2
        + (dma((5,)), dma((5,)))
        + (vmem((ff // SIDE, 2048), bf16),) * 3
        + RowRing(*DOWN_RING).scratch(),
    )

    gate_part, up_part, _, gate_beyond, down_sum = ff_parts
    small = (8, 2048)
    qkv_rows = (3 * 2048, flat[1])
    mixed, input_grad, gate_full, up_full, down_full, qkv_full, out_full, sums, _, _ = call(
        last_kernel,
        4,
        (
            queries,
            keys,
            values,
            d_attended,
            row_info,
            segment_row,
            keep,
            from_after,
            from_before,
            qkv,
            normed1,
            tokens_here,
            d_mid,
            ln1_gain[None],
            ffn_part,
            mid_stream,
            gate_part,
            gate_beyond,
            up_part,
            down_sum,
            out_grad,
            gain2_part,
            shift2_part,
        ),
        [ANY] * 4 + [HELD] * 6 + [ANY] + [HELD] * 3 + [ANY, HELD] + [ANY] * 5 + [HELD] * 2,
        [
            (rows_here, bf16),
            (rows_here, f32),
            (down_weight.shape, bf16),
            (down_weight.shape, bf16),
            (down_weight.shape, bf16),
            (qkv_rows, bf16),
            (out.shape, bf16),
            (small, f32),
            (down_weight.shape, bf16),
            (qkv_rows, bf16),
        ],
        [ANY] * 7 + [HELD] + [ANY] * 2,
        (
            vmem(flat, bf16),
            vmem(flat, bf16),
            vmem(flat, bf16),
            vmem(flat, bf16),
            vmem(flat, f32),
            vmem(flat, f32),
            vmem((row_total, 3 * flat[1]), bf16),
            vmem(rows_all, bf16),
            vmem((2, row_total, TILE), bf16),
            vmem((2, 3 * TILE, flat[1]), bf16),
            vmem(rows_here, f32),
            vmem(rows_here, bf16),
            vmem((SIDE, BLOCK, 2048), bf16),
            dma((2,)),
            dma((2, 3)),
            pltpu.SemaphoreType.REGULAR,
            dma((LINK_COUNT,)),
            dma((LINK_COUNT,)),
            dma((LOCAL_COUNT,)),
            vmem((SIDE, *small), f32),
            vmem((2, *small), f32),
            vmem((SIDE, *small), f32),
            vmem((SIDE, *small), f32),
        )
        + Scatter.scratch
        + Scatter.sems
        + left_scratch(ff, 4)
        + right_scratch(2)
        + (vmem((64, 2048), bf16),) * 3
        + attn_scratch(),
    )
    gate_up_grad = jnp.swapaxes(jnp.stack([gate_full.astype(f32), up_full.astype(f32)]), 1, 2)
    down_grad = down_full.astype(f32)
    qkv_weight_grad = qkv_full.reshape(3, 2048, -1).astype(f32)
    out_weight_grad = out_full.astype(f32)
    width = qkv_bias.shape[1]
    qkv_bias_grad = lax.dynamic_slice_in_dim(sums[4:7], (z_hi * SIDE + x) * width, width, 1)
    return (
        mixed,
        input_grad,
        sums[0],
        sums[1],
        qkv_weight_grad,
        qkv_bias_grad,
        out_weight_grad,
        sums[2],
        sums[3],
        gate_up_grad,
        down_grad,
    )


def solution(mesh):
    placed = (
        P(("dp", "tensor"), None),
        P(),
        P(),
        P(),
        P(),
        P(None, None, "tensor"),
        P(None, "tensor"),
        P("tensor", None),
        P(),
        P(),
        P(None, None, "tensor"),
        P("tensor", None),
        P(("dp", "tensor"), None),
    )
    return jax.shard_map(
        body,
        mesh=mesh,
        in_specs=placed,
        out_specs=(
            P(("dp", "tensor"), None),
            P(("dp", "tensor"), None),
            P(),
            P(),
            P(None, None, "tensor"),
            P(None, "tensor"),
            P("tensor", None),
            P(),
            P(),
            P(None, None, "tensor"),
            P("tensor", None),
        ),
        check_vma=False,
    )
```

```python
import functools

import jax
import jax.numpy as jnp
from jax import lax
from jax.experimental import pallas as pl
from jax.experimental.pallas import tpu as pltpu
from jax.sharding import PartitionSpec as P

HEAD_DIM = 64
ROT = 16
SIDE = 4
BLOCK = 128
SEQUENCES = 64
AXES = ("dp", "tensor")
MESH = pl.DeviceIdType.MESH
VMEM_LIMIT = 54 * 2**20


def here():
    dp, tensor = lax.axis_index("dp"), lax.axis_index("tensor")
    x, z_hi = lax.rem(tensor, SIDE), lax.div(tensor, SIDE)
    y, z_lo, core = lax.div(dp, SIDE), lax.rem(lax.div(dp, 2), 2), lax.rem(dp, 2)
    return x, y, z_hi, z_lo, core


def device(x, y, z_hi, z_lo, core):
    return ((y * 2 + z_lo) * 2 + core, z_hi * SIDE + x)


def turned(value, by):
    return lax.rem(value + by, SIDE)


def pairs(move):
    found = []
    for dp in range(16):
        for tensor in range(8):
            goal = move(tensor % 4, dp // 4, tensor // 4, (dp // 2) % 2, dp % 2)
            if goal is not None:
                to_dp, to_tensor = device(*goal)
                found.append((dp * 8 + tensor, to_dp * 8 + to_tensor))
    return found


def permute(array, move):
    return lax.ppermute(array, AXES, pairs(move))


def swap_rows(x, y, z_hi, z_lo, core):
    return (x, y, core, z_lo, z_hi)


def remote(source, target, sends, arrives, index, device_id):
    return pltpu.make_async_remote_copy(
        src_ref=source,
        dst_ref=target,
        send_sem=sends.at[index],
        recv_sem=arrives.at[index],
        device_id=device_id,
        device_id_type=MESH,
    )


def greet(peers):
    barrier = pltpu.get_barrier_semaphore()
    for peer in peers:
        pl.semaphore_signal(barrier, inc=1, device_id=peer, device_id_type=MESH)
    pl.semaphore_wait(barrier, len(peers))


def line_peers(place):
    x, y, z_hi, z_lo, core = place
    found = [device(turned(x, k), y, z_hi, z_lo, core) for k in (1, 2, 3)]
    return found + [device(x, y, z_hi, z_lo, 1 - core)]


def row_block(full, core, x):
    return full.at[pl.ds(pl.multiple_of((core * SIDE + x) * BLOCK, BLOCK), BLOCK)]


class ByRow:
    def __init__(self, full, place):
        self.full, self.x, self.core = full, place[0], place[4]

    def at(self, step, other):
        core = 1 - self.core if other else self.core
        return row_block(self.full, core, turned(self.x, SIDE - step))

    def landing(self, step, other, by, across):
        return self.at(step, other)


class ByStep:
    def __init__(self, full):
        self.full = full

    def at(self, step, other):
        return self.full.at[pl.ds((step * 2 + other) * BLOCK, BLOCK)]

    def landing(self, step, other, by, across):
        return self.at((step + by) % SIDE, 1 - other if across else other)


class Gather:
    scratch = (
        pltpu.SemaphoreType.DMA((4,)),
        pltpu.SemaphoreType.DMA((4,)),
        pltpu.SemaphoreType.DMA((4,)),
        pltpu.SemaphoreType.DMA((4,)),
    )

    def __init__(self, block, layout, place, sems):
        x, y, z_hi, z_lo, core = place
        x_send, x_arrive, core_send, core_arrive = sems
        half = BLOCK // 2
        right = device(turned(x, 1), y, z_hi, z_lo, core)
        left = device(turned(x, 3), y, z_hi, z_lo, core)
        partner = device(x, y, z_hi, z_lo, 1 - core)

        def passed(step, first, by, index, to):
            part = pl.ds(first, half)
            return remote(
                layout.at(step, 0).at[part],
                layout.landing(step, 0, by, False).at[part],
                x_send,
                x_arrive,
                index,
                to,
            )

        self.right = remote(block, layout.landing(0, 0, 1, False), x_send, x_arrive, 0, right)
        self.left = remote(block, layout.landing(0, 0, 3, False), x_send, x_arrive, 1, left)
        self.right_on = passed(1, 0, 1, 2, right)
        self.left_on = passed(3, half, 3, 3, left)
        self.across = [
            remote(
                block if step == 0 else layout.at(step, 0),
                layout.landing(step, 0, 0, True),
                core_send,
                core_arrive,
                step,
                partner,
            )
            for step in range(SIDE)
        ]

    def start(self):
        self.right.start()
        self.left.start()
        self.across[0].start()

    def arrive(self, step):
        if step == 1:
            self.right.wait_recv()
            self.right_on.start()
        elif step == 3:
            self.left.wait_recv()
            self.left_on.start()
        else:
            self.right_on.wait_recv()
            self.left_on.wait_recv()
        self.across[step].start()

    def finish(self):
        for copy in (self.right, self.left, self.right_on, self.left_on, *self.across):
            copy.wait_send()

    def take(self):
        for copy in self.across:
            copy.wait_recv()


class Scatter:
    buffers = (
        pltpu.VMEM((SIDE, BLOCK, 2048), jnp.bfloat16),
        pltpu.VMEM((3, BLOCK, 2048), jnp.bfloat16),
        pltpu.VMEM((3, BLOCK, 2048), jnp.bfloat16),
    )
    sems = (
        pltpu.SemaphoreType.DMA((SIDE,)),
        pltpu.SemaphoreType.DMA((SIDE,)),
        pltpu.SemaphoreType.DMA((3,)),
        pltpu.SemaphoreType.DMA((3,)),
    )
    scratch = buffers + sems

    def __init__(self, own, given, place, scratch):
        x, y, z_hi, z_lo, core = place
        self.own, (self.other, self.leaving, self.arrived) = own, scratch[:3]
        core_send, core_arrive, x_send, x_arrive = scratch[3:]
        partner = device(x, y, z_hi, z_lo, 1 - core)
        self.across = [
            remote(given(step), self.other.at[step], core_send, core_arrive, step, partner)
            for step in range(SIDE)
        ]
        self.along = [
            remote(
                self.leaving.at[step - 1],
                self.arrived.at[step - 1],
                x_send,
                x_arrive,
                step - 1,
                device(turned(x, SIDE - step), y, z_hi, z_lo, core),
            )
            for step in (1, 2, 3)
        ]

    def merge(self, step):
        self.across[step].wait_recv()

        def add(rows):
            both = self.own(step, rows).astype(jnp.float32) + self.other[step, rows, :].astype(jnp.float32)
            self.leaving[step - 1, rows, :] = both.astype(jnp.bfloat16)

        tile_rows(add)
        self.along[step - 1].start()

    def finish(self):
        self.across[0].wait_recv()
        for copy in self.along:
            copy.wait()
        for copy in self.across:
            copy.wait_send()

    def rows(self, rows):
        total = self.own(0, rows).astype(jnp.float32) + self.other[0, rows, :].astype(jnp.float32)
        for step in range(3):
            total = total + self.arrived[step, rows, :].astype(jnp.float32)
        return total


class Loaded:
    def __init__(self, full, held, place, sems):
        there, here_ = ByRow(full, place), ByStep(held)
        self.copies = [
            pltpu.make_async_copy(there.at(step, other), here_.at(step, other), sems.at[step * 2 + other])
            for step in range(SIDE)
            for other in range(2)
        ]

    def start(self):
        for copy in self.copies:
            copy.start()

    def wait(self):
        for copy in self.copies:
            copy.wait()


class Fetch:
    def __init__(self, weight, filled, cut, place, sems, index):
        x, y, z_hi, z_lo, core = place
        send, arrive, own_sem = sems
        self.own = pltpu.make_async_copy(weight, filled, own_sem.at[index])
        across = device(x, y, 1 - z_hi, 1 - z_lo, z_hi)
        up = device(x, turned(y, 1), z_hi, z_lo, core)
        down = device(x, turned(y, 3), z_hi, z_lo, core)
        base = index * 5

        def moved(ref, quarter, half, slot, to):
            source = cut(ref, quarter, half)
            return remote(source, cut(filled, quarter, half), send, arrive, base + slot, to)

        self.across = moved(weight, y, None, 0, across)
        self.up = moved(filled, y, None, 1, up)
        self.down = moved(filled, y, None, 2, down)
        self.up_on = moved(filled, turned(y, 3), 0, 3, up)
        self.down_on = moved(filled, turned(y, 1), 1, 4, down)

    def spread(self):
        self.across.wait_recv()
        self.up.start()
        self.down.start()

    def pass_on(self):
        self.up.wait_recv()
        self.up_on.start()
        self.down.wait_recv()
        self.down_on.start()

    def finish(self):
        self.up_on.wait_recv()
        self.down_on.wait_recv()
        for copy in (self.across, self.up, self.down, self.up_on, self.down_on):
            copy.wait_send()


def fetch_scratch(count):
    return (
        pltpu.SemaphoreType.DMA((5 * count,)),
        pltpu.SemaphoreType.DMA((5 * count,)),
        pltpu.SemaphoreType.DMA((count,)),
    )


def fetch_peers(place):
    x, y, z_hi, z_lo, core = place
    return [device(x, y, 1 - z_hi, 1 - z_lo, z_hi)] + [
        device(x, turned(y, k), z_hi, z_lo, core) for k in (1, 3)
    ]


def quarter_rows(size, *before):
    quarter_size = size // SIDE
    split = -(-quarter_size // 32) * 16

    def cut(weight, quarter, half):
        first = pl.multiple_of(quarter * quarter_size, 16)
        if half is None:
            rows = pl.ds(first, quarter_size)
        elif half == 0:
            rows = pl.ds(first, split)
        else:
            rows = pl.ds(first + split, quarter_size - split)
        return weight.at[(*before, rows)]

    return cut


QKV_CUT = quarter_rows(2048, slice(None))
OUT_CUT = quarter_rows(256)
FF_CUT = quarter_rows(704)


def moments(values):
    centre = values - jnp.mean(values, axis=-1, keepdims=True)
    return centre, lax.rsqrt(jnp.mean(centre * centre, axis=-1, keepdims=True) + 1e-05)


def tile_rows(body):
    @pl.loop(0, BLOCK, step=16)
    def _(row):
        body(pl.ds(pl.multiple_of(row, 16), 16))


def matmul(left, right, contract):
    return lax.dot_general(left, right, ((contract, ((), ()))), preferred_element_type=jnp.float32)


NN, NT, TN = ((1,), (0,)), ((1,), (1,)), ((0,), (0,))
PAIR = 2 * BLOCK
TILE = 256


class Locals:
    def __init__(self, sems):
        self.sems, self.used = sems, 0

    def of(self, source, target):
        self.used += 1
        return pltpu.make_async_copy(source, target, self.sems.at[self.used - 1])


def attention(queries, keys, values, row_info, segments, segment_row, attended, score_scale):
    bf16 = jnp.bfloat16
    lane = lax.broadcasted_iota(jnp.int32, (1, 128), 1)
    row_info[...] = jnp.where(lane == 4, segments[...], 0.0)
    for block in range(4):
        first, end = block * PAIR, (block + 1) * PAIR
        rows, before = pl.ds(first, PAIR), pl.ds(0, end)
        places = first + lax.broadcasted_iota(jnp.int32, (PAIR, end), 0)
        allowed = (segments[rows, :] == segment_row[:, 0:end]) & (
            lax.broadcasted_iota(jnp.int32, (PAIR, end), 1) <= places
        )

        @pl.loop(0, 2)
        def _(pair):
            lanes = pl.ds(pl.multiple_of(pair * 128, 128), 128)
            query, key, value = queries[rows, lanes], keys[before, lanes], values[before, lanes]
            mixed = jnp.zeros((PAIR, 128), jnp.float32)
            for head in range(2):
                inside = (lane >= head * HEAD_DIM) & (lane < (head + 1) * HEAD_DIM)
                query_h = jnp.where(inside, query, jnp.zeros_like(query))
                value_h = jnp.where(inside, value, jnp.zeros_like(value))
                scores = jnp.where(allowed, matmul(query_h, key, NT) * score_scale, -1e30)
                top = jnp.max(scores, axis=1, keepdims=True)
                raised = jnp.exp(scores - top)
                total = jnp.sum(raised, axis=1, keepdims=True)
                mixed = mixed + matmul((raised / total).astype(bf16), value_h, NN)
                row_info[rows, :] = jnp.where(
                    lane == pair * 2 + head, top + jnp.log(total), row_info[rows, :]
                )
            attended[rows, lanes] = mixed.astype(bf16)

        yield


def first_kernel(
    tokens,
    out_grad,
    gain,
    shift,
    qkv,
    out,
    down,
    gate_up,
    gain_mid,
    shift_mid,
    bias,
    segments,
    segment_row,
    keep,
    from_after,
    from_before,
    tokens_here,
    cot_here,
    normed_full,
    cot_full,
    mid,
    normed_mid,
    qkv_here,
    out_here,
    down_here,
    gate_up_here,
    queries,
    keys,
    values,
    attended,
    row_info,
    tok_buf,
    grad_buf,
    cot_buf,
    bias_buf,
    normed,
    part,
    swap_send,
    swap_arrive,
    own_sems,
    *sems,
):
    bf16 = jnp.bfloat16
    place = here()
    x, y, z_hi, z_lo, core = place
    lacking = core != z_hi
    swap_with = device(x, y, core, z_lo, z_hi)
    fetch_sems = sems[8:11]
    fetches = [
        Fetch(weight, filled, cut, place, fetch_sems, index)
        for index, (weight, filled, cut) in enumerate(
            [
                (qkv, qkv_here, QKV_CUT),
                (out, out_here, OUT_CUT),
                (down, down_here, FF_CUT),
                (gate_up.at[0], gate_up_here.at[0], FF_CUT),
                (gate_up.at[1], gate_up_here.at[1], FF_CUT),
            ]
        )
    ]

    def own_terms(step, rows):
        first = (core * SIDE + turned(x, SIDE - step)) * BLOCK
        return part[pl.ds(pl.multiple_of(first + rows.start, 16), rows.size), :]

    terms = ByRow(part, place)
    scatter = Scatter(own_terms, lambda step: terms.at(step, 1), place, sems[11:])
    moved = [(tokens, tok_buf), (out_grad, grad_buf), (bias, bias_buf)]
    swaps = [
        remote(source, target, swap_send, swap_arrive, index, swap_with)
        for index, (source, target) in enumerate(moved)
    ]
    locals_ = Locals(own_sems)
    stays = [locals_.of(source, target) for source, target in moved]
    gather = Gather(normed.at[pl.ds(0, BLOCK)], ByStep(normed), place, sems[:4])
    gather_cot = Gather(cot_buf, ByRow(cot_full, place), place, sems[4:8])
    by_step, by_row = ByStep(normed), ByRow(normed_full, place)
    normed_out = [
        locals_.of(by_step.at(step, other), by_row.at(step, other)) for step in range(SIDE) for other in range(2)
    ]
    stored = [
        locals_.of(tok_buf, tokens_here),
        locals_.of(cot_buf, cot_here),
        locals_.of(cot_buf, row_block(cot_full, core, x)),
    ]

    @pl.when(lacking)
    def _():
        greet(line_peers(place) + [swap_with] + fetch_peers(place))
        swaps[0].start()
        swaps[2].start()
        fetches[0].across.start()
        swaps[0].wait_recv()
        swaps[1].start()
        fetches[1].across.start()

    @pl.when(jnp.logical_not(lacking))
    def _():
        greet(line_peers(place))
        for copy in stays:
            copy.start()
        for fetch in fetches:
            fetch.own.start()
        stays[0].wait()

    def norm(rows):
        centre, scale = moments(tok_buf[rows, :].astype(jnp.float32))
        normed[rows, :] = (centre * scale * gain[...] + shift[...]).astype(bf16)

    tile_rows(norm)
    gather.start()
    stored[0].start()

    @pl.when(lacking)
    def _():
        fetches[0].spread()
        fetches[2].across.start()
        for copy in swaps:
            copy.wait_send()
        swaps[1].wait_recv()
        swaps[2].wait_recv()
        fetches[3].across.start()

    @pl.when(jnp.logical_not(lacking))
    def _():
        stays[1].wait()
        stays[2].wait()

    def mask(rows):
        place_rows = pl.ds(pl.multiple_of((core * SIDE + x) * BLOCK + rows.start, 16), rows.size)
        grads = grad_buf[rows, :].astype(jnp.float32)
        cot_buf[rows, :] = jnp.where(segments[place_rows, :] < SEQUENCES, grads, 0.0).astype(bf16)

    tile_rows(mask)
    gather.arrive(1)
    gather.arrive(3)
    gather_cot.start()
    stored[1].start()
    stored[2].start()

    @pl.when(lacking)
    def _():
        fetches[0].pass_on()
        fetches[1].spread()
        fetches[2].spread()
        fetches[4].across.start()

    gather.arrive(2)
    gather.take()
    for copy in normed_out:
        copy.start()

    @pl.when(lacking)
    def _():
        fetches[0].finish()

    @pl.when(jnp.logical_not(lacking))
    def _():
        fetches[0].own.wait()

    @pl.loop(0, 8)
    def _(index):
        step, other = lax.div(index, 2), lax.rem(index, 2)
        whose = core + other * (1 - 2 * core)
        first = pl.multiple_of((whose * SIDE + turned(x, SIDE - step)) * BLOCK, BLOCK)
        rows = pl.ds(first, BLOCK)
        block = normed[pl.ds(pl.multiple_of(index * BLOCK, BLOCK), BLOCK), :]
        for channel, target in enumerate((queries, keys, values)):
            projected = matmul(block, qkv_here[channel], NN) + bias_buf[channel : channel + 1, :]
            for pair in range(2):
                lanes = projected[:, pair * 128 : (pair + 1) * 128]
                if channel < 2:
                    lanes = (
                        lanes * keep[rows, :]
                        - pltpu.roll(lanes, 120, 1) * from_after[rows, :]
                        - pltpu.roll(lanes, 8, 1) * from_before[rows, :]
                    )
                target[rows, pair * 128 : (pair + 1) * 128] = lanes.astype(bf16)

    @pl.when(lacking)
    def _():
        fetches[1].pass_on()
        fetches[2].pass_on()
        fetches[3].spread()

    gather_cot.arrive(1)
    gather_cot.arrive(3)
    blocks = attention(
        queries, keys, values, row_info, segments, segment_row, attended, HEAD_DIM ** (-0.5)
    )
    for block in range(4):
        next(blocks)
        rows = pl.ds(block * PAIR, PAIR)
        if block == 0:

            @pl.when(lacking)
            def _():
                fetches[1].finish()

            @pl.when(jnp.logical_not(lacking))
            def _():
                fetches[1].own.wait()

        @pl.loop(0, 2048, step=512)
        def _(column):
            columns = pl.ds(pl.multiple_of(column, 512), 512)
            part[rows, columns] = matmul(attended[rows, :], out_here[:, columns], NN).astype(bf16)

        if block == 0:

            @pl.when(lacking)
            def _():
                fetches[4].spread()

            gather_cot.arrive(2)

        if block == 1:

            @pl.when(core == 1)
            def _():
                for step in (2, 1, 3, 0):
                    scatter.across[step].start()

        if block == 2:

            @pl.when(core == 0)
            def _():
                for step in (2, 1, 3):
                    scatter.merge(step)

    @pl.when(core == 0)
    def _():
        for step in (2, 1, 3, 0):
            scatter.across[step].start()

    @pl.when(core == 1)
    def _():
        for step in (2, 1, 3):
            scatter.merge(step)

    @pl.when(lacking)
    def _():
        fetches[3].pass_on()
        fetches[4].pass_on()

    gather_cot.take()
    for each in (gather, gather_cot):
        each.finish()
    for copy in normed_out + stored:
        copy.wait()

    @pl.when(lacking)
    def _():
        for fetch in fetches[2:]:
            fetch.finish()

    @pl.when(jnp.logical_not(lacking))
    def _():
        for fetch in fetches[2:]:
            fetch.own.wait()

    scatter.finish()

    def norm_mid(rows):
        stream = tok_buf[rows, :].astype(jnp.float32) + scatter.rows(rows)
        mid[rows, :] = stream
        centre, scale = moments(stream)
        normed_mid[rows, :] = (centre * scale * gain_mid[...] + shift_mid[...]).astype(bf16)

    tile_rows(norm_mid)


def middle_kernel(
    normed_mid,
    mid,
    gain,
    gate_up_held,
    down_held,
    cot_full,
    attended_full,
    out_held,
    cot,
    d_mid,
    gain_part,
    shift_part,
    gate_grad,
    up_grad,
    down_grad,
    gate_beyond,
    down_sum,
    ffn_part,
    d_attended,
    out_grad,
    gate_up,
    down,
    out,
    normed,
    cot_rows,
    d_rows,
    attended,
    hidden,
    d_gate,
    d_up,
    d_hidden,
    own_rows,
    given_terms,
    ffn_tile,
    grad_tile,
    load_sems,
    att_sems,
    own_sems,
    ffn_sem,
    grad_sems,
    *scratch,
):
    bf16 = jnp.bfloat16
    place = here()
    x, y, z_hi, z_lo, core = place
    lacking = core != z_hi
    second = Scatter(
        lambda step, rows: own_rows[step, rows, :], lambda step: given_terms.at[step], place, scratch[:7]
    )
    gather = Gather(normed.at[pl.ds(0, BLOCK)], ByStep(normed), place, scratch[7:11])
    gather_d = Gather(d_rows.at[pl.ds(0, BLOCK)], ByStep(d_rows), place, scratch[11:15])
    scratch = scratch[15:]
    around = Around(place)
    links = Links(*scratch[:2])
    over = links.to(gate_grad, gate_beyond, around.beyond)
    ring = RowRing(*DOWN_RING)
    ring_terms = scratch[2:5]
    ring_loads = [
        pltpu.make_async_copy(ring.quarter(down_grad, turned(y, k)), held, load_sems.at[index])
        for index, (k, held) in enumerate(zip((1, 3, 0), ring_terms))
    ]
    ring.bind(links, around, scratch[5:], ring.quarter(down_grad, turned(y, 2)), *ring_terms)
    load_cot = Loaded(cot_full, cot_rows, place, load_sems)
    load_att = Loaded(attended_full, attended, place, att_sems)
    load_normed = pltpu.make_async_copy(normed_mid, normed.at[pl.ds(0, BLOCK)], own_sems.at[0])
    load_gate_up = pltpu.make_async_copy(gate_up_held, gate_up, own_sems.at[1])
    load_down = pltpu.make_async_copy(down_held, down, own_sems.at[2])
    load_out = pltpu.make_async_copy(out_held, out, own_sems.at[3])

    load_normed.start()
    load_down.start()
    load_cot.start()
    load_gate_up.start()
    load_att.start()
    load_out.start()
    greet(line_peers(place) + [around.up, around.down, around.beyond])
    load_normed.wait()
    gather.start()
    load_down.wait()
    load_cot.wait()

    @pl.loop(0, 4)
    def _(index):
        rows = pl.ds(pl.multiple_of(index * PAIR, PAIR), PAIR)
        d_hidden[rows, :] = matmul(cot_rows[rows, :], down[...], NT)

    load_gate_up.wait()
    order = (0, 1, 3, 2)

    @pl.loop(0, 4)
    def _(turn):
        step = turn + lax.div(turn, 2) * (5 - 2 * turn)
        for index in range(4):

            @pl.when(turn == index)
            def _(index=index):
                for arrived in ((), (1, 3), (), (2,))[index]:
                    gather.arrive(arrived)
                gather.across[order[index]].wait_recv()

        rows = pl.ds(pl.multiple_of(step * PAIR, PAIR), PAIR)
        gate = matmul(normed[rows, :], gate_up[0], NT)
        up = matmul(normed[rows, :], gate_up[1], NT)
        sigmoid = jax.nn.sigmoid(gate)
        silu = gate * sigmoid
        hidden[rows, :] = (silu * up).astype(bf16)
        d_hid = d_hidden[rows, :]
        d_gate[rows, :] = (d_hid * up * sigmoid * (1.0 + gate * (1.0 - sigmoid))).astype(bf16)
        d_up[rows, :] = (d_hid * silu).astype(bf16)
        for index in (2, 3):

            @pl.when(turn == index)
            def _(index=index):
                second.merge(order[index - 1])

        @pl.loop(0, 2048, step=512)
        def _(column):
            columns = pl.ds(pl.multiple_of(column, 512), 512)
            terms = matmul(d_gate[rows, :], gate_up[0, :, columns], NN) + matmul(
                d_up[rows, :], gate_up[1, :, columns], NN
            )
            terms = terms.astype(bf16)
            own_rows[step, :, columns] = terms[:BLOCK]
            given_terms[step, :, columns] = terms[BLOCK:]

        for index in range(4):

            @pl.when(turn == index)
            def _(index=index):
                second.across[order[index]].start()

    second.merge(2)
    load_att.wait()
    load_out.wait()

    def ffn_terms():
        @pl.loop(0, 4)
        def _(index):
            rows = pl.ds(pl.multiple_of(index * PAIR, PAIR), PAIR)

            @pl.when(index > 0)
            def _():
                pltpu.make_async_copy(ffn_tile, ffn_part.at[rows], ffn_sem).wait()

            @pl.loop(0, 2048, step=512)
            def _(column):
                columns = pl.ds(pl.multiple_of(column, 512), 512)
                ffn_tile[:, columns] = matmul(hidden[rows, :], down[:, columns], NN).astype(bf16)

            pltpu.make_async_copy(ffn_tile, ffn_part.at[rows], ffn_sem).start()

    def weight_grad(target, left, right):
        def stored(tile, slot):
            columns = pl.ds(pl.multiple_of(tile * TILE, TILE), TILE)
            return pltpu.make_async_copy(grad_tile.at[slot], target.at[:, columns], grad_sems.at[slot])

        @pl.loop(0, 8)
        def _(tile):
            slot = lax.rem(tile, 2)

            @pl.when(tile > 1)
            def _():
                stored(tile, slot).wait()

            columns = pl.ds(pl.multiple_of(tile * TILE, TILE), TILE)
            grad_tile[slot] = matmul(left[...], right[:, columns], TN).astype(bf16)
            stored(tile, slot).start()

        for slot in range(2):
            stored(slot, slot).wait()

    weight_grad(gate_grad, d_gate, normed)

    @pl.when(lacking)
    def _():
        over.start()

    weight_grad(down_grad, hidden, cot_rows)
    ring.begin()
    for copy in ring_loads:
        copy.start()
    second.finish()
    gain_part[...] = jnp.zeros_like(gain_part)
    shift_part[...] = jnp.zeros_like(shift_part)

    def back(rows):
        grad = second.rows(rows)
        centre, scale = moments(mid[rows, :])
        unit = centre * scale
        gain_part[...] += jnp.sum(grad * unit, axis=0, keepdims=True)
        shift_part[...] += jnp.sum(grad, axis=0, keepdims=True)
        scaled = grad * gain[...]
        total = cot[rows, :].astype(jnp.float32) + scale * (
            scaled
            - jnp.mean(scaled, axis=-1, keepdims=True)
            - unit * jnp.mean(scaled * unit, axis=-1, keepdims=True)
        )
        d_mid[rows, :] = total
        d_rows[rows, :] = total.astype(bf16)

    tile_rows(back)
    gather_d.start()
    for copy in ring_loads:
        copy.wait()
    ring.merge()
    ffn_terms()
    gather_d.arrive(1)
    gather_d.arrive(3)
    weight_grad(up_grad, d_up, normed)
    gather_d.arrive(2)
    for step in (0, 1, 3, 2):
        gather_d.across[step].wait_recv()
        terms = matmul(d_rows[pl.ds(step * PAIR, PAIR), :], out[...], NT).astype(bf16)
        behind = turned(x, SIDE - step)
        for other in range(2):
            whose = (1 - core) if other else core
            first_row = pl.multiple_of((whose * SIDE + behind) * BLOCK, BLOCK)
            d_attended[pl.ds(first_row, BLOCK), :] = terms[other * BLOCK : (other + 1) * BLOCK]

    @pl.loop(0, 2048, step=512)
    def _(column):
        columns = pl.ds(pl.multiple_of(column, 512), 512)
        out_grad[:, columns] = matmul(attended[...], d_rows[:, columns], TN).astype(bf16)

    gather.finish()
    gather_d.finish()
    pltpu.make_async_copy(ffn_tile, ffn_part.at[pl.ds(0, PAIR)], ffn_sem).wait()
    ring.sum()
    down_stored = pltpu.make_async_copy(ring.total, down_sum, own_sems.at[0])
    down_stored.start()
    ring.sent()
    down_stored.wait()

    @pl.when(lacking)
    def _():
        over.wait_send()

    @pl.when(jnp.logical_not(lacking))
    def _():
        over.wait_recv()


class Links:
    def __init__(self, sends, arrives):
        self.sends, self.arrives, self.used = sends, arrives, 0

    def to(self, source, target, device_id):
        self.used += 1
        return remote(source, target, self.sends, self.arrives, self.used - 1, device_id)


def each_rows(count, step, body):
    if count == step:
        body(pl.ds(0, count))
        return

    @pl.loop(0, count, step=step)
    def _(row):
        body(pl.ds(pl.multiple_of(row, 16), step))


def add_into(target, *terms, count, step):
    def body(rows):
        total = terms[0](rows).astype(jnp.float32)
        for term in terms[1:]:
            total = total + term(rows).astype(jnp.float32)
        target[rows, :] = total.astype(jnp.bfloat16)

    each_rows(count, step, body)


def of(ref, first=0):
    return lambda rows: ref[pl.ds(rows.start + first, rows.size), :]


class Around:
    def __init__(self, place):
        x, y, z_hi, z_lo, core = place
        self.y, self.z_lo = y, z_lo
        self.up = device(x, turned(y, 1), z_hi, z_lo, core)
        self.down = device(x, turned(y, 3), z_hi, z_lo, core)
        self.beyond = device(x, y, 1 - z_hi, 1 - z_lo, core)
        self.twin = device(x, y, z_hi, 1 - z_lo, core)
        self.partner = device(x, y, z_hi, z_lo, 1 - core)
        self.keeps = core == z_hi
        self.gives = jnp.logical_not(self.keeps)


class RowRing:
    def __init__(self, size, width, step):
        self.size, self.width, self.step = size, width, step
        self.split = -(-size // 32) * 16

    def scratch(self):
        kind = jnp.bfloat16
        return (
            pltpu.VMEM((self.split, self.width), kind),
            pltpu.VMEM((self.size - self.split, self.width), kind),
            pltpu.VMEM((self.size, self.width), kind),
            pltpu.VMEM((self.size, self.width), kind),
            pltpu.VMEM((self.size, self.width), kind),
        )

    def quarter(self, ref, index, first=0):
        return ref.at[pl.ds(pl.multiple_of(first + index * self.size, 16), self.size)]

    def halves(self, ref):
        return ref.at[pl.ds(0, self.split)], ref.at[pl.ds(self.split, self.size - self.split)]

    def bind(self, links, around, scratch, far, up_terms, down_terms, own_terms):
        self.from_below, self.from_above, self.got_up, self.got_down, self.total = scratch
        self.up_terms, self.down_terms, self.own_terms = up_terms, down_terms, own_terms
        first, second = self.halves(far)
        self.first = (
            links.to(first, self.from_below, around.up),
            links.to(second, self.from_above, around.down),
        )
        self.second = (
            links.to(up_terms, self.got_up, around.up),
            links.to(down_terms, self.got_down, around.down),
        )

    def begin(self):
        for copy in self.first:
            copy.start()

    def merge(self):
        self.first[0].wait_recv()
        low, high = self.split, self.size - self.split
        up_low, _ = self.halves(self.up_terms)
        _, down_high = self.halves(self.down_terms)
        add_into(up_low, of(up_low), of(self.from_below), count=low, step=low)
        self.second[0].start()
        self.first[1].wait_recv()
        add_into(down_high, of(down_high), of(self.from_above), count=high, step=high)
        self.second[1].start()

    def sum(self):
        for copy in self.second:
            copy.wait_recv()
        add_into(
            self.total,
            of(self.own_terms),
            of(self.got_up),
            of(self.got_down),
            count=self.size,
            step=self.step,
        )

    def sent(self):
        for copy in (*self.first, *self.second):
            copy.wait_send()


class RowSpread:
    def __init__(self, ring, links, locals_, around, total, full, first=0):
        y = around.y
        mine = ring.quarter(full, y, first)
        below, above = ring.quarter(full, turned(y, 3), first), ring.quarter(full, turned(y, 1), first)
        self.own = locals_.of(total, mine)
        self.direct = (links.to(total, mine, around.up), links.to(total, mine, around.down))
        low, high = ring.halves(below)[0], ring.halves(above)[1]
        self.passed = (links.to(low, low, around.up), links.to(high, high, around.down))

    def begin(self):
        self.own.start()
        for copy in self.direct:
            copy.start()

    def pass_on(self):
        for copy, onward in zip(self.direct, self.passed):
            copy.wait_recv()
            onward.start()

    def end(self):
        self.own.wait()
        for copy in self.passed:
            copy.wait_recv()

    def sent(self):
        for copy in (*self.direct, *self.passed):
            copy.wait_send()


WIDE = 1024
DOWN_RING = (176, 2048, 16)
ATTN_UNITS = ((768, 256, 96, 0), (768, 256, 96, 3072), (64, 2048, 16, 0))
LINK_COUNT, LOCAL_COUNT = 112, 64


def left_ring():
    return RowRing(176, WIDE // 2, 176)


def right_ring():
    return RowRing(176, WIDE, 16)


def left_scratch(rows, count):
    kind = jnp.bfloat16
    half = pltpu.VMEM((rows, WIDE // 2), kind)
    return (pltpu.VMEM((rows, WIDE), kind),) * 3 + ((half,) + left_ring().scratch()) * count


def right_scratch(count):
    return (pltpu.VMEM((176, WIDE), jnp.bfloat16),) * (4 * count)


def attn_scratch():
    found = ()
    for size, width, step, _ in ATTN_UNITS:
        ring = RowRing(size, width, step)
        found += (pltpu.VMEM((size, width), jnp.bfloat16),) * 2 + ring.scratch()
    return found


def left_sum(part, beyond, full, column, fetch, links, locals_, around, mine, got, scratch):
    half = scratch[0]
    rows, width = got.shape[0], WIDE // 2
    ring = left_ring()
    side = lambda z_lo: pl.ds(pl.multiple_of(z_lo * width, 128), width)
    columns = pl.ds(column, WIDE)
    stretch = full.at[:, columns]
    own_side = full.at[:, pl.ds(pl.multiple_of(column + around.z_lo * width, 128), width)]
    loads = (locals_.of(part.at[:, columns], mine), locals_.of(beyond.at[:, columns], got))
    if fetch:
        over = links.to(part.at[:, columns], beyond.at[:, columns], around.beyond)
    kept, sent_on = side(around.z_lo), side(1 - around.z_lo)
    twin = links.to(got.at[:, sent_on], half, around.twin)
    quarter = lambda k: ring.quarter(half, turned(around.y, k))
    ring.bind(links, around, scratch[1:], quarter(2), quarter(1), quarter(3), quarter(0))
    spread = RowSpread(ring, links, locals_, around, ring.total, own_side)
    both = links.to(own_side, own_side, around.twin)
    core = links.to(stretch, stretch, around.partner)

    if fetch:

        @pl.when(around.gives)
        def _():
            over.start()

        yield

    @pl.when(around.keeps)
    def _():
        if fetch:
            over.wait_recv()
        for copy in loads:
            copy.start()

    yield

    @pl.when(around.keeps)
    def _():
        for copy in loads:
            copy.wait()
        add_into(got, of(got), of(mine), count=rows, step=64)
        twin.start()

    yield

    @pl.when(around.keeps)
    def _():
        twin.wait_recv()
        add_into(half, of(half), lambda rows: got[rows, kept], count=rows, step=64)
        ring.begin()
        twin.wait_send()

    yield

    @pl.when(around.keeps)
    def _():
        ring.merge()

    yield

    @pl.when(around.keeps)
    def _():
        ring.sum()
        spread.begin()

    yield

    @pl.when(around.keeps)
    def _():
        spread.pass_on()

    yield

    @pl.when(around.keeps)
    def _():
        spread.end()
        both.start()

    yield

    @pl.when(around.keeps)
    def _():
        both.wait_recv()
        core.start()

    yield

    @pl.when(around.keeps)
    def _():
        ring.sent()
        spread.sent()
        both.wait_send()
        core.wait_send()

    @pl.when(around.gives)
    def _():
        if fetch:
            over.wait_send()
        core.wait_recv()

    yield


def across_and_back(ring, total, spare, from_beyond, from_twin, full, first, links, locals_, around):
    over = links.to(total, from_beyond, around.beyond)
    twin = links.to(total, from_twin, around.twin)
    spread = RowSpread(ring, links, locals_, around, spare, full, first)
    span = full.at[pl.ds(first, SIDE * ring.size)]
    core = links.to(span, span, around.partner)

    @pl.when(around.gives)
    def _():
        over.start()

    yield

    @pl.when(around.keeps)
    def _():
        over.wait_recv()
        add_into(total, of(total), of(from_beyond), count=ring.size, step=ring.step)
        twin.start()

    yield

    @pl.when(around.keeps)
    def _():
        twin.wait_recv()
        add_into(spare, of(total), of(from_twin), count=ring.size, step=ring.step)
        spread.begin()

    yield

    @pl.when(around.keeps)
    def _():
        spread.pass_on()

    yield

    @pl.when(around.keeps)
    def _():
        spread.end()
        core.start()

    yield

    @pl.when(around.keeps)
    def _():
        twin.wait_send()
        spread.sent()
        core.wait_send()

    @pl.when(around.gives)
    def _():
        over.wait_send()
        core.wait_recv()

    yield


def right_sum(summed, full, unit, links, locals_, around, scratch):
    stretch = full.at[:, pl.ds(unit, WIDE)]
    total, spare, from_beyond, from_twin = scratch
    ring = right_ring()
    load = locals_.of(summed.at[:, pl.ds(unit, WIDE)], total)
    load.start()
    yield
    load.wait()
    yield from across_and_back(
        ring, total, spare, from_beyond, from_twin, stretch, 0, links, locals_, around
    )


def attn_sum(part, full, unit, links, locals_, around, held_terms, scratch):
    own_terms, up_terms, down_terms = held_terms
    from_beyond, from_twin = scratch[:2]
    *sizes, first = unit
    ring = RowRing(*sizes)
    quarter = lambda k: ring.quarter(part, turned(around.y, k), first)
    loads = [
        locals_.of(quarter(k), held) for k, held in ((1, up_terms), (3, down_terms), (0, own_terms))
    ]
    ring.bind(links, around, scratch[2:], quarter(2), up_terms, down_terms, own_terms)
    ring.begin()
    for copy in loads:
        copy.start()
    yield
    for copy in loads:
        copy.wait()
    ring.merge()
    yield
    ring.sum()
    yield from across_and_back(
        ring, ring.total, own_terms, from_beyond, from_twin, full, first, links, locals_, around
    )
    ring.sent()
    yield


def sum_everywhere(values, places, links, place):
    x, y, z_hi, z_lo, core = place
    by_x, by_core, by_y, by_z = places
    z = z_hi * 2 + z_lo
    rounds = (
        (by_x, x, [device(turned(x, k), y, z_hi, z_lo, core) for k in (1, 2, 3)]),
        (by_core, core, [device(x, y, z_hi, z_lo, 1 - core)]),
        (by_y, y, [device(x, turned(y, k), z_hi, z_lo, core) for k in (1, 2, 3)]),
        (by_z, z, [z_device(x, y, turned(z, k), core) for k in (1, 2, 3)]),
    )
    for slots, mine, peers in rounds:
        slots[mine] = values[...]
        copies = [links.to(slots.at[mine], slots.at[mine], peer) for peer in peers]
        for copy in copies:
            copy.start()
        yield
        for copy in copies:
            copy.wait()
        total = slots[0]
        for slot in range(1, slots.shape[0]):
            total = total + slots[slot]
        values[...] = total
    yield


def z_device(x, y, z, core):
    return device(x, y, lax.div(z, 2), lax.rem(z, 2), core)


def attention_back(
    queries, keys, values, d_attended, row_info, segment_row, turns, qkv, d_keys, d_values, d_proj, d_normed, score_scale
):
    bf16, f32 = jnp.bfloat16, jnp.float32
    keep, from_after, from_before = turns
    lane = lax.broadcasted_iota(jnp.int32, (1, 128), 1)
    d_keys[...] = jnp.zeros_like(d_keys)
    d_values[...] = jnp.zeros_like(d_values)

    def turned_back(grads, rows):
        return (
            grads * keep[rows, :]
            + pltpu.roll(grads, 120, 1) * from_after[rows, :]
            + pltpu.roll(grads, 8, 1) * from_before[rows, :]
        )

    for block in (3, 2, 1, 0):
        first, end = block * PAIR, (block + 1) * PAIR
        rows, before = pl.ds(first, PAIR), pl.ds(0, end)
        info = row_info[rows, :]
        places = first + lax.broadcasted_iota(jnp.int32, (PAIR, end), 0)
        allowed = (info[:, 4:5] == segment_row[:, 0:end]) & (
            lax.broadcasted_iota(jnp.int32, (PAIR, end), 1) <= places
        )
        info_lane = lax.broadcasted_iota(jnp.int32, info.shape, 1)

        @pl.loop(0, 2)
        def _(pair):
            lanes = pl.ds(pl.multiple_of(pair * 128, 128), 128)
            query, grad = queries[rows, lanes], d_attended[rows, lanes]
            key, value = keys[before, lanes], values[before, lanes]
            d_query = jnp.zeros((PAIR, 128), f32)
            for head in range(2):
                inside = (lane >= head * HEAD_DIM) & (lane < (head + 1) * HEAD_DIM)
                query_h = jnp.where(inside, query, jnp.zeros_like(query))
                grad_h = jnp.where(inside, grad, jnp.zeros_like(grad))
                key_h = jnp.where(inside, key, jnp.zeros_like(key))
                log_norm = jnp.sum(
                    jnp.where(info_lane == pair * 2 + head, info, 0.0), axis=1, keepdims=True
                )
                scores = jnp.where(allowed, matmul(query_h, key, NT) * score_scale, -1e30)
                prob = jnp.exp(scores - log_norm)
                d_prob = matmul(grad_h, value, NT)
                row_dots = jnp.sum(prob * d_prob, axis=1, keepdims=True)
                d_score = (prob * (d_prob - row_dots)).astype(bf16)
                d_query = d_query + matmul(d_score, key_h, NN)
                d_keys[before, lanes] += matmul(d_score, query_h, TN)
                d_values[before, lanes] += matmul(prob.astype(bf16), grad_h, TN)
            d_proj[rows, lanes] = turned_back(d_query * score_scale, rows).astype(bf16)
            key_lanes = pl.ds(pl.multiple_of(256 + pair * 128, 128), 128)
            d_proj[rows, key_lanes] = turned_back(d_keys[rows, lanes] * score_scale, rows).astype(bf16)
            value_lanes = pl.ds(pl.multiple_of(512 + pair * 128, 128), 128)
            d_proj[rows, value_lanes] = d_values[rows, lanes].astype(bf16)

        @pl.loop(0, 2048, step=512)
        def _(column):
            columns = pl.ds(pl.multiple_of(column, 512), 512)
            total = matmul(d_proj[rows, 0:256], qkv[0, columns, :], NT)
            total = total + matmul(d_proj[rows, 256:512], qkv[1, columns, :], NT)
            total = total + matmul(d_proj[rows, 512:768], qkv[2, columns, :], NT)
            d_normed[rows, columns] = total.astype(bf16)

        yield


ORDER = (
    "l3", "l0", "f", "l2", "a2", "r0", "r1", "l0", "l1", "f", "l1", "f", "l0", "f",
    "l1", "l0", "f", "l1", "l2", "l0", "a2", "l2", "l3", "f", "l3", "l1", "l0", "f",
    "a0", "a1", "l1", "l2", "f", "l0", "l3", "a2", "r0", "f", "r1", "a0", "f", "a1",
    "l1", "l2", "a2", "l3", "r0", "l0", "r1", "a0", "l0", "l1", "a2", "a0", "a1", "l1",
    "l2", "r0", "l3", "f", "r1", "e", "a1", "l2", "a2", "f", "a0", "r0", "e", "l3",
    "e", "a1", "r1", "l2", "a2", "a2", "a0", "r0", "l3", "e", "r0", "a1", "l2", "r1",
    "a0", "l2", "a1", "r1", "l3", "a0", "e", "a1", "l3",
)


def last_kernel(
    queries_in,
    keys_in,
    values_in,
    d_attended_in,
    row_info,
    segment_row,
    keep,
    from_after,
    from_before,
    qkv,
    normed,
    tokens,
    d_mid,
    gain,
    ffn_part,
    mid,
    gate_part,
    gate_beyond,
    up_part,
    down_sum,
    out_part,
    gain_part,
    shift_part,
    mixed,
    input_grad,
    gate_full,
    up_full,
    down_full,
    qkv_full,
    out_full,
    sums,
    up_beyond,
    qkv_part,
    queries,
    keys,
    values,
    d_attended,
    d_keys,
    d_values,
    d_proj,
    d_normed,
    normed_tile,
    grad_tile,
    d_in,
    mixed_rows,
    ffn_rows,
    normed_sems,
    grad_sems,
    ready,
    sends,
    arrives,
    local_sems,
    by_x,
    by_core,
    by_y,
    by_z,
    *scratch,
):
    bf16 = jnp.bfloat16
    place = here()
    x, y, z_hi, z_lo, core = place
    z = z_hi * 2 + z_lo
    around = Around(place)
    links, locals_ = Links(sends, arrives), Locals(local_sems)
    swap_with = device(x, y, core, z_lo, z_hi)
    terms, ffn_terms = ByRow(d_normed, place), ByStep(ffn_part)

    def own_terms(step, rows):
        first = (core * SIDE + turned(x, SIDE - step)) * BLOCK
        return d_normed[pl.ds(pl.multiple_of(first + rows.start, 16), rows.size), :]

    scatter_ffn = Scatter(
        lambda step, rows: ffn_rows[step, rows, :], lambda step: ffn_terms.at(step, 1), place, scratch[:7]
    )
    scatter = Scatter(own_terms, lambda step: terms.at(step, 1), place, scratch[:3] + scratch[7:11])
    scratch = scratch[11:]
    units = {}
    mine, *got = scratch[:3]
    scratch = scratch[3:]
    refs_of = ((gate_part, gate_beyond, gate_full), (up_part, up_beyond, up_full))
    for index in range(4):
        units[f"l{index}"] = left_sum(
            *refs_of[index // 2],
            (index % 2) * WIDE,
            index > 1,
            links,
            locals_,
            around,
            mine,
            got[index % 2],
            scratch[:6],
        )
        scratch = scratch[6:]
    for index in range(2):
        units[f"r{index}"] = right_sum(down_sum, down_full, index * WIDE, links, locals_, around, scratch[:4])
        scratch = scratch[4:]
    out_terms, scratch = scratch[:3], scratch[3:]
    held_terms = (
        [ref.at[pl.ds(0, 768)] for ref in (queries, keys, values)],
        [d_proj.at[pl.ds(0, 768), pl.ds(256 * index, 256)] for index in range(3)],
        out_terms,
    )
    for index, unit in enumerate(ATTN_UNITS):
        refs = (out_part, out_full) if index == 2 else (qkv_part, qkv_full)
        units[f"a{index}"] = attn_sum(*refs, unit, links, locals_, around, held_terms[index], scratch[:7])
        scratch = scratch[7:]
    units["e"] = sum_everywhere(sums, (by_x, by_core, by_y, by_z), links, place)
    units["t"] = attention_back(
        queries,
        keys,
        values,
        d_attended,
        row_info,
        segment_row,
        (keep, from_after, from_before),
        qkv,
        d_keys,
        d_values,
        d_proj,
        d_normed,
        HEAD_DIM ** (-0.5),
    )

    def on(*names):
        for name in names:
            next(units[name])

    load_attn = [
        locals_.of(source, held)
        for source, held in (
            (queries_in, queries),
            (keys_in, keys),
            (values_in, values),
            (d_attended_in, d_attended),
        )
    ]
    load_ffn = [locals_.of(ffn_terms.at(step, 0), ffn_rows.at[step]) for step in range(SIDE)]
    swaps = [links.to(mixed_rows, mixed, swap_with), links.to(d_in, input_grad, swap_with)]
    stays = [locals_.of(mixed_rows, mixed), locals_.of(d_in, input_grad)]

    def give(index):
        @pl.when(around.gives)
        def _():
            swaps[index].start()

        @pl.when(around.keeps)
        def _():
            stays[index].start()

    def load_normed(chunk):
        columns = pl.ds(pl.multiple_of(chunk * TILE, TILE), TILE)
        slot = lax.rem(chunk, 2)
        return pltpu.make_async_copy(normed.at[:, columns], normed_tile.at[slot], normed_sems.at[slot])

    def store_grad(chunk):
        slot = lax.rem(chunk, 2)
        return [
            pltpu.make_async_copy(
                grad_tile.at[slot, pl.ds(channel * TILE, TILE)],
                qkv_part.at[pl.ds(pl.multiple_of(channel * 2048 + chunk * TILE, TILE), TILE)],
                grad_sems.at[slot, channel],
            )
            for channel in range(3)
        ]

    def qkv_grads(first, end):
        @pl.loop(first, end)
        def _(chunk):
            slot = lax.rem(chunk, 2)
            load_normed(chunk).wait()

            @pl.when(chunk + 1 < 8)
            def _():
                load_normed(chunk + 1).start()

            @pl.when(chunk > first + 1)
            def _():
                for copy in store_grad(chunk):
                    copy.wait()

            grads = matmul(normed_tile[slot], d_proj[...], TN).astype(bf16)
            for channel in range(3):
                grad_tile[slot, channel * TILE : (channel + 1) * TILE, :] = grads[
                    :, channel * TILE : (channel + 1) * TILE
                ]
            for copy in store_grad(chunk):
                copy.start()

        for chunk in (end - 2, end - 1):
            for copy in store_grad(jnp.int32(chunk)):
                copy.wait()

    for copy in load_ffn + load_attn:
        copy.start()
    load_normed(jnp.int32(0)).start()
    peers = line_peers(place) + [device(x, turned(y, k), z_hi, z_lo, core) for k in (1, 2, 3)]
    peers += [z_device(x, y, turned(z, k), core) for k in (1, 2, 3)]

    @pl.when(around.gives)
    def _():
        greet(peers + [swap_with])

    @pl.when(around.keeps)
    def _():
        greet(peers)

    def mix(rows):
        mixed_rows[rows, :] = (mid[rows, :] + scatter_ffn.rows(rows)).astype(bf16)

    def bias_grads():
        width = d_proj.shape[1] // 3
        mine_columns = pl.ds(pl.multiple_of((core * SIDE + x) * width, width), width)
        for channel in range(3):
            grads = d_proj[:, channel * width : (channel + 1) * width].astype(jnp.float32)
            sums[4 + channel : 5 + channel, mine_columns] = jnp.sum(grads, axis=0, keepdims=True)

    def back(rows):
        grad = scatter.rows(rows)
        centre, scale = moments(tokens[rows, :].astype(jnp.float32))
        unit = centre * scale
        sums[0:1, :] += jnp.sum(grad * unit, axis=0, keepdims=True)
        sums[1:2, :] += jnp.sum(grad, axis=0, keepdims=True)
        scaled = grad * gain[...]
        d_in[rows, :] = d_mid[rows, :] + scale * (
            scaled
            - jnp.mean(scaled, axis=-1, keepdims=True)
            - unit * jnp.mean(scaled * unit, axis=-1, keepdims=True)
        )

    def foreground():
        for step in (2, 1, 3, 0):
            scatter_ffn.across[step].start()
        yield
        for copy in load_ffn:
            copy.wait()
        for step in (2, 1, 3):
            scatter_ffn.merge(step)
        yield
        for copy in load_attn:
            copy.wait()
        sums[...] = jnp.zeros_like(sums)
        sums[2:3, :] = gain_part[...]
        sums[3:4, :] = shift_part[...]
        on("t")
        yield
        on("t")
        yield
        on("t")
        yield
        on("t")
        yield
        qkv_grads(0, 8)
        bias_grads()
        yield
        scatter_ffn.finish()
        tile_rows(mix)
        for peer in line_peers(place):
            pl.semaphore_signal(ready, inc=1, device_id=peer, device_id_type=MESH)
        give(0)
        yield
        pl.semaphore_wait(ready, SIDE)
        for step in (2, 1, 3, 0):
            scatter.across[step].start()
        yield
        for step in (2, 1, 3):
            scatter.merge(step)
        yield
        scatter.finish()
        tile_rows(back)
        yield
        give(1)
        yield

    units["f"] = foreground()
    on(*ORDER)
    for unit in units.values():
        for _ in unit:
            pass

    @pl.when(around.gives)
    def _():
        for copy in swaps:
            copy.wait()

    @pl.when(around.keeps)
    def _():
        for copy in stays:
            copy.wait()


ANY = pl.BlockSpec(memory_space=pl.ANY)
HELD = pl.BlockSpec(memory_space=pltpu.VMEM)


def call(kernel, collective_id, args, in_specs, outs, out_specs, scratch):
    return pl.pallas_call(
        kernel,
        out_shape=[jax.ShapeDtypeStruct(shape, kind) for shape, kind in outs],
        in_specs=in_specs,
        out_specs=out_specs,
        scratch_shapes=list(scratch),
        compiler_params=pltpu.CompilerParams(
            collective_id=collective_id, has_side_effects=True, vmem_limit_bytes=VMEM_LIMIT
        ),
    )(*args)


def member_layout(seq_length, seq_owner, member, row_total):
    entry_total = seq_length.shape[0]
    row_ids = jnp.arange(row_total, dtype=jnp.int32)
    entry_ids = jnp.arange(entry_total, dtype=jnp.int32)
    earlier = (entry_ids[:, None] < entry_ids[None, :]).astype(jnp.int32)
    sharing = (seq_owner[:, None] == seq_owner[None, :]).astype(jnp.int32)
    starts = jnp.sum(seq_length[:, None] * sharing * earlier, axis=0)
    owned_now = (seq_owner == member).astype(jnp.int32)
    inside = (
        owned_now[None, :]
        * (row_ids[:, None] >= starts[None, :]).astype(jnp.int32)
        * (row_ids[:, None] < (starts + seq_length)[None, :]).astype(jnp.int32)
    )
    live_rows = jnp.sum(inside, axis=1)
    segment = jnp.sum(inside * entry_ids[None, :], axis=1) + (1 - live_rows) * (
        entry_total + row_ids
    )
    position = jnp.sum(inside * (row_ids[:, None] - starts[None, :]), axis=1)
    return (segment, position, live_rows)


def rotary_tables(position):
    half_rot = ROT // 2
    frequency = jnp.power(
        jnp.float32(10000.0), -2.0 * jnp.arange(half_rot, dtype=jnp.float32) / ROT
    )
    lane = jnp.arange(128) % HEAD_DIM
    frequency = jnp.where(lane < ROT, jnp.tile(frequency, 128 // half_rot), 0.0)
    angles = position.astype(jnp.float32)[:, None] * frequency[None, :]
    sine = jnp.sin(angles)
    from_after = jnp.where(lane < half_rot, sine, 0.0)
    from_before = jnp.where(lane >= half_rot, -sine, 0.0)
    return (jnp.cos(angles), from_after, from_before)


def body(
    tokens,
    seq_length,
    seq_owner,
    ln1_gain,
    ln1_bias,
    qkv_weight,
    qkv_bias,
    out_weight,
    ln2_gain,
    ln2_bias,
    gate_up_weight,
    down_weight,
    out_grad,
):
    bf16, f32 = jnp.bfloat16, jnp.float32
    x, y, z_hi, z_lo, core = here()
    row_total = BLOCK * 8
    rows_here, rows_all = (BLOCK, 2048), (row_total, 2048)
    local_heads = qkv_weight.shape[2] // HEAD_DIM
    member = (y * 2 + z_lo) * 2 + z_hi
    segment, position, _ = member_layout(seq_length, seq_owner, member, row_total)
    segments = segment.astype(f32)[:, None]
    segment_row = segment.astype(f32)[None]
    keep, from_after, from_before = rotary_tables(position)
    flat = (row_total, qkv_weight.shape[2])
    dma, vmem = pltpu.SemaphoreType.DMA, pltpu.VMEM
    gate_up_t = jnp.swapaxes(gate_up_weight, 1, 2)
    (
        tokens_here,
        cot,
        normed1,
        cot_rows,
        mid_stream,
        normed2,
        qkv,
        out,
        down,
        gate_up,
        queries,
        keys,
        values,
        attended,
        row_info,
    ) = call(
        first_kernel,
        1,
        (
            tokens,
            out_grad,
            ln1_gain[None],
            ln1_bias[None],
            qkv_weight,
            out_weight,
            down_weight,
            gate_up_t,
            ln2_gain[None],
            ln2_bias[None],
            qkv_bias,
            segments,
            segment_row,
            keep,
            from_after,
            from_before,
        ),
        [ANY, ANY, HELD, HELD, ANY, ANY, ANY, ANY] + [HELD] * 8,
        [
            (rows_here, bf16),
            (rows_here, bf16),
            (rows_all, bf16),
            (rows_all, bf16),
            (rows_here, f32),
            (rows_here, bf16),
            (qkv_weight.shape, bf16),
            (out_weight.shape, bf16),
            (down_weight.shape, bf16),
            (gate_up_t.shape, bf16),
            (flat, bf16),
            (flat, bf16),
            (flat, bf16),
            (flat, bf16),
            ((row_total, 128), f32),
        ],
        [ANY] * 4 + [HELD] * 11,
        (
            vmem(rows_here, bf16),
            vmem(rows_here, bf16),
            vmem(rows_here, bf16),
            vmem(qkv_bias.shape, f32),
            vmem(rows_all, bf16),
            vmem(rows_all, bf16),
            dma((3,)),
            dma((3,)),
            dma((16,)),
        )
        + Gather.scratch * 2
        + fetch_scratch(5)
        + Scatter.scratch,
    )

    ff = down_weight.shape[0]
    d_mid, gain2_part, shift2_part, *ff_parts, ffn_part, d_attended, out_grad = call(
        middle_kernel,
        2,
        (
            normed2,
            mid_stream,
            ln2_gain[None],
            gate_up,
            down,
            cot_rows,
            attended,
            out,
            cot,
        ),
        [ANY, HELD, HELD, ANY, ANY, ANY, ANY, ANY, HELD],
        [
            (rows_here, f32),
            ((1, 2048), f32),
            ((1, 2048), f32),
            (down_weight.shape, bf16),
            (down_weight.shape, bf16),
            (down_weight.shape, bf16),
            (down_weight.shape, bf16),
            ((ff // SIDE, 2048), bf16),
            (rows_all, bf16),
            (attended.shape, bf16),
            (out.shape, bf16),
        ],
        [HELD] * 3 + [ANY] * 6 + [HELD, HELD],
        (
            vmem((2, ff, 2048), bf16),
            vmem((ff, 2048), bf16),
            vmem(out.shape, bf16),
            vmem(rows_all, bf16),
            vmem(rows_all, bf16),
            vmem(rows_all, bf16),
            vmem(attended.shape, bf16),
            vmem((row_total, ff), bf16),
            vmem((row_total, ff), bf16),
            vmem((row_total, ff), bf16),
            vmem((row_total, ff), f32),
            vmem((SIDE, BLOCK, 2048), bf16),
            vmem((SIDE, BLOCK, 2048), bf16),
            vmem((PAIR, 2048), bf16),
            vmem((2, ff, TILE), bf16),
            dma((8,)),
            dma((8,)),
            dma((6,)),
            dma,
            dma((2,)),
        )
        + Scatter.scratch
        + Gather.scratch * 2
        + (dma((5,)), dma((5,)))
        + (vmem((ff // SIDE, 2048), bf16),) * 3
        + RowRing(*DOWN_RING).scratch(),
    )

    gate_part, up_part, _, gate_beyond, down_sum = ff_parts
    small = (8, 2048)
    qkv_rows = (3 * 2048, flat[1])
    mixed, input_grad, gate_full, up_full, down_full, qkv_full, out_full, sums, _, _ = call(
        last_kernel,
        4,
        (
            queries,
            keys,
            values,
            d_attended,
            row_info,
            segment_row,
            keep,
            from_after,
            from_before,
            qkv,
            normed1,
            tokens_here,
            d_mid,
            ln1_gain[None],
            ffn_part,
            mid_stream,
            gate_part,
            gate_beyond,
            up_part,
            down_sum,
            out_grad,
            gain2_part,
            shift2_part,
        ),
        [ANY] * 4 + [HELD] * 6 + [ANY] + [HELD] * 3 + [ANY, HELD] + [ANY] * 5 + [HELD] * 2,
        [
            (rows_here, bf16),
            (rows_here, f32),
            (down_weight.shape, bf16),
            (down_weight.shape, bf16),
            (down_weight.shape, bf16),
            (qkv_rows, bf16),
            (out.shape, bf16),
            (small, f32),
            (down_weight.shape, bf16),
            (qkv_rows, bf16),
        ],
        [ANY] * 7 + [HELD] + [ANY] * 2,
        (
            vmem(flat, bf16),
            vmem(flat, bf16),
            vmem(flat, bf16),
            vmem(flat, bf16),
            vmem(flat, f32),
            vmem(flat, f32),
            vmem((row_total, 3 * flat[1]), bf16),
            vmem(rows_all, bf16),
            vmem((2, row_total, TILE), bf16),
            vmem((2, 3 * TILE, flat[1]), bf16),
            vmem(rows_here, f32),
            vmem(rows_here, bf16),
            vmem((SIDE, BLOCK, 2048), bf16),
            dma((2,)),
            dma((2, 3)),
            pltpu.SemaphoreType.REGULAR,
            dma((LINK_COUNT,)),
            dma((LINK_COUNT,)),
            dma((LOCAL_COUNT,)),
            vmem((SIDE, *small), f32),
            vmem((2, *small), f32),
            vmem((SIDE, *small), f32),
            vmem((SIDE, *small), f32),
        )
        + Scatter.scratch
        + Scatter.sems
        + left_scratch(ff, 4)
        + right_scratch(2)
        + (vmem((64, 2048), bf16),) * 3
        + attn_scratch(),
    )
    gate_up_grad = jnp.swapaxes(jnp.stack([gate_full.astype(f32), up_full.astype(f32)]), 1, 2)
    down_grad = down_full.astype(f32)
    qkv_weight_grad = qkv_full.reshape(3, 2048, -1).astype(f32)
    out_weight_grad = out_full.astype(f32)
    width = qkv_bias.shape[1]
    qkv_bias_grad = lax.dynamic_slice_in_dim(sums[4:7], (z_hi * SIDE + x) * width, width, 1)
    return (
        mixed,
        input_grad,
        sums[0],
        sums[1],
        qkv_weight_grad,
        qkv_bias_grad,
        out_weight_grad,
        sums[2],
        sums[3],
        gate_up_grad,
        down_grad,
    )


def solution(mesh):
    placed = (
        P(("dp", "tensor"), None),
        P(),
        P(),
        P(),
        P(),
        P(None, None, "tensor"),
        P(None, "tensor"),
        P("tensor", None),
        P(),
        P(),
        P(None, None, "tensor"),
        P("tensor", None),
        P(("dp", "tensor"), None),
    )
    return jax.shard_map(
        body,
        mesh=mesh,
        in_specs=placed,
        out_specs=(
            P(("dp", "tensor"), None),
            P(("dp", "tensor"), None),
            P(),
            P(),
            P(None, None, "tensor"),
            P(None, "tensor"),
            P("tensor", None),
            P(),
            P(),
            P(None, None, "tensor"),
            P("tensor", None),
        ),
        check_vma=False,
    )
```
